32 devices in a mesh: cells: 2 (over x), spots: 8 (over z, y), genes: 2 (over core).
Axes of the slice: x: 2, y: 2, z: 4, core: 2. Of those that a mesh axis runs over, the one named last changes fastest.
Arguments:
- logits: float32 [16384, 8192], P('cells', ('spots', 'genes')), may hold values from -6 to 6
- filter_logits: float32 [16384], P('cells'), may hold values from -6 to 6
- expression: bfloat16 [16384, 2048], P(('cells', 'spots'), 'genes'), may hold values from -6 to 6
- spot_expression: float32 [8192, 2048], P('spots', 'genes'), may hold values from -6 to 6
- cell_mask: int32 [16384], P('cells'), may hold values from 0 to 1, as said below
- spot_counts: int32 [8192], P(('spots', 'genes')), may hold values from 1 to 32
Outputs:
- predicted: float32 [8192, 2048], P('spots', 'genes')
- total_loss: float32 [], replicated
- grad_logits: float32 [16384, 8192], P('cells', ('spots', 'genes'))
- filter_grad: float32 [16384], P('cells')
The draws below stay inside these ranges and needn't reach their ends.
Inputs may be any that keep to these rules, and one draw needn't show every extreme that they name: `cell_mask`: 1 marks a cell that takes part in the mapping.
All inputs are finite; a program needn't handle non-finite values.
Results may differ from the reference program's by a relative error of at most 0.0034.
Values may be sent and summed in bfloat16 or wider, within the bound.
No kernel may reach another device: no remote copies, remote signals or barrier semaphores. Data moves between devices by JAX's collectives and lax.ppermute only.
A program may use at most 192 MiB of HBM per device.

```python
import jax
import jax.numpy as jnp
from jax import lax

GENES = 2048
CELLS = 16384
SPOTS = 8192


def draw_cell_mask(key, part):
    key = jax.random.fold_in(key, 7)
    ramp = 3200 + 6600 * jnp.arange(CELLS, dtype=jnp.int32) // CELLS
    rolled = jax.random.randint(key, (CELLS,), 0, 10000, dtype=jnp.int32)
    return (rolled < ramp).astype(jnp.int32)


def touch_ends(drawn, own_key, smallest, largest):
    longest = drawn.shape.index(max(drawn.shape))
    spots = []
    for shift in (0, 1):
        where = [jax.random.randint(jax.random.fold_in(own_key, axis), (), 0, length) for axis, length in enumerate(drawn.shape)]
        where[longest] = (where[longest] + shift) % drawn.shape[longest]
        spots.append(tuple(where))
    return drawn.at[spots[0]].set(smallest).at[spots[1]].set(largest)


def block_levels(key, dims, cuts, smallest, top_value):
    loudness = 1.0
    for position, blocks in cuts:
        draws = jax.random.uniform(jax.random.fold_in(jax.random.fold_in(key, 6), position), (blocks,), jnp.float32, smallest / len(cuts), top_value / len(cuts))
        loudness = loudness * jnp.repeat(jnp.exp(draws), dims[position] // blocks).reshape((-1,) + (1,) * (len(dims) - 1 - position))
    return loudness


def bell_draw(own_key, dims, spread, limit, shards=(), held_as=jnp.bfloat16):
    array = spread * jax.random.normal(own_key, dims, jnp.float32)
    if shards:
        array = array * block_levels(own_key, dims, shards, -0.22, 0.18)
    return jnp.clip(array, -limit, limit).astype(held_as)


def setup_inputs(seed: int = 0) -> dict:
    streams_of = jax.random.split(jax.random.key(seed), 7)
    logits = bell_draw(streams_of[0], (CELLS, SPOTS), 1.0, 6.0, ((0, 2), (1, 16)), jnp.float32)
    filter_logits = bell_draw(streams_of[1], (CELLS,), 1.5, 6.0, ((0, 2),), jnp.float32)
    expression = bell_draw(streams_of[2], (CELLS, GENES), 1.0, 6.0, ((0, 16), (1, 2)))
    spot_expression = bell_draw(streams_of[3], (SPOTS, GENES), 1.0, 6.0, ((0, 8), (1, 2)), jnp.float32)
    cell_mask = draw_cell_mask(jax.random.fold_in(streams_of[6], 71), 0)
    spot_counts = touch_ends(jax.random.randint(streams_of[5], (SPOTS,), 1, 33), jax.random.fold_in(streams_of[5], 1), 1, 32).astype(jnp.int32)
    return dict(logits=logits, filter_logits=filter_logits, expression=expression, spot_expression=spot_expression, cell_mask=cell_mask, spot_counts=spot_counts)


@jax.custom_vjp
def low(v):
    return lax.optimization_barrier(v.astype(jnp.bfloat16)).astype(jnp.float32)

@jax.custom_vjp
def low_back(v):
    return v

def low_keep(v):
    return (low(v), None)

def low_pass(kept, grad):
    return (grad,)

def back_keep(v):
    return (v, None)

def back_low(kept, grad):
    return (low(grad),)
low.defvjp(low_keep, low_pass)
low_back.defvjp(back_keep, back_low)
epsilon = 1e-06

def forward(logits, filter_logits, expression, target, enable, counts):
    masked = jnp.where(enable[:, None] > 0, logits, -1e+30)
    col_top = lax.optimization_barrier(jnp.max(masked, axis=0))
    exponent = enable[:, None] * jnp.exp(logits - col_top[None, :])
    mapping = exponent / lax.optimization_barrier(jnp.sum(exponent, axis=0))[None, :]
    retain = jax.nn.sigmoid(filter_logits)
    mapped = retain[:, None] * mapping
    density = lax.optimization_barrier(jnp.sum(mapped, axis=0))
    cell_count = jnp.sum(enable * retain)
    predicted = jnp.dot(low(mapped).T, expression, precision=lax.Precision.HIGHEST)
    pred_used = low_back(predicted)
    gene_cos = lax.optimization_barrier(jnp.sum(pred_used * target, axis=0)) * lax.rsqrt(lax.optimization_barrier(jnp.sum(pred_used * pred_used, axis=0)) + epsilon) * lax.rsqrt(lax.optimization_barrier(jnp.sum(target * target, axis=0)) + epsilon)
    spot_cos = lax.optimization_barrier(jnp.sum(pred_used * target, axis=1)) * lax.rsqrt(lax.optimization_barrier(jnp.sum(pred_used * pred_used, axis=1)) + epsilon) * lax.rsqrt(lax.optimization_barrier(jnp.sum(target * target, axis=1)) + epsilon)
    count_total = jnp.sum(counts)
    kl_term = jnp.sum(counts * (jnp.log(counts) - jnp.log(density))) / count_total - jnp.log(count_total) + jnp.log(jnp.sum(density))
    offset = (cell_count - 0.5 * CELLS) / CELLS
    penalty = jnp.sqrt(offset * offset + 0.01)
    total_loss = -jnp.mean(gene_cos) - jnp.mean(spot_cos) + kl_term + penalty
    return (total_loss, predicted)

def reference(logits, filter_logits, expression, spot_expression, cell_mask, spot_counts):
    expr_wide = expression.astype(jnp.float32)
    enable = cell_mask.astype(jnp.float32)
    counts = spot_counts.astype(jnp.float32)

    def loss_of(logit_arg, filter_arg):
        return forward(logit_arg, filter_arg, expr_wide, spot_expression, enable, counts)
    total_loss, back_fn, predicted = jax.vjp(loss_of, logits, filter_logits, has_aux=True)
    grad_logits, filter_grad = back_fn(jnp.ones((), jnp.float32))
    return (predicted, total_loss, grad_logits, filter_grad)
```

```python
import functools

import jax
import jax.numpy as jnp
from jax import lax
from jax.experimental import pallas as pl
from jax.experimental.pallas import tpu as pltpu
from jax.sharding import PartitionSpec as P

epsilon = 1e-06
bf16 = jnp.bfloat16
f32 = jnp.float32
PIECES = 8
MIB = 1024 * 1024


def params(limit=48):
    return pltpu.CompilerParams(vmem_limit_bytes=limit * MIB)


def cost(flops=0, bytes_accessed=0, transcendentals=0):
    return pl.CostEstimate(flops=flops, bytes_accessed=bytes_accessed, transcendentals=transcendentals)


def col_stats_kernel(logits_ref, cell_ref, out_ref, top, total, dens):
    step = pl.program_id(0)

    @pl.when(step == 0)
    def _():
        top[...] = jnp.full_like(top, -1e30)
        total[...] = jnp.zeros_like(total)
        dens[...] = jnp.zeros_like(dens)

    rows, spots = logits_ref.shape
    cell = cell_ref[...]
    enable = cell[:, 0:1]
    retain = cell[:, 1:2]
    masked = jnp.where(enable > 0, logits_ref[...], -1e30)
    old = top[...]
    new = jnp.maximum(old, jnp.max(masked.reshape(rows // 8, 8, spots), axis=0))
    shrink = jnp.exp(old - new)
    part = jnp.exp(masked.reshape(rows // 8, 8, spots) - new[None]) * enable.reshape(rows // 8, 8, 1)
    top[...] = new
    total[...] = total[...] * shrink + jnp.sum(part, axis=0)
    dens[...] = dens[...] * shrink + jnp.sum(part * retain.reshape(rows // 8, 8, 1), axis=0)

    @pl.when(step == pl.num_programs(0) - 1)
    def _():
        slots = top[...]
        best = jnp.max(slots, axis=0, keepdims=True)
        scale = jnp.exp(slots - best)
        out_ref[0:1, :] = best
        out_ref[1:2, :] = jnp.sum(total[...] * scale, axis=0, keepdims=True)
        out_ref[2:3, :] = jnp.sum(dens[...] * scale, axis=0, keepdims=True)


def col_stats(logits, cell, block=512):
    cells, spots = logits.shape
    return pl.pallas_call(
        col_stats_kernel,
        grid=(cells // block,),
        in_specs=[
            pl.BlockSpec((block, spots), lambda i: (i, 0)),
            pl.BlockSpec((block, cell.shape[1]), lambda i: (i, 0)),
        ],
        out_specs=pl.BlockSpec((3, spots), lambda i: (0, 0)),
        out_shape=jax.ShapeDtypeStruct((3, spots), f32),
        scratch_shapes=[pltpu.VMEM((8, spots), f32)] * 3,
        compiler_params=params(),
        cost_estimate=cost(cells * spots * 8, cells * spots * 4, cells * spots),
        name="col_stats",
    )(logits, cell)


def mapped_kernel(order_ref, logits_ref, cell_ref, col_ref, out_ref):
    cell = cell_ref[...]
    weight = cell[:, 0:1] * cell[:, 1:2]
    masked = jnp.where(cell[:, 0:1] > 0, logits_ref[...], -1e30)
    mapping = jnp.exp(masked - col_ref[0:1, :]) * col_ref[1:2, :]
    out_ref[...] = (weight * mapping).T.astype(bf16)


def mapped_turned(order, logits, cell, col, block=512):
    cells, spots = logits.shape
    per = cells // PIECES // block

    def source(i, order):
        return (order[i // per] * per + i % per, 0)

    return pl.pallas_call(
        mapped_kernel,
        grid_spec=pltpu.PrefetchScalarGridSpec(
            num_scalar_prefetch=1,
            grid=(cells // block,),
            in_specs=[
                pl.BlockSpec((block, spots), source),
                pl.BlockSpec((block, cell.shape[1]), source),
                pl.BlockSpec((2, spots), lambda i, order: (0, 0)),
            ],
            out_specs=pl.BlockSpec((spots, block), lambda i, order: (0, i)),
        ),
        out_shape=jax.ShapeDtypeStruct((spots, cells), bf16),
        compiler_params=params(),
        cost_estimate=cost(cells * spots * 6, cells * spots * 6, cells * spots),
        name="mapped_turned",
    )(order, logits, cell, col)


def forward_kernel(table, spots, wide, mapped_ref, *refs):
    n = len(table)
    own_refs, other_refs = refs[:n], refs[n : 2 * n]
    pred_ref, panel_ref = refs[2 * n :]
    step = pl.program_id(0)

    @pl.when(step == 0)
    def _():
        pred_ref[...] = jnp.zeros_like(pred_ref)

    for source in range(n):
        used = [r for r in range(PIECES) if table[source][r] is not None]

        @pl.when(functools.reduce(jnp.logical_or, [step == r for r in used]))
        def _(source=source):
            both = jnp.concatenate([own_refs[source][...], other_refs[source][...]], axis=1)
            panel_ref[...] = both
            pred_ref[...] += jnp.dot(mapped_ref[...], both, preferred_element_type=f32)


def block_of(row):
    filled = []
    last = next(v for v in row if v is not None)
    for v in row:
        last = last if v is None else v
        filled.append(last)

    def pick(i):
        at = jnp.int32(filled[0])
        for r in range(1, len(filled)):
            if filled[r] != filled[r - 1]:
                at = jnp.where(i >= r, jnp.int32(filled[r]), at)
        return at

    return pick


def forward(mapped, own, other, table, columns, wide):
    spots, cells = mapped.shape
    rows = cells // PIECES
    specs = []
    for s in range(len(own)):
        pick = block_of(table[s])
        specs.append(pl.BlockSpec((rows, wide), lambda i, pick=pick, c=columns[s]: (pick(i), c)))
    return pl.pallas_call(
        functools.partial(forward_kernel, table, spots, wide),
        grid=(PIECES,),
        in_specs=[pl.BlockSpec((spots, rows), lambda i: (0, i))] + specs + specs,
        out_specs=[
            pl.BlockSpec((spots, 2 * wide), lambda i: (0, 0)),
            pl.BlockSpec((rows, 2 * wide), lambda i: (i, 0)),
        ],
        out_shape=[
            jax.ShapeDtypeStruct((spots, 2 * wide), f32),
            jax.ShapeDtypeStruct((cells, 2 * wide), bf16),
        ],
        compiler_params=params(),
        cost_estimate=cost(4 * spots * cells * wide, 2 * cells * (spots + 4 * wide)),
        name="forward",
    )(mapped, *own, *other)


def stats_kernel(wide, near_ref, far_ref, own_ref, other_ref, pred_ref, gene_ref, spot_ref):
    pred = near_ref[...] + far_ref[...]
    pred_ref[...] = pred
    target = jnp.concatenate([own_ref[...], other_ref[...]], axis=1)
    terms = (pred * target, pred * pred, target * target)
    lane = lax.broadcasted_iota(jnp.int32, spot_ref.shape, 1)
    spot = jnp.zeros(spot_ref.shape, f32)
    for k, term in enumerate(terms):
        gene_ref[k : k + 1, :] = jnp.sum(term, axis=0, keepdims=True)
        spot = jnp.where(lane == k, jnp.sum(term, axis=1, keepdims=True), spot)
    spot_ref[...] = spot


def pred_stats(near, far, target_own, target_other, column, wide):
    spots = near.shape[0]
    whole = pl.BlockSpec((spots, 2 * wide), lambda i: (0, 0))
    part = pl.BlockSpec((spots, wide), lambda i: (0, column))
    return pl.pallas_call(
        functools.partial(stats_kernel, wide),
        grid=(1,),
        in_specs=[whole, whole, part, part],
        out_specs=[
            whole,
            pl.BlockSpec((3, 2 * wide), lambda i: (0, 0)),
            pl.BlockSpec((spots, 4), lambda i: (0, 0)),
        ],
        out_shape=[
            jax.ShapeDtypeStruct((spots, 2 * wide), f32),
            jax.ShapeDtypeStruct((3, 2 * wide), f32),
            jax.ShapeDtypeStruct((spots, 4), f32),
        ],
        compiler_params=params(),
        cost_estimate=cost(spots * wide * 20, spots * wide * 40),
        name="pred_stats",
    )(near, far, target_own, target_other)


def grad_pred_kernel(widths, genes_total, spots_total, spot_ref, gene_ref, own_ref, other_ref, *refs):
    n = len(widths)
    pred_refs = refs[:n]
    turned_ref, inner_ref, sums_ref = refs[n:]
    spot = spot_ref[...]
    spot_pg, spot_pp, spot_gg = spot[:, 0:1], spot[:, 1:2], spot[:, 2:3]
    spot_scale = lax.rsqrt(spot_pp + epsilon) * lax.rsqrt(spot_gg + epsilon)
    spot_cos = spot_pg * spot_scale
    spot_back = spot_cos / (spot_pp + epsilon)
    gene = gene_ref[...]
    gene_scale = lax.rsqrt(gene[1:2, :] + epsilon) * lax.rsqrt(gene[2:3, :] + epsilon)
    gene_cos = gene[0:1, :] * gene_scale
    gene_back = gene_cos / (gene[1:2, :] + epsilon)
    folded = jnp.zeros((spot.shape[0], 128), f32)
    at = 0
    low = 0
    for q in range(n):
        wide = widths[q]
        pred = pred_refs[q][...]
        target = jnp.concatenate([own_ref[:, low : low + wide], other_ref[:, low : low + wide]], axis=1)
        cols = slice(at, at + 2 * wide)
        grad = -(target * gene_scale[:, cols] - gene_back[:, cols] * pred) / genes_total
        grad = grad - (target * spot_scale - spot_back * pred) / spots_total
        grad_low = grad.astype(bf16)
        turned_ref[at : at + 2 * wide, :] = grad_low.astype(f32).T.astype(bf16)
        prod = grad_low.astype(f32) * pred
        for k in range(0, 2 * wide, 128):
            folded = folded + prod[:, k : k + 128]
        at += 2 * wide
        low += wide
    inner_ref[...] = jnp.sum(folded.T, axis=0, keepdims=True)
    lane = lax.broadcasted_iota(jnp.int32, (1, 128), 1)
    gene_sum = jnp.sum(gene_cos, axis=1, keepdims=True)
    spot_sum = jnp.sum(spot_cos, axis=0, keepdims=True)
    sums_ref[...] = jnp.where(lane == 0, gene_sum, jnp.where(lane == 1, spot_sum, 0.0))


def grad_pred(widths, genes_total, spots_total, spot, gene, target_own, target_other, preds):
    spots, half = target_own.shape
    genes = 2 * half
    return pl.pallas_call(
        functools.partial(grad_pred_kernel, widths, genes_total, spots_total),
        out_shape=[
            jax.ShapeDtypeStruct((genes, spots), bf16),
            jax.ShapeDtypeStruct((1, spots), f32),
            jax.ShapeDtypeStruct((1, 128), f32),
        ],
        compiler_params=params(),
        cost_estimate=cost(spots * genes * 14, spots * genes * 10),
        name="grad_pred",
    )(spot, gene, target_own, target_other, *preds)


def backward_kernel(widths, order_ref, logits_ref, cell_ref, col_ref, turned_ref, *refs):
    n = len(widths)
    panel_refs = refs[:n]
    grad_ref, row_ref = refs[n:]
    panel = jnp.concatenate([ref[...] for ref in panel_refs], axis=1)
    inner = jnp.dot(panel, turned_ref[...], preferred_element_type=f32)
    cell = cell_ref[...]
    enable, retain = cell[:, 0:1], cell[:, 1:2]
    grad_mapped = inner + col_ref[2:3, :]
    masked = jnp.where(enable > 0, logits_ref[...], -1e30)
    mapping = enable * (jnp.exp(masked - col_ref[0:1, :]) * col_ref[1:2, :])
    grad_ref[...] = mapping * (retain * grad_mapped - col_ref[3:4, :])
    prod = grad_mapped * mapping
    folded = prod[:, 0:128]
    for k in range(128, prod.shape[1], 128):
        folded = folded + prod[:, k : k + 128]
    row_ref[...] = jnp.sum(folded.T, axis=0, keepdims=True)[None]


def backward(order, logits, cell, col, turned, panels, block=512):
    cells, spots = logits.shape
    genes = turned.shape[0]
    per = cells // PIECES // block
    widths = tuple(p.shape[1] for p in panels)

    def place(i, order):
        return (order[i // per] * per + i % per, 0)

    return pl.pallas_call(
        functools.partial(backward_kernel, widths),
        grid_spec=pltpu.PrefetchScalarGridSpec(
            num_scalar_prefetch=1,
            grid=(cells // block,),
            in_specs=[
                pl.BlockSpec((block, spots), place),
                pl.BlockSpec((block, cell.shape[1]), place),
                pl.BlockSpec((4, spots), lambda i, order: (0, 0)),
                pl.BlockSpec((genes, spots), lambda i, order: (0, 0)),
            ]
            + [pl.BlockSpec((block, w), lambda i, order: (i, 0)) for w in widths],
            out_specs=[
                pl.BlockSpec((block, spots), place),
                pl.BlockSpec((1, 1, block), lambda i, order: place(i, order) + (0,)),
            ],
        ),
        out_shape=[
            jax.ShapeDtypeStruct((cells, spots), f32),
            jax.ShapeDtypeStruct((cells // block, 1, block), f32),
        ],
        compiler_params=params(56),
        cost_estimate=cost(2 * cells * spots * genes, cells * (8 * spots + 2 * genes), cells * spots),
        name="backward",
    )(order, logits, cell, col, turned, *panels)


def swap_cells(x):
    return lax.ppermute(x, "cells", [(0, 1), (1, 0)])


def swap_genes(x):
    return lax.ppermute(x, "genes", [(0, 1), (1, 0)])


def line(spots):
    near = [(2 * z + y, 2 * (z ^ 1) + y) for z in range(4) for y in range(2)]
    middle = [(2 * z + y, 2 * (3 - z) + y) for z in (1, 2) for y in range(2)]
    across = [(i, i ^ 1) for i in range(8)]
    return near, middle, across


def sum_spots_genes(x, mirror=lambda v: v):
    if lax.axis_size("spots") != 8:
        x = lax.psum(x, "spots")
        return x + mirror(swap_genes(x))
    moved = [lax.ppermute(x, "spots", [(i, i ^ d) for i in range(8)]) for d in (2, 4, 6)]
    x = (x + moved[0]) + (moved[1] + moved[2])
    pairs = [lax.ppermute(x, ("spots", "genes"), [(i, i ^ d) for i in range(16)]) for d in (1, 2, 3)]
    return (x + pairs[1]) + mirror(pairs[0] + pairs[2])


def gathered(expression):
    rows, half = expression.shape
    if lax.axis_size("spots") != 8:
        own = lax.all_gather(expression, "spots", axis=0, tiled=True)
        other = swap_genes(own)
        wide = half // 4
        table = (tuple(range(PIECES)),)
        return jnp.arange(PIECES, dtype=jnp.int32), [
            (wide, q * wide, [own], [other], table, (q,)) for q in range(4)
        ]
    near, middle, across = line(8)
    spot = lax.axis_index("spots")
    z, y = spot // 2, spot % 2
    inside = (z == 1) | (z == 2)
    low = z < 2
    column = jnp.stack([z, z ^ 1, jnp.where(low, 2, 1), jnp.where(low, 3, 0)])
    order = jnp.concatenate([2 * column + y, 2 * column + (1 - y)]).astype(jnp.int32)

    def move(x, pairs):
        return lax.ppermute(x, "spots", pairs)

    beside = move(expression, across)
    own_other = swap_genes(expression)
    beside_other = swap_genes(beside)
    unit = half // 8
    plan = [(2 * unit, False), (2 * unit, False), (unit, False), (unit, False), (unit, False), (unit, True)]
    chunks = []
    at = 0
    for wide, early in plan:
        sent = expression[:, at : at + wide]
        if early:
            sent = jnp.concatenate([sent, beside[:, at : at + wide]], axis=0)
        near1 = move(sent, near)
        mid1 = move(sent, middle)
        mid2 = move(near1, middle)
        near2 = move(mid1, near)
        near3 = move(mid2, near)
        rest = jnp.concatenate([near1, jnp.where(inside, mid1, near2), jnp.where(inside, mid2, near3)], axis=0)
        rest_other = swap_genes(rest)
        x = None
        if early:
            table = (
                (0, x, x, x, x, x, x, x),
                (x, 0, 2, 4, x, 1, 3, 5),
                (x, x, x, x, 0, x, x, x),
            )
            own = [expression, rest, beside]
            other = [own_other, rest_other, beside_other]
            columns = (at // wide, 0, at // wide)
        else:
            table = (
                (0, x, x, x, x, x, x, x),
                (x, 0, 1, 2, x, x, x, x),
                (x, x, x, x, 0, x, x, x),
                (x, x, x, x, x, 0, 1, 2),
            )
            far = move(rest, across)
            far_other = swap_genes(far)
            own = [expression, rest, beside, far]
            other = [own_other, rest_other, beside_other, far_other]
            columns = (at // wide, 0, at // wide, 0)
        chunks.append((wide, at, own, other, table, columns))
        at += wide
    return order, chunks


def body(logits, filter_logits, expression, spot_expression, cell_mask, spot_counts):
    core = lax.axis_index("genes")
    cells_total = logits.shape[0] * lax.axis_size("cells")
    spots = logits.shape[1]
    spots_total = spots * lax.axis_size("spots") * lax.axis_size("genes")
    genes_total = expression.shape[1] * lax.axis_size("genes")

    order, chunks = gathered(expression)

    target_own = lax.dynamic_slice_in_dim(spot_expression, core * spots, spots, 0)
    target_other = swap_genes(lax.dynamic_slice_in_dim(spot_expression, (1 - core) * spots, spots, 0))

    enable = cell_mask.astype(f32)
    retain = jax.nn.sigmoid(filter_logits)
    cell = jnp.stack([enable, retain], axis=1)
    part = col_stats(logits, cell)
    part = jnp.concatenate([part, jnp.broadcast_to(jnp.sum(enable * retain), (1, spots))], axis=0)
    away = swap_cells(part)
    col_top = jnp.maximum(part[0], away[0])
    here, there = jnp.exp(part[0] - col_top), jnp.exp(away[0] - col_top)
    col_total = part[1] * here + away[1] * there
    density = (part[2] * here + away[2] * there) / col_total
    cell_count = part[3, 0] + away[3, 0]
    inverse = 1.0 / col_total
    col = jnp.stack([col_top, inverse])
    mapped = mapped_turned(order, logits, cell, col)

    counts = spot_counts.astype(f32)
    totals = sum_spots_genes(
        jnp.stack([jnp.sum(density), jnp.sum(counts * (jnp.log(counts) - jnp.log(density))), jnp.sum(counts)])
    )
    dens_total, kl_part, count_total = totals[0], totals[1], totals[2]
    kl_term = kl_part / count_total - jnp.log(count_total) + jnp.log(dens_total)
    offset = (cell_count - 0.5 * cells_total) / cells_total
    penalty = jnp.sqrt(offset * offset + 0.01)
    dens_grad = -counts / (count_total * density) + 1.0 / dens_total

    widths, preds, panels, genes_stats, spot_stats = [], [], [], [], []
    for wide, at, own, other, table, columns in chunks:
        partial, panel = forward(mapped, own, other, table, columns, wide)
        pred, gene_stat, spot_stat = pred_stats(
            partial, swap_cells(partial), target_own, target_other, at // wide, wide
        )
        widths.append(wide)
        preds.append(pred)
        panels.append(panel)
        genes_stats.append(gene_stat)
        spot_stats.append(spot_stat)

    def mirrored(some):
        def mirror(v):
            out, at = [], 0
            for wide in some:
                out += [v[:, at + wide : at + 2 * wide], v[:, at : at + wide]]
                at += 2 * wide
            return jnp.concatenate(out, axis=1)

        return mirror

    n = len(widths)
    last = n - 2
    early = [q for q in range(n) if q != last]
    early_sum = sum_spots_genes(
        jnp.concatenate([genes_stats[q] for q in early], axis=1), mirrored([widths[q] for q in early])
    )
    last_sum = sum_spots_genes(genes_stats[last], mirrored([widths[last]]))
    split = 2 * sum(widths[:last])
    gene = jnp.concatenate([early_sum[:, :split], last_sum, early_sum[:, split:]], axis=1)
    spot = functools.reduce(jnp.add, spot_stats)

    turned, inner, sums = grad_pred(
        tuple(widths), genes_total, spots_total, spot, gene, target_own, target_other, preds
    )
    col = jnp.stack([col_top, inverse, dens_grad, inner[0] + density * dens_grad])
    grad_logits, row = backward(order, logits, cell, col, turned, panels)

    all_sums = sum_spots_genes(sums)
    copies = lax.axis_size("spots") * lax.axis_size("genes")
    gene_sum, spot_sum = all_sums[0, 0] / copies, all_sums[0, 1]
    total_loss = -gene_sum / genes_total - spot_sum / spots_total + kl_term + penalty

    retain_grad = sum_spots_genes(row.reshape(-1, 128)).reshape(-1)
    retain_grad = retain_grad + enable * offset / (penalty * cells_total)
    filter_grad = retain_grad * retain * (1.0 - retain)

    mine = jnp.concatenate([p[:, :w] for p, w in zip(preds, widths)], axis=1)
    theirs = swap_genes(jnp.concatenate([p[:, w:] for p, w in zip(preds, widths)], axis=1))
    predicted = jnp.where(core == 0, jnp.concatenate([mine, theirs]), jnp.concatenate([theirs, mine]))
    return (predicted, total_loss, grad_logits, filter_grad)


def solution(mesh):
    placed = (
        P("cells", ("spots", "genes")),
        P("cells"),
        P(("cells", "spots"), "genes"),
        P("spots", "genes"),
        P("cells"),
        P(("spots", "genes")),
    )
    return jax.shard_map(
        body,
        mesh=mesh,
        in_specs=placed,
        out_specs=(P("spots", "genes"), P(), P("cells", ("spots", "genes")), P("cells")),
        check_vma=False,
    )
```

```python
import functools

import jax
import jax.numpy as jnp
from jax import lax
from jax.experimental import pallas as pl
from jax.experimental.pallas import tpu as pltpu
from jax.sharding import PartitionSpec as P

epsilon = 1e-06
bf16 = jnp.bfloat16
f32 = jnp.float32
PIECES = 8
MIB = 1024 * 1024
VMEM = pl.BlockSpec(memory_space=pltpu.VMEM)


def params(limit):
    return pltpu.CompilerParams(vmem_limit_bytes=limit * MIB)


def cost(flops=0, bytes_accessed=0, transcendentals=0):
    return pl.CostEstimate(flops=flops, bytes_accessed=bytes_accessed, transcendentals=transcendentals)


def hold(*values):
    return lax.optimization_barrier(values)


def col_stats_kernel(logits_ref, enable_ref, retain_ref, out_ref, top, total, dens):
    step = pl.program_id(0)

    @pl.when(step == 0)
    def _():
        top[...] = jnp.full_like(top, -1e29)
        total[...] = jnp.zeros_like(total)
        dens[...] = jnp.zeros_like(dens)

    rows, spots = logits_ref.shape
    enable = enable_ref[...].T
    retain = retain_ref[...].T
    blocks = []
    new = top[...]
    for k in range(rows // 128):
        block = jnp.where(enable[:, k : k + 1] > 0, logits_ref[128 * k : 128 * (k + 1), :], -1e30)
        blocks.append(block.reshape(16, 8, spots))
        new = jnp.maximum(new, jnp.max(blocks[-1], axis=0))
    shrink = jnp.exp(top[...] - new)
    top[...] = new
    sums = total[...] * shrink
    kept = dens[...] * shrink
    for k in range(rows // 128):
        part = jnp.exp(blocks[k] - new[None])
        share = jnp.broadcast_to(retain[:, k : k + 1], (128, spots)).reshape(16, 8, spots)
        sums = sums + jnp.sum(part, axis=0)
        kept = kept + jnp.sum(part * share, axis=0)
    total[...] = sums
    dens[...] = kept

    @pl.when(step == pl.num_programs(0) - 1)
    def _():
        best = jnp.max(new, axis=0, keepdims=True)
        scale = jnp.exp(new - best)
        out_ref[0:1, :] = best
        out_ref[1:2, :] = jnp.sum(sums * scale, axis=0, keepdims=True)
        out_ref[2:3, :] = jnp.sum(kept * scale, axis=0, keepdims=True)


def col_stats(logits, enable, retain, block=1024):
    cells, spots = logits.shape
    cell = pl.BlockSpec((block // 128, 128), lambda i: (i, 0))
    return pl.pallas_call(
        col_stats_kernel,
        grid=(cells // block,),
        in_specs=[pl.BlockSpec((block, spots), lambda i: (i, 0)), cell, cell],
        out_specs=pl.BlockSpec((3, spots), lambda i: (0, 0)),
        out_shape=jax.ShapeDtypeStruct((3, spots), f32),
        scratch_shapes=[pltpu.VMEM((8, spots), f32)] * 3,
        compiler_params=params(20),
        cost_estimate=cost(cells * spots * 8, cells * spots * 4, cells * spots),
        name="col_stats",
    )(logits, enable, retain)


def mapped_kernel(order_ref, logits_ref, enable_ref, retain_ref, shift_ref, out_ref):
    rows, spots = logits_ref.shape
    enable = enable_ref[...].T
    retain = retain_ref[...].T
    shift = shift_ref[...]
    for k in range(rows // 128):
        block = jnp.where(enable[:, k : k + 1] > 0, logits_ref[128 * k : 128 * (k + 1), :], -1e30)
        mapped = retain[:, k : k + 1] * jnp.exp(block - shift)
        out_ref[:, 128 * k : 128 * (k + 1)] = mapped.astype(bf16).T


def mapped_turned(order, logits, enable, retain, shift):
    cells, spots = logits.shape
    block = cells // PIECES
    cell = pl.BlockSpec((block // 128, 128), lambda i, order: (order[i], 0))
    return pl.pallas_call(
        mapped_kernel,
        grid_spec=pltpu.PrefetchScalarGridSpec(
            num_scalar_prefetch=1,
            grid=(PIECES,),
            in_specs=[
                pl.BlockSpec((block, spots), lambda i, order: (order[i], 0)),
                cell,
                cell,
                pl.BlockSpec((1, spots), lambda i, order: (0, 0)),
            ],
            out_specs=pl.BlockSpec((spots, block), lambda i, order: (0, i)),
        ),
        out_shape=jax.ShapeDtypeStruct((spots, cells), bf16),
        compiler_params=params(20),
        cost_estimate=cost(cells * spots * 6, cells * spots * 6, cells * spots),
        name="mapped_turned",
    )(order, logits, enable, retain, shift)


def forward_kernel(table, rows, mapped_ref, *refs):
    n = (len(refs) - 2) // 2
    own_refs, other_refs = refs[:n], refs[n : 2 * n]
    pred_ref, panel_ref = refs[2 * n :]
    total = None
    for r, (source, block) in enumerate(table):
        part = slice(block * rows, (block + 1) * rows)
        both = jnp.concatenate([own_refs[source][part, :], other_refs[source][part, :]], axis=1)
        here = slice(r * rows, (r + 1) * rows)
        panel_ref[here, :] = both
        more = jnp.dot(mapped_ref[:, here], both, preferred_element_type=f32)
        total = more if total is None else total + more
    pred_ref[...] = total


def forward(mapped, own, other, table, column, wide):
    spots, cells = mapped.shape
    rows = cells // PIECES
    specs = []
    for x in own:
        cut = x.shape[1] != wide
        specs.append(pl.BlockSpec((x.shape[0], wide), lambda i: (0, column)) if cut else VMEM)
    return pl.pallas_call(
        functools.partial(forward_kernel, table, rows),
        grid=(1,),
        in_specs=[VMEM] + specs + specs,
        out_specs=[VMEM, VMEM],
        out_shape=[
            jax.ShapeDtypeStruct((spots, 2 * wide), f32),
            pltpu.VMEM((cells, 2 * wide), bf16),
        ],
        compiler_params=params(12),
        cost_estimate=cost(4 * spots * cells * wide, 2 * cells * (spots + 4 * wide)),
        name="forward",
    )(mapped, *own, *other)


def stats_kernel(wide, near_ref, far_ref, own_ref, other_ref, pred_ref, gene_ref, spot_ref):
    pred = near_ref[...] + far_ref[...]
    pred_ref[...] = pred
    target = jnp.concatenate([own_ref[...], other_ref[...]], axis=1)
    terms = (pred * target, pred * pred, target * target)
    lane = lax.broadcasted_iota(jnp.int32, spot_ref.shape, 1)
    spot = jnp.zeros(spot_ref.shape, f32)
    for k, term in enumerate(terms):
        gene_ref[k : k + 1, :] = jnp.sum(term, axis=0, keepdims=True)
        spot = jnp.where(lane == k, jnp.sum(term, axis=1, keepdims=True), spot)
    spot_ref[...] = spot


def pred_stats(near, far, target_own, target_other, column, wide):
    spots = near.shape[0]
    whole = pl.BlockSpec((spots, 2 * wide), lambda i: (0, 0))
    part = pl.BlockSpec((spots, wide), lambda i: (0, column))
    return pl.pallas_call(
        functools.partial(stats_kernel, wide),
        grid=(1,),
        in_specs=[whole, whole, part, part],
        out_specs=[
            whole,
            pl.BlockSpec((3, 2 * wide), lambda i: (0, 0)),
            pl.BlockSpec((spots, 4), lambda i: (0, 0)),
        ],
        out_shape=[
            jax.ShapeDtypeStruct((spots, 2 * wide), f32),
            jax.ShapeDtypeStruct((3, 2 * wide), f32),
            jax.ShapeDtypeStruct((spots, 4), f32),
        ],
        compiler_params=params(16),
        cost_estimate=cost(spots * wide * 20, spots * wide * 40),
        name="pred_stats",
    )(near, far, target_own, target_other)


def grad_pred_kernel(widths, genes_total, spots_total, spot_ref, gene_ref, own_ref, other_ref, *refs):
    n = len(widths)
    pred_refs = refs[:n]
    turned_ref, inner_ref, sums_ref = refs[n:]
    spot = spot_ref[...]
    spot_pg, spot_pp, spot_gg = spot[:, 0:1], spot[:, 1:2], spot[:, 2:3]
    spot_scale = lax.rsqrt(spot_pp + epsilon) * lax.rsqrt(spot_gg + epsilon)
    spot_cos = spot_pg * spot_scale
    spot_back = spot_cos / (spot_pp + epsilon)
    gene = gene_ref[...]
    gene_scale = lax.rsqrt(gene[1:2, :] + epsilon) * lax.rsqrt(gene[2:3, :] + epsilon)
    gene_cos = gene[0:1, :] * gene_scale
    gene_back = gene_cos / (gene[1:2, :] + epsilon)
    folded = jnp.zeros((spot.shape[0], 128), f32)
    at = 0
    low = 0
    for q in range(n):
        wide = widths[q]
        pred = pred_refs[q][...]
        target = jnp.concatenate([own_ref[:, low : low + wide], other_ref[:, low : low + wide]], axis=1)
        cols = slice(at, at + 2 * wide)
        grad = -(target * gene_scale[:, cols] - gene_back[:, cols] * pred) / genes_total
        grad = grad - (target * spot_scale - spot_back * pred) / spots_total
        grad_low = grad.astype(bf16)
        turned_ref[at : at + 2 * wide, :] = grad_low.T
        prod = grad_low.astype(f32) * pred
        for k in range(0, 2 * wide, 128):
            folded = folded + prod[:, k : k + 128]
        at += 2 * wide
        low += wide
    inner_ref[...] = jnp.sum(folded.T, axis=0, keepdims=True)
    lane = lax.broadcasted_iota(jnp.int32, (1, 128), 1)
    gene_sum = jnp.sum(gene_cos, axis=1, keepdims=True)
    spot_sum = jnp.sum(spot_cos, axis=0, keepdims=True)
    sums_ref[...] = jnp.where(lane == 0, gene_sum, jnp.where(lane == 1, spot_sum, 0.0))


def grad_pred(widths, genes_total, spots_total, spot, gene, target_own, target_other, preds):
    spots, half = target_own.shape
    genes = 2 * half
    return pl.pallas_call(
        functools.partial(grad_pred_kernel, widths, genes_total, spots_total),
        in_specs=[VMEM] * (4 + len(preds)),
        out_specs=[VMEM] * 3,
        out_shape=[
            pltpu.VMEM((genes, spots), bf16),
            jax.ShapeDtypeStruct((1, spots), f32),
            jax.ShapeDtypeStruct((1, 128), f32),
        ],
        compiler_params=params(12),
        cost_estimate=cost(spots * genes * 14, spots * genes * 10),
        name="grad_pred",
    )(spot, gene, target_own, target_other, *preds)


def backward_kernel(widths, order_ref, logits_ref, enable_ref, retain_ref, col_ref, turned_ref, *refs):
    n = len(widths)
    panel_refs = refs[:n]
    grad_ref, row_ref = refs[n:]
    rows, spots = logits_ref.shape
    first = pl.multiple_of(pl.program_id(0) * rows, rows)
    enable = enable_ref[...].T
    retain = retain_ref[...].T
    shift, dens, inner = col_ref[0:1, :], col_ref[1:2, :], col_ref[2:3, :]
    part = rows // 2
    for h in range(2):
        here = pl.ds(first + h * part, part)
        panel = jnp.concatenate([ref[here, :] for ref in panel_refs], axis=1)
        grad_mapped = jnp.dot(panel, turned_ref[...], preferred_element_type=f32) + dens
        for k in range(part // 128):
            at = h * (part // 128) + k
            lines = slice(128 * at, 128 * (at + 1))
            block = jnp.where(enable[:, at : at + 1] > 0, logits_ref[lines, :], -1e30)
            mapping = jnp.exp(block - shift)
            grad = grad_mapped[128 * k : 128 * (k + 1), :]
            grad_ref[lines, :] = mapping * (retain[:, at : at + 1] * grad - inner)
            prod = grad * mapping
            folded = prod[:, 0:128]
            for c in range(128, spots, 128):
                folded = folded + prod[:, c : c + 128]
            row_ref[at : at + 1, :] = jnp.sum(folded.T, axis=0, keepdims=True)


def backward(order, logits, enable, retain, col, turned, panels):
    cells, spots = logits.shape
    genes = turned.shape[0]
    block = cells // PIECES
    widths = tuple(p.shape[1] for p in panels)
    cell = pl.BlockSpec((block // 128, 128), lambda i, order: (order[i], 0))
    return pl.pallas_call(
        functools.partial(backward_kernel, widths),
        grid_spec=pltpu.PrefetchScalarGridSpec(
            num_scalar_prefetch=1,
            grid=(PIECES,),
            in_specs=[
                pl.BlockSpec((block, spots), lambda i, order: (order[i], 0)),
                cell,
                cell,
                pl.BlockSpec((3, spots), lambda i, order: (0, 0)),
            ]
            + [VMEM] * (1 + len(panels)),
            out_specs=[pl.BlockSpec((block, spots), lambda i, order: (order[i], 0)), cell],
        ),
        out_shape=[
            jax.ShapeDtypeStruct((cells, spots), f32),
            jax.ShapeDtypeStruct((cells // 128, 128), f32),
        ],
        compiler_params=params(20),
        cost_estimate=cost(2 * cells * spots * genes, cells * 8 * spots, cells * spots),
        name="backward",
    )(order, logits, enable, retain, col, turned, *panels)


def stack_kernel(inside_ref, near_ref, mid1_ref, near2_ref, mid2_ref, near3_ref, *out_refs):
    rows = near_ref.shape[0]
    cut = out_refs[0].shape[1]
    inside = inside_ref[0] > 0
    for k, out in enumerate(out_refs):
        cols = slice(k * cut, (k + 1) * cut)
        out[0:rows, :] = near_ref[:, cols]

        @pl.when(inside)
        def _():
            out[rows : 2 * rows, :] = mid1_ref[:, cols]
            out[2 * rows : 3 * rows, :] = mid2_ref[:, cols]

        @pl.when(jnp.logical_not(inside))
        def _():
            out[rows : 2 * rows, :] = near2_ref[:, cols]
            out[2 * rows : 3 * rows, :] = near3_ref[:, cols]


def stack(inside, near, mid1, near2, mid2, near3, parts=1):
    rows, wide = near.shape
    return pl.pallas_call(
        stack_kernel,
        in_specs=[pl.BlockSpec(memory_space=pltpu.SMEM)] + [VMEM] * 5,
        out_specs=[VMEM] * parts,
        out_shape=[jax.ShapeDtypeStruct((3 * rows, wide // parts), bf16)] * parts,
        compiler_params=params(12),
        cost_estimate=cost(0, 12 * rows * wide),
        name="stack",
    )(inside, near, mid1, near2, mid2, near3)


def lay_kernel(core_ref, theirs_ref, *refs):
    out_ref = refs[-1]
    mine = pl.program_id(0) == core_ref[0]

    @pl.when(mine)
    def _():
        at = 0
        for ref in refs[:-1]:
            out_ref[:, at : at + ref.shape[1]] = ref[...]
            at += ref.shape[1]

    @pl.when(jnp.logical_not(mine))
    def _():
        out_ref[...] = theirs_ref[...]


def lay(core, theirs, preds):
    spots, half = theirs.shape
    return pl.pallas_call(
        lay_kernel,
        grid_spec=pltpu.PrefetchScalarGridSpec(
            num_scalar_prefetch=1,
            grid=(2,),
            in_specs=[pl.BlockSpec((spots, half), lambda i, core: (0, 0))]
            + [pl.BlockSpec((spots, p.shape[1] // 2), lambda i, core: (0, 0)) for p in preds],
            out_specs=pl.BlockSpec((spots, half), lambda i, core: (i, 0)),
        ),
        out_shape=jax.ShapeDtypeStruct((2 * spots, half), f32),
        compiler_params=params(20),
        cost_estimate=cost(0, spots * half * 16),
        name="lay",
    )(core, theirs, *preds)


def swap_cells(x):
    return lax.ppermute(x, "cells", [(0, 1), (1, 0)])


def swap_genes(x):
    return lax.ppermute(x, "genes", [(0, 1), (1, 0)])


def sum_spots_genes(x, mirror=lambda v: v):
    if lax.axis_size("spots") != 8:
        x = lax.psum(x, "spots")
        return x + mirror(swap_genes(x))
    moved = [lax.ppermute(x, "spots", [(i, i ^ d) for i in range(8)]) for d in (2, 4, 6)]
    x = (x + moved[0]) + (moved[1] + moved[2])
    pairs = [lax.ppermute(x, ("spots", "genes"), [(i, i ^ d) for i in range(16)]) for d in (1, 2, 3)]
    return (x + pairs[1]) + mirror(pairs[0] + pairs[2])


class Step:
    def __init__(self, logits, filter_logits, expression, spot_expression, cell_mask):
        self.logits = logits
        self.expression = expression
        self.core = lax.axis_index("genes")
        self.enable = cell_mask.astype(f32).reshape(-1, 128)
        self.retain = jax.nn.sigmoid(filter_logits).reshape(-1, 128)
        self.spots = logits.shape[1]
        mine = lax.dynamic_slice_in_dim(spot_expression, self.core * self.spots, self.spots, 0)
        theirs = lax.dynamic_slice_in_dim(spot_expression, (1 - self.core) * self.spots, self.spots, 0)
        self.target_own = mine
        self.target_sent = theirs
        self.half = expression.shape[1]

    def local_stats(self, logits):
        part = col_stats(logits, self.enable, self.retain)
        count = jnp.broadcast_to(jnp.sum(self.enable * self.retain), (1, self.spots))
        return jnp.concatenate([part, count], axis=0)

    def merge_stats(self, part, away):
        top = jnp.maximum(part[0], away[0])
        here, there = jnp.exp(part[0] - top), jnp.exp(away[0] - top)
        total = part[1] * here + away[1] * there
        self.density = (part[2] * here + away[2] * there) / total
        self.cell_count = part[3, 0] + away[3, 0]
        self.shift = (top + jnp.log(total))[None, :]

    def turned(self, order, shift):
        return mapped_turned(order, self.logits, self.enable, self.retain, shift)

    def stats(self, partial, away, at, wide):
        return pred_stats(partial, away, self.target_own, self.target_other, at // wide, wide)

    def gathered_whole(self):
        own = lax.all_gather(self.expression, "spots", axis=0, tiled=True)
        other = swap_genes(own)
        self.target_other = swap_genes(self.target_sent)
        part = self.local_stats(self.logits)
        self.merge_stats(part, swap_cells(part))
        order = jnp.arange(PIECES, dtype=jnp.int32)
        mapped = self.turned(order, self.shift)
        wide = self.half // 4
        table = tuple((0, r) for r in range(PIECES))
        chunks = []
        for q in range(4):
            cols = slice(q * wide, (q + 1) * wide)
            partial, panel = forward(mapped, [own[:, cols]], [other[:, cols]], table, 0, wide)
            chunks.append((wide, panel) + tuple(self.stats(partial, swap_cells(partial), q * wide, wide)))
        return order, chunks

    def gathered_line(self):
        near_pairs = [(2 * z + y, 2 * (z ^ 1) + y) for z in range(4) for y in range(2)]
        middle_pairs = [(2 * z + y, 2 * (3 - z) + y) for z in (1, 2) for y in range(2)]
        across_pairs = [(i, i ^ 1) for i in range(8)]

        def near(x):
            return lax.ppermute(x, "spots", near_pairs)

        def middle(x):
            return lax.ppermute(x, "spots", middle_pairs)

        def across(x):
            return lax.ppermute(x, "spots", across_pairs)

        spot = lax.axis_index("spots")
        z, y = spot // 2, spot % 2
        inside = (z == 1) | (z == 2)
        inside_flag = inside.astype(jnp.int32).reshape(1)
        column = jnp.stack([z, z ^ 1, jnp.where(z < 2, 2, 1), jnp.where(z < 2, 3, 0)])
        order = jnp.concatenate([2 * column + y, 2 * column + (1 - y)]).astype(jnp.int32)
        unit = self.half // 8
        expr = self.expression
        late_table = ((0, 0), (1, 0), (1, 1), (1, 2), (2, 0), (3, 0), (3, 1), (3, 2))
        split_table = ((0, 0), (1, 0), (1, 1), (2, 0), (3, 0), (4, 0), (4, 1), (5, 0))
        early_table = ((0, 0), (1, 0), (1, 2), (1, 4), (2, 0), (1, 1), (1, 3), (1, 5))

        def cut(x, at, wide):
            return x[:, at * unit : (at + wide) * unit]

        s0, s1 = cut(expr, 0, 2), cut(expr, 2, 2)
        a0, b0 = near(s0), middle(s0)
        beside = across(expr)
        a1, b1 = near(s1), middle(s1)
        expr_other = swap_genes(expr)
        part = self.local_stats(self.logits)
        a0, b0, part, target = hold(a0, b0, part, self.target_sent)
        a02, b02 = near(b0), middle(a0)
        away = swap_cells(part)
        target_other = swap_genes(target)
        s2, s3 = cut(expr, 4, 2), cut(expr, 6, 1)
        a1, b1, away, s2, s3, expr_other = hold(a1, b1, away, s2, s3, expr_other)
        a12, b12 = near(b1), middle(a1)
        self.merge_stats(part, away)
        mapped = self.turned(order, self.shift)
        a02, b02, mapped, self.target_other = hold(a02, b02, mapped, target_other)
        a03 = near(b02)
        nm0 = jnp.concatenate([a0, jnp.where(inside, b0, a02)], axis=0)
        y0nm = across(nm0)
        a12, b12, s2, nm0 = hold(a12, b12, s2, nm0)
        a13 = near(b12)
        a2, b2 = near(s2), middle(s2)
        nm0_other = swap_genes(nm0)
        a03, b02, s3 = hold(a03, b02, s3)
        f0 = jnp.where(inside, b02, a03)
        y0f = across(f0)
        f0_other = swap_genes(f0)
        a3, b3 = near(s3), middle(s3)
        a13, b12, beside, nm0_other = hold(a13, b12, beside, nm0_other)
        (rest1,) = stack(inside_flag, a1, b1, a12, b12, a13)
        y1 = across(rest1)
        rest1_other = swap_genes(rest1)
        beside_other = swap_genes(beside)
        sf = jnp.concatenate([cut(expr, 7, 1), cut(beside, 7, 1)], axis=0)
        a2, b2, y0nm, rest1, sf, f0_other = hold(a2, b2, y0nm, rest1, sf, f0_other)
        a22, b22 = near(b2), middle(a2)
        y0nm_other = swap_genes(y0nm)
        a3, b3, y0f, rest1_other = hold(a3, b3, y0f, rest1_other)
        a32, b32 = near(b3), middle(a3)
        y0f_other = swap_genes(y0f)
        a22, b22, y0f_other, y0nm_other, beside_other = hold(a22, b22, y0f_other, y0nm_other, beside_other)
        a23 = near(b22)
        partial0, panel0 = forward(
            mapped,
            [expr, nm0, f0, beside, y0nm, y0f],
            [expr_other, nm0_other, f0_other, beside_other, y0nm_other, y0f_other],
            split_table,
            0,
            2 * unit,
        )
        a32, b32, partial0, sf = hold(a32, b32, partial0, sf)
        a33 = near(b32)
        af, bf = near(sf), middle(sf)
        away0 = swap_cells(partial0)
        a23, b22 = hold(a23, b22)
        rest2, rest3 = stack(inside_flag, a2, b2, a22, b22, a23, parts=2)
        y2 = across(rest2)
        y3 = across(rest3)
        rest2_other, rest3_other = swap_genes(rest2), swap_genes(rest3)
        a33, y1, rest2 = hold(a33, y1, rest2)
        (rest4,) = stack(inside_flag, a3, b3, a32, b32, a33)
        y4 = across(rest4)
        rest4_other = swap_genes(rest4)
        y1_other = swap_genes(y1)
        af, bf, y1_other, rest4, rest2_other = hold(af, bf, y1_other, rest4, rest2_other)
        af2, bf2 = near(bf), middle(af)
        partial1, panel1 = forward(
            mapped,
            [expr, rest1, beside, y1],
            [expr_other, rest1_other, beside_other, y1_other],
            late_table,
            1,
            2 * unit,
        )
        af2, bf2, y2, partial1, away0 = hold(af2, bf2, y2, partial1, away0)
        af3 = near(bf2)
        away1 = swap_cells(partial1)
        y2_other = swap_genes(y2)
        stats0 = self.stats(partial0, away0, 0, 2 * unit)
        y2_other, rest3_other, rest4_other = hold(y2_other, rest3_other, rest4_other)
        partial2, panel2 = forward(
            mapped, [expr, rest2, beside, y2], [expr_other, rest2_other, beside_other, y2_other], late_table, 4, unit
        )
        y3, partial2 = hold(y3, partial2)
        away2 = swap_cells(partial2)
        y3_other = swap_genes(y3)
        af3, y3_other = hold(af3, y3_other)
        (restf,) = stack(inside_flag, af, bf, af2, bf2, af3)
        restf_other = swap_genes(restf)
        partial3, panel3 = forward(
            mapped, [expr, rest3, beside, y3], [expr_other, rest3_other, beside_other, y3_other], late_table, 5, unit
        )
        restf_other, partial3, away1 = hold(restf_other, partial3, away1)
        away3 = swap_cells(partial3)
        partialf, panelf = forward(
            mapped,
            [expr, restf, beside],
            [expr_other, restf_other, beside_other],
            early_table,
            7,
            unit,
        )
        y4, partialf = hold(y4, partialf)
        y4_other = swap_genes(y4)
        awayf = swap_cells(partialf)
        partial4, panel4 = forward(
            mapped, [expr, rest4, beside, y4], [expr_other, rest4_other, beside_other, y4_other], late_table, 6, unit
        )
        away4 = swap_cells(partial4)
        chunks = [(2 * unit, panel0) + tuple(stats0)]
        rows = [
            (partial1, away1, 2, 2, panel1),
            (partial2, away2, 4, 1, panel2),
            (partial3, away3, 5, 1, panel3),
            (partial4, away4, 6, 1, panel4),
            (partialf, awayf, 7, 1, panelf),
        ]
        for partial, away, at, wide, panel in rows:
            chunks.append((wide * unit, panel) + tuple(self.stats(partial, away, at * unit, wide * unit)))
        return order, chunks


def body(logits, filter_logits, expression, spot_expression, cell_mask, spot_counts):
    cells_total = logits.shape[0] * lax.axis_size("cells")
    spots = logits.shape[1]
    spots_total = spots * lax.axis_size("spots") * lax.axis_size("genes")
    genes_total = expression.shape[1] * lax.axis_size("genes")
    step = Step(logits, filter_logits, expression, spot_expression, cell_mask)
    order, chunks = step.gathered_line() if lax.axis_size("spots") == 8 else step.gathered_whole()
    widths, panels, preds, gene_stats, spot_stats = zip(*chunks)
    density = step.density

    counts = spot_counts.astype(f32)
    kl_parts = jnp.stack([jnp.sum(density), jnp.sum(counts * (jnp.log(counts) - jnp.log(density))), jnp.sum(counts)])

    def mirrored(some):
        def mirror(v):
            out, at = [], 0
            for wide in some:
                out += [v[:, at + wide : at + 2 * wide], v[:, at : at + wide]]
                at += 2 * wide
            return jnp.concatenate(out + [v[:, at:]], axis=1)

        return mirror

    early = len(widths) // 2
    early_sum = sum_spots_genes(
        jnp.concatenate(gene_stats[:early] + (jnp.broadcast_to(kl_parts[:, None], (3, 128)),), axis=1),
        mirrored(widths[:early]),
    )
    late_sum = sum_spots_genes(jnp.concatenate(gene_stats[early:], axis=1), mirrored(widths[early:]))
    split = 2 * sum(widths[:early])
    gene = jnp.concatenate([early_sum[:, :split], late_sum], axis=1)
    dens_total, kl_part, count_total = early_sum[0, split], early_sum[1, split], early_sum[2, split]
    kl_term = kl_part / count_total - jnp.log(count_total) + jnp.log(dens_total)
    offset = (step.cell_count - 0.5 * cells_total) / cells_total
    penalty = jnp.sqrt(offset * offset + 0.01)
    dens_grad = -counts / (count_total * density) + 1.0 / dens_total
    spot = functools.reduce(jnp.add, spot_stats)

    turned, inner, sums = grad_pred(
        widths, genes_total, spots_total, spot, gene, step.target_own, step.target_other, preds
    )
    theirs = swap_genes(jnp.concatenate([p[:, w:] for p, w in zip(preds, widths)], axis=1))
    col = jnp.concatenate([step.shift, dens_grad[None], inner + (density * dens_grad)[None]], axis=0)
    grad_logits, row = backward(order, logits, step.enable, step.retain, col, turned, panels)

    row_sums = sum_spots_genes(jnp.concatenate([row, sums], axis=0))
    copies = lax.axis_size("spots") * lax.axis_size("genes")
    gene_sum, spot_sum = row_sums[-1, 0] / copies, row_sums[-1, 1]
    total_loss = -gene_sum / genes_total - spot_sum / spots_total + kl_term + penalty
    retain_grad = row_sums[:-1] + step.enable * offset / (penalty * cells_total)
    filter_grad = (retain_grad * step.retain * (1.0 - step.retain)).reshape(-1)

    predicted = lay(step.core.astype(jnp.int32).reshape(1), theirs, preds)
    return (predicted, total_loss, grad_logits, filter_grad)


def solution(mesh):
    placed = (
        P("cells", ("spots", "genes")),
        P("cells"),
        P(("cells", "spots"), "genes"),
        P("spots", "genes"),
        P("cells"),
        P(("spots", "genes")),
    )
    return jax.shard_map(
        body,
        mesh=mesh,
        in_specs=placed,
        out_specs=(P("spots", "genes"), P(), P("cells", ("spots", "genes")), P("cells")),
        check_vma=False,
    )
```

```python
import functools

import jax
import jax.numpy as jnp
from jax import lax
from jax.experimental import pallas as pl
from jax.experimental.pallas import tpu as pltpu
from jax.sharding import PartitionSpec as P

epsilon = 1e-06
bf16 = jnp.bfloat16
f32 = jnp.float32
PIECES = 8
MIB = 1024 * 1024
VMEM = pl.BlockSpec(memory_space=pltpu.VMEM)


def params(limit):
    return pltpu.CompilerParams(vmem_limit_bytes=limit * MIB)


def cost(flops=0, bytes_accessed=0, transcendentals=0):
    return pl.CostEstimate(flops=1, bytes_accessed=1, transcendentals=0)


def in_hbm(x):
    return pltpu.with_memory_space_constraint(x, pltpu.HBM)


def hold(*values):
    return lax.optimization_barrier(values)


def col_stats_kernel(logits_ref, enable_ref, retain_ref, out_ref, top, total, dens):
    step = pl.program_id(0)

    @pl.when(step == 0)
    def _():
        top[...] = jnp.full_like(top, -1e29)
        total[...] = jnp.zeros_like(total)
        dens[...] = jnp.zeros_like(dens)

    rows, spots = logits_ref.shape
    enable = enable_ref[...].T
    retain = retain_ref[...].T
    blocks = []
    new = top[...]
    for k in range(rows // 128):
        block = jnp.where(enable[:, k : k + 1] > 0, logits_ref[128 * k : 128 * (k + 1), :], -1e30)
        blocks.append(block.reshape(16, 8, spots))
        new = jnp.maximum(new, jnp.max(blocks[-1], axis=0))
    shrink = jnp.exp(top[...] - new)
    top[...] = new
    sums = total[...] * shrink
    kept = dens[...] * shrink
    for k in range(rows // 128):
        part = jnp.exp(blocks[k] - new[None])
        share = jnp.broadcast_to(retain[:, k : k + 1], (128, spots)).reshape(16, 8, spots)
        sums = sums + jnp.sum(part, axis=0)
        kept = kept + jnp.sum(part * share, axis=0)
    total[...] = sums
    dens[...] = kept

    @pl.when(step == pl.num_programs(0) - 1)
    def _():
        best = jnp.max(new, axis=0, keepdims=True)
        scale = jnp.exp(new - best)
        out_ref[0:1, :] = best
        out_ref[1:2, :] = jnp.sum(sums * scale, axis=0, keepdims=True)
        out_ref[2:3, :] = jnp.sum(kept * scale, axis=0, keepdims=True)


def col_stats(logits, enable, retain, block=1024):
    cells, spots = logits.shape
    cell = pl.BlockSpec((block // 128, 128), lambda i: (i, 0))
    return pl.pallas_call(
        col_stats_kernel,
        grid=(cells // block,),
        in_specs=[pl.BlockSpec((block, spots), lambda i: (i, 0)), cell, cell],
        out_specs=pl.BlockSpec((3, spots), lambda i: (0, 0)),
        out_shape=jax.ShapeDtypeStruct((3, spots), f32),
        scratch_shapes=[pltpu.VMEM((8, spots), f32)] * 3,
        compiler_params=params(20),
        cost_estimate=cost(cells * spots * 8, cells * spots * 4, cells * spots),
        name="col_stats",
    )(logits, enable, retain)


def mapped_kernel(order_ref, logits_ref, enable_ref, retain_ref, shift_ref, out_ref):
    rows, spots = logits_ref.shape
    enable = enable_ref[...].T
    retain = retain_ref[...].T
    shift = shift_ref[...]
    for k in range(rows // 128):
        block = jnp.where(enable[:, k : k + 1] > 0, logits_ref[128 * k : 128 * (k + 1), :], -1e30)
        mapped = retain[:, k : k + 1] * jnp.exp(block - shift)
        out_ref[:, 128 * k : 128 * (k + 1)] = mapped.astype(bf16).T


def mapped_turned(order, logits, enable, retain, shift):
    cells, spots = logits.shape
    block = cells // PIECES
    cell = pl.BlockSpec((block // 128, 128), lambda i, order: (order[i], 0))
    return pl.pallas_call(
        mapped_kernel,
        grid_spec=pltpu.PrefetchScalarGridSpec(
            num_scalar_prefetch=1,
            grid=(PIECES,),
            in_specs=[
                pl.BlockSpec((block, spots), lambda i, order: (order[i], 0)),
                cell,
                cell,
                pl.BlockSpec((1, spots), lambda i, order: (0, 0)),
            ],
            out_specs=pl.BlockSpec((spots, block), lambda i, order: (0, i)),
        ),
        out_shape=pltpu.HBM((spots, cells), bf16),
        compiler_params=params(20),
        cost_estimate=cost(cells * spots * 6, cells * spots * 6, cells * spots),
        name="mapped_turned",
    )(order, logits, enable, retain, shift)


def forward_kernel(table, kinds, columns, rows, wide, core_ref, mapped_ref, *refs):
    sources, at = [], 0
    for kind in kinds:
        sources.append(refs[at : at + kind])
        at += kind
    pred_ref, panel_ref, held, turned, first_sems, second_sems, mapped_sems, panel_sems = refs[at:]

    def piece(r, which, column, sems):
        source, block = table[r]
        cols = pl.ds(columns[source] * wide, wide)
        if kinds[source] == 1:
            ref = sources[source][0]
            row = which * (ref.shape[0] // 2) + block * rows
        else:
            ref = sources[source][which]
            row = block * rows
        target = held.at[pl.ds(r * rows, rows), pl.ds(column, wide)]
        return pltpu.make_async_copy(ref.at[pl.ds(row, rows), cols], target, sems.at[r])

    def load(r):
        cols = pl.ds(r * rows, rows)
        return pltpu.make_async_copy(mapped_ref.at[:, cols], turned.at[:, cols], mapped_sems.at[r])

    def save(r):
        here = pl.ds(r * rows, rows)
        return pltpu.make_async_copy(held.at[here, :], panel_ref.at[here, :], panel_sems.at[r])

    for r in range(PIECES):
        if kinds[table[r][0]] == 1:
            piece(r, 0, 0, first_sems).start()
            piece(r, 1, wide, second_sems).start()
        else:
            for core in range(2):

                @pl.when(core_ref[0] == core)
                def _(core=core, r=r):
                    piece(r, 0, core * wide, first_sems).start()
                    piece(r, 1, (1 - core) * wide, second_sems).start()

        load(r).start()
    total = None
    for r in range(PIECES):
        piece(r, 0, 0, first_sems).wait()
        piece(r, 1, 0, second_sems).wait()
        save(r).start()
        load(r).wait()
        here = slice(r * rows, (r + 1) * rows)
        more = jnp.dot(turned[:, here], held[here, :], preferred_element_type=f32)
        total = more if total is None else total + more
    pred_ref[...] = total
    for r in range(PIECES):
        save(r).wait()


def forward(core, mapped, sources, table, columns, wide):
    spots, cells = mapped.shape
    rows = cells // PIECES
    sources = [x if isinstance(x, tuple) else (x,) for x in sources]
    arrays = [in_hbm(x) for source in sources for x in source]
    hbm = pl.BlockSpec(memory_space=pltpu.HBM)
    return pl.pallas_call(
        functools.partial(forward_kernel, table, [len(x) for x in sources], columns, rows, wide),
        in_specs=[pl.BlockSpec(memory_space=pltpu.SMEM), hbm] + [hbm] * len(arrays),
        out_specs=[VMEM, hbm],
        out_shape=[
            jax.ShapeDtypeStruct((spots, 2 * wide), f32),
            pltpu.HBM((cells, 2 * wide), bf16),
        ],
        scratch_shapes=[pltpu.VMEM((cells, 2 * wide), bf16), pltpu.VMEM((spots, cells), bf16)]
        + [pltpu.SemaphoreType.DMA((PIECES,))] * 4,
        compiler_params=params(14 + 16 * wide // 512),
        cost_estimate=cost(4 * spots * cells * wide, 2 * cells * (spots + 4 * wide)),
        name="forward",
    )(core, in_hbm(mapped), *arrays)


def stats_kernel(parts, core_ref, *refs):
    own_ref, other_ref, pred_ref, gene_ref, spot_ref = refs[parts:]
    pred = functools.reduce(jnp.add, [ref[...] for ref in refs[:parts]])
    pred_ref[...] = pred
    target = jnp.concatenate([own_ref[...], other_ref[...]], axis=1)
    terms = (pred * target, pred * pred, target * target)
    lane = lax.broadcasted_iota(jnp.int32, spot_ref.shape, 1)
    spot = jnp.zeros(spot_ref.shape, f32)
    for k, term in enumerate(terms):
        gene_ref[k : k + 1, :] = jnp.sum(term, axis=0, keepdims=True)
        spot = jnp.where(lane == k, jnp.sum(term, axis=1, keepdims=True), spot)
    spot_ref[...] = spot


def pred_stats(core, parts, target, column, wide):
    spots = parts[0].shape[0]
    whole = pl.BlockSpec((spots, 2 * wide), lambda i, core: (0, 0))
    return pl.pallas_call(
        functools.partial(stats_kernel, len(parts)),
        grid_spec=pltpu.PrefetchScalarGridSpec(
            num_scalar_prefetch=1,
            grid=(1,),
            in_specs=[whole] * len(parts)
            + [
                pl.BlockSpec((spots, wide), lambda i, core: (core[0], column)),
                pl.BlockSpec((spots, wide), lambda i, core: (2 + core[0], column)),
            ],
            out_specs=[
                whole,
                pl.BlockSpec((3, 2 * wide), lambda i, core: (0, 0)),
                pl.BlockSpec((spots, 4), lambda i, core: (0, 0)),
            ],
        ),
        out_shape=[
            jax.ShapeDtypeStruct((spots, 2 * wide), f32),
            jax.ShapeDtypeStruct((3, 2 * wide), f32),
            jax.ShapeDtypeStruct((spots, 4), f32),
        ],
        compiler_params=params(16),
        cost_estimate=cost(spots * wide * 20, spots * wide * 40),
        name="pred_stats",
    )(core, *parts, target, target)


def grad_pred_kernel(widths, genes_total, spots_total, core_ref, spot_ref, gene_ref, own_ref, other_ref, *refs):
    n = len(widths)
    pred_refs = refs[:n]
    turned_ref, inner_ref, sums_ref = refs[n:]
    spot = spot_ref[...]
    spot_pg, spot_pp, spot_gg = spot[:, 0:1], spot[:, 1:2], spot[:, 2:3]
    spot_scale = lax.rsqrt(spot_pp + epsilon) * lax.rsqrt(spot_gg + epsilon)
    spot_cos = spot_pg * spot_scale
    spot_back = spot_cos / (spot_pp + epsilon)
    gene = gene_ref[:, : 2 * sum(widths)]
    gene_scale = lax.rsqrt(gene[1:2, :] + epsilon) * lax.rsqrt(gene[2:3, :] + epsilon)
    gene_cos = gene[0:1, :] * gene_scale
    gene_back = gene_cos / (gene[1:2, :] + epsilon)
    folded = jnp.zeros((spot.shape[0], 128), f32)
    at = 0
    low = 0
    for q in range(n):
        wide = widths[q]
        pred = pred_refs[q][...]
        target = jnp.concatenate([own_ref[:, low : low + wide], other_ref[:, low : low + wide]], axis=1)
        cols = slice(at, at + 2 * wide)
        grad = -(target * gene_scale[:, cols] - gene_back[:, cols] * pred) / genes_total
        grad = grad - (target * spot_scale - spot_back * pred) / spots_total
        grad_low = grad.astype(bf16)
        turned_ref[at : at + 2 * wide, :] = grad_low.T
        prod = grad_low.astype(f32) * pred
        for k in range(0, 2 * wide, 128):
            folded = folded + prod[:, k : k + 128]
        at += 2 * wide
        low += wide
    inner_ref[...] = jnp.sum(folded.T, axis=0, keepdims=True)
    lane = lax.broadcasted_iota(jnp.int32, (1, 128), 1)
    gene_sum = jnp.sum(gene_cos, axis=1, keepdims=True)
    spot_sum = jnp.sum(spot_cos, axis=0, keepdims=True)
    sums_ref[...] = jnp.where(lane == 0, gene_sum, jnp.where(lane == 1, spot_sum, 0.0))


def grad_pred(core, widths, genes_total, spots_total, spot, gene, target, preds):
    spots = spot.shape[0]
    half = target.shape[1]
    genes = 2 * half
    return pl.pallas_call(
        functools.partial(grad_pred_kernel, widths, genes_total, spots_total),
        grid_spec=pltpu.PrefetchScalarGridSpec(
            num_scalar_prefetch=1,
            grid=(1,),
            in_specs=[VMEM] * 2
            + [
                pl.BlockSpec((spots, half), lambda i, core: (core[0], 0)),
                pl.BlockSpec((spots, half), lambda i, core: (2 + core[0], 0)),
            ]
            + [VMEM] * len(preds),
            out_specs=[VMEM] * 3,
        ),
        out_shape=[
            pltpu.VMEM((genes, spots), bf16),
            jax.ShapeDtypeStruct((1, spots), f32),
            jax.ShapeDtypeStruct((1, 128), f32),
        ],
        compiler_params=params(22),
        cost_estimate=cost(spots * genes * 14, spots * genes * 10),
        name="grad_pred",
    )(core, spot, gene, target, target, *preds)


def backward_kernel(widths, order_ref, logits_ref, enable_ref, retain_ref, col_ref, turned_ref, *refs):
    n = len(widths)
    panel_refs = refs[:n]
    grad_ref, row_ref = refs[n:]
    rows, spots = logits_ref.shape
    first = pl.multiple_of(pl.program_id(0) * rows, rows)
    enable = enable_ref[...].T
    retain = retain_ref[...].T
    shift, dens, inner = col_ref[0:1, :], col_ref[1:2, :], col_ref[2:3, :]
    part = rows // 2
    for h in range(2):
        here = pl.ds(first + h * part, part)
        panel = jnp.concatenate([ref[here, :] for ref in panel_refs], axis=1)
        grad_mapped = jnp.dot(panel, turned_ref[...], preferred_element_type=f32) + dens
        for k in range(part // 128):
            at = h * (part // 128) + k
            lines = slice(128 * at, 128 * (at + 1))
            block = jnp.where(enable[:, at : at + 1] > 0, logits_ref[lines, :], -1e30)
            mapping = jnp.exp(block - shift)
            grad = grad_mapped[128 * k : 128 * (k + 1), :]
            grad_ref[lines, :] = mapping * (retain[:, at : at + 1] * grad - inner)
            prod = grad * mapping
            folded = prod[:, 0:128]
            for c in range(128, spots, 128):
                folded = folded + prod[:, c : c + 128]
            row_ref[at : at + 1, :] = jnp.sum(folded.T, axis=0, keepdims=True)


def backward(order, logits, enable, retain, col, turned, panels):
    cells, spots = logits.shape
    genes = turned.shape[0]
    block = cells // PIECES
    widths = tuple(p.shape[1] for p in panels)
    cell = pl.BlockSpec((block // 128, 128), lambda i, order: (order[i], 0))
    return pl.pallas_call(
        functools.partial(backward_kernel, widths),
        grid_spec=pltpu.PrefetchScalarGridSpec(
            num_scalar_prefetch=1,
            grid=(PIECES,),
            in_specs=[
                pl.BlockSpec((block, spots), lambda i, order: (order[i], 0)),
                cell,
                cell,
                pl.BlockSpec((3, spots), lambda i, order: (0, 0)),
            ]
            + [VMEM] * (1 + len(panels)),
            out_specs=[pl.BlockSpec((block, spots), lambda i, order: (order[i], 0)), cell],
        ),
        out_shape=[
            jax.ShapeDtypeStruct((cells, spots), f32),
            jax.ShapeDtypeStruct((cells // 128, 128), f32),
        ],
        compiler_params=params(20),
        cost_estimate=cost(2 * cells * spots * genes, cells * 8 * spots, cells * spots),
        name="backward",
    )(order, logits, enable, retain, col, turned, *panels)


def join_kernel(*refs):
    at = 0
    for ref in refs[:-1]:
        refs[-1][at : at + ref.shape[0], :] = ref[...]
        at += ref.shape[0]


def join(*parts):
    rows = sum(p.shape[0] for p in parts)
    return pl.pallas_call(
        join_kernel,
        in_specs=[VMEM] * len(parts),
        out_specs=VMEM,
        out_shape=jax.ShapeDtypeStruct((rows, parts[0].shape[1]), bf16),
        compiler_params=params(12),
        cost_estimate=cost(0, 4 * rows * parts[0].shape[1]),
        name="join",
    )(*parts)


def select_kernel(inside_ref, middle_ref, end_ref, *out_refs):
    cut = out_refs[0].shape[1]
    for k, out in enumerate(out_refs):
        for flag, ref in ((1, middle_ref), (0, end_ref)):

            @pl.when(inside_ref[0] == flag)
            def _(out=out, ref=ref, k=k):
                out[...] = ref[:, k * cut : (k + 1) * cut]


def select(inside, middle, end, parts=1):
    rows, wide = middle.shape
    return pl.pallas_call(
        select_kernel,
        in_specs=[pl.BlockSpec(memory_space=pltpu.SMEM)] + [VMEM] * 2,
        out_specs=[VMEM] * parts,
        out_shape=[jax.ShapeDtypeStruct((rows, wide // parts), bf16)] * parts,
        compiler_params=params(12),
        cost_estimate=cost(0, 4 * rows * wide),
        name="select",
    )(inside, middle, end)


def lay_kernel(core_ref, theirs_ref, *refs):
    out_ref = refs[-1]
    mine = pl.program_id(0) == core_ref[0]

    @pl.when(mine)
    def _():
        at = 0
        for ref in refs[:-1]:
            out_ref[:, at : at + ref.shape[1]] = ref[...]
            at += ref.shape[1]

    @pl.when(jnp.logical_not(mine))
    def _():
        out_ref[...] = theirs_ref[...]


def lay(core, theirs, preds):
    spots, half = theirs.shape
    return pl.pallas_call(
        lay_kernel,
        grid_spec=pltpu.PrefetchScalarGridSpec(
            num_scalar_prefetch=1,
            grid=(2,),
            in_specs=[pl.BlockSpec((spots, half), lambda i, core: (0, 0))]
            + [pl.BlockSpec((spots, p.shape[1] // 2), lambda i, core: (0, core[0])) for p in preds],
            out_specs=pl.BlockSpec((spots, half), lambda i, core: (i, 0)),
        ),
        out_shape=jax.ShapeDtypeStruct((2 * spots, half), f32),
        compiler_params=params(20),
        cost_estimate=cost(0, spots * half * 16),
        name="lay",
    )(core, theirs, *preds)


def swap_cells(x):
    return lax.ppermute(x, "cells", [(0, 1), (1, 0)])


def swap_genes(x):
    return lax.ppermute(x, "genes", [(0, 1), (1, 0)])


def sum_spots_genes(x):
    if lax.axis_size("spots") != 8:
        return lax.psum(x, ("spots", "genes"))
    moved = [lax.ppermute(x, "spots", [(i, i ^ d) for i in range(8)]) for d in (2, 4, 6)]
    x = (x + moved[0]) + (moved[1] + moved[2])
    pairs = [lax.ppermute(x, ("spots", "genes"), [(i, i ^ d) for i in range(16)]) for d in (1, 2, 3)]
    return (x + pairs[0]) + (pairs[1] + pairs[2])


def both_genes(x):
    return lax.all_gather(x, "genes", axis=0, tiled=True)


class Step:
    def __init__(self, logits, filter_logits, expression, spot_expression, cell_mask):
        self.logits = pltpu.with_memory_space_constraint(logits, pltpu.HBM)
        self.expression = expression
        self.core = lax.axis_index("genes")
        self.enable = cell_mask.astype(f32).reshape(-1, 128)
        self.retain = jax.nn.sigmoid(filter_logits).reshape(-1, 128)
        self.spots = logits.shape[1]
        self.target = both_genes(spot_expression)
        self.core_flag = self.core.astype(jnp.int32).reshape(1)
        self.half = expression.shape[1]

    def local_stats(self):
        part = col_stats(self.logits, self.enable, self.retain)
        count = jnp.broadcast_to(jnp.sum(self.enable * self.retain), (1, self.spots))
        return jnp.concatenate([part, count], axis=0)

    def merge_stats(self, part, away):
        top = jnp.maximum(part[0], away[0])
        here, there = jnp.exp(part[0] - top), jnp.exp(away[0] - top)
        total = part[1] * here + away[1] * there
        self.density = (part[2] * here + away[2] * there) / total
        self.cell_count = part[3, 0] + away[3, 0]
        self.shift = (top + jnp.log(total))[None, :]

    def turned(self, order, shift, logits):
        return mapped_turned(order, logits, self.enable, self.retain, shift)

    def stats(self, parts, at, wide):
        return pred_stats(self.core_flag, parts, self.target, at // wide, wide)

    def gathered_whole(self):
        own = lax.all_gather(self.expression, "spots", axis=0, tiled=True)
        other = swap_genes(own)
        part = self.local_stats()
        self.merge_stats(part, swap_cells(part))
        order = jnp.arange(PIECES, dtype=jnp.int32)
        mapped = self.turned(order, self.shift, self.logits)
        wide = self.half // 4
        table = tuple((0, r) for r in range(PIECES))
        chunks = []
        for q in range(4):
            partial, panel = forward(self.core_flag, mapped, [(own, other)], table, [q], wide)
            chunks.append((wide, panel) + tuple(self.stats([lax.psum(partial, "cells")], q * wide, wide)))
        return order, chunks

    def gathered_line(self):
        near_pairs = [(2 * z + y, 2 * (z ^ 1) + y) for z in range(4) for y in range(2)]
        middle_pairs = [(2 * z + y, 2 * (3 - z) + y) for z in (1, 2) for y in range(2)]
        across_pairs = [(i, i ^ 1) for i in range(8)]

        def near(x):
            return lax.ppermute(x, "spots", near_pairs)

        def middle(x):
            return lax.ppermute(x, "spots", middle_pairs)

        def across(x):
            return lax.ppermute(x, "spots", across_pairs)

        spot = lax.axis_index("spots")
        z, y = spot // 2, spot % 2
        inside = (z == 1) | (z == 2)
        inside_flag = inside.astype(jnp.int32).reshape(1)
        column = jnp.stack([z, z ^ 1, jnp.where(z < 2, 2, 1), jnp.where(z < 2, 3, 0)])
        order = jnp.concatenate([2 * column + y, 2 * column + (1 - y)]).astype(jnp.int32)
        unit = self.half // 8
        expr = self.expression

        def cut(x, at, wide):
            return x[:, at * unit : (at + wide) * unit]

        def pick(middle, end, parts=1):
            return select(inside_flag, middle, end, parts)

        first = ((0, 0), (1, 0), (2, 0), (2, 1), (3, 0), (4, 0), (5, 0), (5, 1))
        second = ((0, 0), (1, 1), (2, 0), (2, 1), (3, 0), (4, 1), (5, 0), (5, 1))
        early = ((0, 0), (1, 0), (2, 0), (2, 2), (3, 0), (1, 1), (2, 1), (2, 3))
        core = self.core_flag
        s0, s1, sv, sf = cut(expr, 0, 2), cut(expr, 2, 2), cut(expr, 4, 3), cut(expr, 7, 1)
        expr_all = both_genes(expr)
        a0 = near(s0)
        bs01 = across(cut(expr, 0, 4))
        part = self.local_stats()
        a0, part, s0, s1 = hold(a0, part, s0, s1)
        a1 = near(s1)
        b0 = middle(join(s0, a0))
        away = swap_cells(part)
        a1, away, sv, logits, bs01, ev4 = hold(a1, away, sv, self.logits, bs01, cut(expr, 4, 4))
        bsv = across(ev4)
        av = near(sv)
        n01 = join(a0, a1)
        n01_all = both_genes(n01)
        self.merge_stats(part, away)
        mapped = self.turned(order, self.shift, logits)
        b0, a1, s1 = hold(b0, a1, s1)
        b1 = middle(join(s1, a1))
        av, b0, mapped = hold(av, b0, mapped)
        e0 = near(b0)
        av_all = both_genes(av)
        bsv, n01, sf, bs01 = hold(bsv, n01, sf, bs01)
        yn = across(n01)
        bs01_o = swap_genes(bs01)
        bsv_all = both_genes(bsv)
        sf = join(sf, cut(bsv, 3, 1))
        b1, sv, av = hold(b1, sv, av)
        bv = middle(join(sv, av))
        e0, b0, b1 = hold(e0, b0, b1)
        (mf0,) = pick(b0, e0)
        e1 = near(b1)
        mf0_o = swap_genes(mf0)
        yn, bs01_o, mf0 = hold(yn, bs01_o, mf0)
        ymf0 = across(mf0)
        yn_all = both_genes(yn)
        e1, mf0_o, sf, b1 = hold(e1, mf0_o, sf, b1)
        (mf1,) = pick(b1, e1)
        af = near(sf)
        mf1_o = swap_genes(mf1)
        ymf0, bv, mf1 = hold(ymf0, bv, mf1)
        ymf1 = across(mf1)
        ymf0_o = swap_genes(ymf0)
        af, bv, sf, mapped = hold(af, bv, sf, mapped)
        ev = near(bv)
        bf = middle(join(sf, af))
        af_all = both_genes(af)
        partial0, panel0 = forward(
            core,
            mapped,
            [expr_all, n01_all, (mf0, mf0_o), (bs01, bs01_o), yn_all, (ymf0, ymf0_o)],
            first,
            (0, 0, 0, 0, 0, 0),
            2 * unit,
        )
        away0 = swap_cells(partial0)
        ymf1, partial0, mf1_o, av, mapped = hold(ymf1, partial0, mf1_o, av, mapped)
        ynv = across(av)
        ymf1_o = swap_genes(ymf1)
        partial1, panel1 = forward(
            core,
            mapped,
            [expr_all, n01_all, (mf1, mf1_o), (bs01, bs01_o), yn_all, (ymf1, ymf1_o)],
            second,
            (1, 0, 0, 1, 0, 0),
            2 * unit,
        )
        away1 = swap_cells(partial1)
        ynv, ev, bv, partial1, bf = hold(ynv, ev, bv, partial1, bf)
        m2, m3, m4 = pick(bv, ev, 3)
        ym2 = across(m2)
        ef = near(bf)
        m2_o = swap_genes(m2)
        ynv_o = swap_genes(ynv)
        ym2, m2_o, ynv_o, away0, m3, mapped = hold(ym2, m2_o, ynv_o, away0, m3, mapped)
        ym3 = across(m3)
        ym2_o = swap_genes(ym2)
        m3_o = swap_genes(m3)
        partial2, panel2 = forward(
            core,
            mapped,
            [expr_all, av_all, (m2, m2_o), bsv_all, (ynv, ynv_o), (ym2, ym2_o)],
            first,
            (4, 0, 0, 0, 0, 0),
            unit,
        )
        away2 = swap_cells(partial2)
        ym3, ef, bf, partial2, m3_o, m4, mapped = hold(ym3, ef, bf, partial2, m3_o, m4, mapped)
        ym4 = across(m4)
        ym3_o = swap_genes(ym3)
        (mff,) = pick(bf, ef)
        mff_o = swap_genes(mff)
        m4_o = swap_genes(m4)
        partial3, panel3 = forward(
            core,
            mapped,
            [expr_all, av_all, (m3, m3_o), bsv_all, (ynv, ynv_o), (ym3, ym3_o)],
            first,
            (5, 1, 0, 1, 1, 0),
            unit,
        )
        away3 = swap_cells(partial3)
        ym4, partial3, away1, mff_o, mapped = hold(ym4, partial3, away1, mff_o, mapped)
        ym4_o = swap_genes(ym4)
        partialf, panelf = forward(
            core, mapped, [expr_all, af_all, (mff, mff_o), bsv_all], early, (7, 0, 0, 3), unit
        )
        awayf = swap_cells(partialf)
        ym4_o, partialf, m4_o, mapped = hold(ym4_o, partialf, m4_o, mapped)
        partial4, panel4 = forward(
            core,
            mapped,
            [expr_all, av_all, (m4, m4_o), bsv_all, (ynv, ynv_o), (ym4, ym4_o)],
            first,
            (6, 2, 0, 2, 2, 0),
            unit,
        )
        away4 = swap_cells(partial4)
        chunks = []
        rows = [
            ([partial0, away0], 0, 2, panel0),
            ([partial1, away1], 2, 2, panel1),
            ([partial2, away2], 4, 1, panel2),
            ([partial3, away3], 5, 1, panel3),
            ([partial4, away4], 6, 1, panel4),
            ([partialf, awayf], 7, 1, panelf),
        ]
        for parts, at, wide, panel in rows:
            chunks.append((wide * unit, panel) + tuple(self.stats(parts, at * unit, wide * unit)))
        return order, chunks


def body(logits, filter_logits, expression, spot_expression, cell_mask, spot_counts):
    cells_total = logits.shape[0] * lax.axis_size("cells")
    spots = logits.shape[1]
    spots_total = spots * lax.axis_size("spots") * lax.axis_size("genes")
    genes_total = expression.shape[1] * lax.axis_size("genes")
    step = Step(logits, filter_logits, expression, spot_expression, cell_mask)
    order, chunks = step.gathered_line() if lax.axis_size("spots") == 8 else step.gathered_whole()
    widths, panels, preds, gene_stats, spot_stats = zip(*chunks)
    density = step.density

    counts = spot_counts.astype(f32)
    kl_parts = jnp.stack([jnp.sum(density), jnp.sum(counts * (jnp.log(counts) - jnp.log(density))), jnp.sum(counts)])

    kl_block = jnp.broadcast_to(kl_parts[:, None], (3, 128))
    gene = sum_spots_genes(jnp.concatenate(gene_stats + (kl_block,), axis=1))
    dens_total, kl_part, count_total = gene[0, -1], gene[1, -1], gene[2, -1]
    kl_term = kl_part / count_total - jnp.log(count_total) + jnp.log(dens_total)
    offset = (step.cell_count - 0.5 * cells_total) / cells_total
    penalty = jnp.sqrt(offset * offset + 0.01)
    dens_grad = -counts / (count_total * density) + 1.0 / dens_total
    spot = functools.reduce(jnp.add, spot_stats)

    turned, inner, sums = grad_pred(
        step.core_flag, widths, genes_total, spots_total, spot, gene, step.target, preds
    )
    theirs = swap_genes(
        jnp.concatenate([jnp.where(step.core == 0, p[:, w:], p[:, :w]) for p, w in zip(preds, widths)], axis=1)
    )
    col = jnp.concatenate([step.shift, dens_grad[None], inner + (density * dens_grad)[None]], axis=0)
    grad_logits, row = backward(order, step.logits, step.enable, step.retain, col, turned, panels)

    row_sums = sum_spots_genes(jnp.concatenate([row, sums], axis=0))
    copies = lax.axis_size("spots") * lax.axis_size("genes")
    gene_sum, spot_sum = row_sums[-1, 0] / copies, row_sums[-1, 1]
    total_loss = -gene_sum / genes_total - spot_sum / spots_total + kl_term + penalty
    retain_grad = row_sums[:-1] + step.enable * offset / (penalty * cells_total)
    filter_grad = (retain_grad * step.retain * (1.0 - step.retain)).reshape(-1)

    predicted = lay(step.core_flag, theirs, preds)
    return (predicted, total_loss, grad_logits, filter_grad)


def solution(mesh):
    placed = (
        P("cells", ("spots", "genes")),
        P("cells"),
        P(("cells", "spots"), "genes"),
        P("spots", "genes"),
        P("cells"),
        P(("spots", "genes")),
    )
    return jax.shard_map(
        body,
        mesh=mesh,
        in_specs=placed,
        out_specs=(P("spots", "genes"), P(), P("cells", ("spots", "genes")), P("cells")),
        check_vma=False,
    )
```

```python
import functools

import jax
import jax.numpy as jnp
from jax import lax
from jax.experimental import pallas as pl
from jax.experimental.pallas import tpu as pltpu
from jax.sharding import PartitionSpec as P

epsilon = 1e-06
bf16 = jnp.bfloat16
f32 = jnp.float32
PIECES = 8
MIB = 1024 * 1024
VMEM = pl.BlockSpec(memory_space=pltpu.VMEM)


def params(limit):
    return pltpu.CompilerParams(vmem_limit_bytes=limit * MIB)


def cost(flops=0, bytes_accessed=0, transcendentals=0):
    return pl.CostEstimate(flops=1, bytes_accessed=1, transcendentals=0)


def in_hbm(x):
    return pltpu.with_memory_space_constraint(x, pltpu.HBM)


def hold(*values):
    return lax.optimization_barrier(values)


def col_stats_kernel(logits_ref, enable_ref, retain_ref, out_ref, top, total, dens):
    step = pl.program_id(0)

    @pl.when(step == 0)
    def _():
        top[...] = jnp.full_like(top, -1e29)
        total[...] = jnp.zeros_like(total)
        dens[...] = jnp.zeros_like(dens)

    rows, spots = logits_ref.shape
    enable = enable_ref[...].T
    retain = retain_ref[...].T
    blocks = []
    new = top[...]
    for k in range(rows // 128):
        block = jnp.where(enable[:, k : k + 1] > 0, logits_ref[128 * k : 128 * (k + 1), :], -1e30)
        blocks.append(block.reshape(16, 8, spots))
        new = jnp.maximum(new, jnp.max(blocks[-1], axis=0))
    shrink = jnp.exp(top[...] - new)
    top[...] = new
    sums = total[...] * shrink
    kept = dens[...] * shrink
    for k in range(rows // 128):
        part = jnp.exp(blocks[k] - new[None])
        share = jnp.broadcast_to(retain[:, k : k + 1], (128, spots)).reshape(16, 8, spots)
        sums = sums + jnp.sum(part, axis=0)
        kept = kept + jnp.sum(part * share, axis=0)
    total[...] = sums
    dens[...] = kept

    @pl.when(step == pl.num_programs(0) - 1)
    def _():
        best = jnp.max(new, axis=0, keepdims=True)
        scale = jnp.exp(new - best)
        out_ref[0:1, :] = best
        out_ref[1:2, :] = jnp.sum(sums * scale, axis=0, keepdims=True)
        out_ref[2:3, :] = jnp.sum(kept * scale, axis=0, keepdims=True)


def col_stats(logits, enable, retain, block=1024):
    cells, spots = logits.shape
    cell = pl.BlockSpec((block // 128, 128), lambda i: (i, 0))
    return pl.pallas_call(
        col_stats_kernel,
        grid=(cells // block,),
        in_specs=[pl.BlockSpec((block, spots), lambda i: (i, 0)), cell, cell],
        out_specs=pl.BlockSpec((3, spots), lambda i: (0, 0)),
        out_shape=jax.ShapeDtypeStruct((3, spots), f32),
        scratch_shapes=[pltpu.VMEM((8, spots), f32)] * 3,
        compiler_params=params(20),
        cost_estimate=cost(cells * spots * 8, cells * spots * 4, cells * spots),
        name="col_stats",
    )(logits, enable, retain)


def mapped_kernel(order_ref, logits_ref, enable_ref, retain_ref, shift_ref, out_ref):
    rows, spots = logits_ref.shape
    enable = enable_ref[...].T
    retain = retain_ref[...].T
    shift = shift_ref[...]
    for k in range(rows // 128):
        block = jnp.where(enable[:, k : k + 1] > 0, logits_ref[128 * k : 128 * (k + 1), :], -1e30)
        mapped = retain[:, k : k + 1] * jnp.exp(block - shift)
        out_ref[:, 128 * k : 128 * (k + 1)] = mapped.astype(bf16).T


def mapped_turned(order, logits, enable, retain, shift):
    cells, spots = logits.shape
    block = cells // PIECES
    cell = pl.BlockSpec((block // 128, 128), lambda i, order: (order[i], 0))
    return pl.pallas_call(
        mapped_kernel,
        grid_spec=pltpu.PrefetchScalarGridSpec(
            num_scalar_prefetch=1,
            grid=(PIECES,),
            in_specs=[
                pl.BlockSpec((block, spots), lambda i, order: (order[i], 0)),
                cell,
                cell,
                pl.BlockSpec((1, spots), lambda i, order: (0, 0)),
            ],
            out_specs=pl.BlockSpec((spots, block), lambda i, order: (0, i)),
        ),
        out_shape=pltpu.HBM((spots, cells), bf16),
        compiler_params=params(20),
        cost_estimate=cost(cells * spots * 6, cells * spots * 6, cells * spots),
        name="mapped_turned",
    )(order, logits, enable, retain, shift)


def forward_kernel(pieces, table, columns, rows, wide, more, core_ref, mapped_ref, *refs):
    n = len(columns)
    sources = (refs[:n], refs[n : 2 * n])
    refs = refs[2 * n :]
    base = refs[0][...] if more else None
    pred_ref, panel_ref, held, turned, own_sems, other_sems, mapped_sems, panel_sems = refs[2 if more else 0 :]

    def piece(r, which, column):
        source, block = table[r]
        part = sources[which][source].at[pl.ds(block * rows, rows), pl.ds(columns[source] * wide, wide)]
        target = held.at[pl.ds(r * rows, rows), pl.ds(column, wide)]
        return pltpu.make_async_copy(part, target, (own_sems, other_sems)[which].at[r])

    def load(r):
        cols = pl.ds(r * rows, rows)
        return pltpu.make_async_copy(mapped_ref.at[:, cols], turned.at[:, cols], mapped_sems.at[r])

    def save(r):
        here = pl.ds(r * rows, rows)
        return pltpu.make_async_copy(held.at[here, :], panel_ref.at[here, :], panel_sems.at[r])

    for r in pieces:
        for core in range(2):

            @pl.when(core_ref[0] == core)
            def _(core=core, r=r):
                piece(r, 0, core * wide).start()
                piece(r, 1, (1 - core) * wide).start()

        load(r).start()
    total = base
    for r in pieces:
        piece(r, 0, 0).wait()
        piece(r, 1, 0).wait()
        save(r).start()
        load(r).wait()
        here = slice(r * rows, (r + 1) * rows)
        part = jnp.dot(turned[:, here], held[here, :], preferred_element_type=f32)
        total = part if total is None else total + part
    pred_ref[...] = total
    for r in pieces:
        save(r).wait()


def forward(core, mapped, sources, table, columns, wide, pieces=tuple(range(PIECES)), begun=None):
    spots, cells = mapped.shape
    rows = cells // PIECES
    own, other = zip(*sources)
    hbm = pl.BlockSpec(memory_space=pltpu.HBM)
    n = 2 + 2 * len(own)
    return pl.pallas_call(
        functools.partial(forward_kernel, pieces, table, columns, rows, wide, begun is not None),
        in_specs=[pl.BlockSpec(memory_space=pltpu.SMEM), hbm] + [hbm] * (n - 2) + ([VMEM, hbm] if begun else []),
        out_specs=[VMEM, hbm],
        out_shape=[
            jax.ShapeDtypeStruct((spots, 2 * wide), f32),
            pltpu.HBM((cells, 2 * wide), bf16),
        ],
        scratch_shapes=[pltpu.VMEM((cells, 2 * wide), bf16), pltpu.VMEM((spots, cells), bf16)]
        + [pltpu.SemaphoreType.DMA((PIECES,))] * 4,
        input_output_aliases={n + 1: 1} if begun else {},
        compiler_params=params(14 + 16 * wide // 512),
        cost_estimate=cost(4 * spots * cells * wide, 2 * cells * (spots + 4 * wide)),
        name="forward",
    )(core, in_hbm(mapped), *[in_hbm(x) for x in own + other], *(begun or ()))


def in_order(core, own, other):
    first = core == 0
    return jnp.concatenate([jnp.where(first, own, other), jnp.where(first, other, own)], axis=1)


def stats_kernel(parts, core_ref, *refs):
    own_ref, other_ref, pred_ref, gene_ref, spot_ref, sent_ref = refs[parts:]
    wide = own_ref.shape[1]
    pred = functools.reduce(jnp.add, [ref[...] for ref in refs[:parts]])
    pred_ref[...] = pred
    sent_ref[...] = jnp.where(core_ref[0] == 0, pred[:, wide:], pred[:, :wide])
    target = in_order(core_ref[0], own_ref[...], other_ref[...])
    terms = (pred * target, pred * pred, target * target)
    lane = lax.broadcasted_iota(jnp.int32, spot_ref.shape, 1)
    spot = jnp.zeros(spot_ref.shape, f32)
    for k, term in enumerate(terms):
        gene_ref[k : k + 1, :] = jnp.sum(term, axis=0, keepdims=True)
        spot = jnp.where(lane == k, jnp.sum(term, axis=1, keepdims=True), spot)
    spot_ref[...] = spot


def pred_stats(core, parts, target, other, column, other_column, wide):
    spots = parts[0].shape[0]
    whole = pl.BlockSpec((spots, 2 * wide), lambda i, core: (0, 0))
    return pl.pallas_call(
        functools.partial(stats_kernel, len(parts)),
        grid_spec=pltpu.PrefetchScalarGridSpec(
            num_scalar_prefetch=1,
            grid=(1,),
            in_specs=[whole] * len(parts)
            + [
                pl.BlockSpec((spots, wide), lambda i, core: (core[0], column)),
                pl.BlockSpec((spots, wide), lambda i, core: (0, other_column)),
            ],
            out_specs=[
                whole,
                pl.BlockSpec((3, 2 * wide), lambda i, core: (0, 0)),
                pl.BlockSpec((spots, 4), lambda i, core: (0, 0)),
                pl.BlockSpec((spots, wide), lambda i, core: (0, 0)),
            ],
        ),
        out_shape=[
            jax.ShapeDtypeStruct((spots, 2 * wide), f32),
            jax.ShapeDtypeStruct((3, 2 * wide), f32),
            jax.ShapeDtypeStruct((spots, 4), f32),
            jax.ShapeDtypeStruct((spots, wide), f32),
        ],
        compiler_params=params(16),
        cost_estimate=cost(spots * wide * 20, spots * wide * 40),
        name="pred_stats",
    )(core, *parts, target, other)


def grad_pred_kernel(widths, genes_total, spots_total, core_ref, spot_ref, gene_ref, own_ref, *refs):
    n = len(widths)
    other_refs, pred_refs = refs[:3], refs[3 : 3 + n]
    refs = refs[3:]
    quarter = other_refs[0].shape[1]
    turned_ref, inner_ref, sums_ref = refs[n:]
    spot = spot_ref[...]
    spot_pg, spot_pp, spot_gg = spot[:, 0:1], spot[:, 1:2], spot[:, 2:3]
    spot_scale = lax.rsqrt(spot_pp + epsilon) * lax.rsqrt(spot_gg + epsilon)
    spot_cos = spot_pg * spot_scale
    spot_back = spot_cos / (spot_pp + epsilon)
    gene = gene_ref[:, : 2 * sum(widths)]
    gene_scale = lax.rsqrt(gene[1:2, :] + epsilon) * lax.rsqrt(gene[2:3, :] + epsilon)
    gene_cos = gene[0:1, :] * gene_scale
    gene_back = gene_cos / (gene[1:2, :] + epsilon)
    folded = jnp.zeros((spot.shape[0], 128), f32)
    at = 0
    low = 0
    for q in range(n):
        wide = widths[q]
        pred = pred_refs[q][...]
        other = other_refs[min(low // quarter, 2)]
        other_low = low - min(low // quarter, 2) * quarter
        target = in_order(core_ref[0], own_ref[:, low : low + wide], other[:, other_low : other_low + wide])
        cols = slice(at, at + 2 * wide)
        grad = -(target * gene_scale[:, cols] - gene_back[:, cols] * pred) / genes_total
        grad = grad - (target * spot_scale - spot_back * pred) / spots_total
        grad_low = grad.astype(bf16)
        turned_ref[at : at + 2 * wide, :] = grad_low.T
        prod = grad_low.astype(f32) * pred
        for k in range(0, 2 * wide, 128):
            folded = folded + prod[:, k : k + 128]
        at += 2 * wide
        low += wide
    inner_ref[...] = jnp.sum(folded.T, axis=0, keepdims=True)
    lane = lax.broadcasted_iota(jnp.int32, (1, 128), 1)
    gene_sum = jnp.sum(gene_cos, axis=1, keepdims=True)
    spot_sum = jnp.sum(spot_cos, axis=0, keepdims=True)
    sums_ref[...] = jnp.where(lane == 0, gene_sum, jnp.where(lane == 1, spot_sum, 0.0))


def grad_pred(core, widths, genes_total, spots_total, spot, gene, target, others, preds):
    half = target.shape[1]
    spots = spot.shape[0]
    genes = 2 * half
    return pl.pallas_call(
        functools.partial(grad_pred_kernel, widths, genes_total, spots_total),
        grid_spec=pltpu.PrefetchScalarGridSpec(
            num_scalar_prefetch=1,
            grid=(1,),
            in_specs=[VMEM] * 2
            + [pl.BlockSpec((spots, half), lambda i, core: (core[0], 0))]
            + [VMEM] * (3 + len(preds)),
            out_specs=[VMEM] * 3,
        ),
        out_shape=[
            pltpu.VMEM((genes, spots), bf16),
            jax.ShapeDtypeStruct((1, spots), f32),
            jax.ShapeDtypeStruct((1, 128), f32),
        ],
        compiler_params=params(20),
        cost_estimate=cost(spots * genes * 14, spots * genes * 10),
        name="grad_pred",
    )(core, spot, gene, target, *others, *preds)


def backward_kernel(widths, order_ref, logits_ref, enable_ref, retain_ref, col_ref, turned_ref, *refs):
    n = len(widths)
    panel_refs = refs[:n]
    grad_ref, row_ref = refs[n:]
    rows, spots = logits_ref.shape
    first = pl.multiple_of(pl.program_id(0) * rows, rows)
    enable = enable_ref[...].T
    retain = retain_ref[...].T
    shift, dens, inner = col_ref[0:1, :], col_ref[1:2, :], col_ref[2:3, :]
    part = rows // 2
    for h in range(2):
        here = pl.ds(first + h * part, part)
        near = slice(h * part, (h + 1) * part)
        panel = jnp.concatenate([ref[near if ref.shape[0] == rows else here, :] for ref in panel_refs], axis=1)
        grad_mapped = jnp.dot(panel, turned_ref[...], preferred_element_type=f32) + dens
        for k in range(part // 128):
            at = h * (part // 128) + k
            lines = slice(128 * at, 128 * (at + 1))
            block = jnp.where(enable[:, at : at + 1] > 0, logits_ref[lines, :], -1e30)
            mapping = jnp.exp(block - shift)
            grad = grad_mapped[128 * k : 128 * (k + 1), :]
            grad_ref[lines, :] = mapping * (retain[:, at : at + 1] * grad - inner)
            prod = grad * mapping
            folded = prod[:, 0:128]
            for c in range(128, spots, 128):
                folded = folded + prod[:, c : c + 128]
            row_ref[at : at + 1, :] = jnp.sum(folded.T, axis=0, keepdims=True)


def backward(order, logits, enable, retain, col, turned, panels):
    cells, spots = logits.shape
    genes = turned.shape[0]
    block = cells // PIECES
    widths = tuple(p.shape[1] for p in panels)
    streamed = (0,) + tuple(range(len(panels) - 2, len(panels)))
    cell = pl.BlockSpec((block // 128, 128), lambda i, order: (order[i], 0))
    return pl.pallas_call(
        functools.partial(backward_kernel, widths),
        grid_spec=pltpu.PrefetchScalarGridSpec(
            num_scalar_prefetch=1,
            grid=(PIECES,),
            in_specs=[
                pl.BlockSpec((block, spots), lambda i, order: (order[i], 0)),
                cell,
                cell,
                pl.BlockSpec((3, spots), lambda i, order: (0, 0)),
            ]
            + [VMEM]
            + [pl.BlockSpec((block, w), lambda i, order: (i, 0)) if q in streamed else VMEM for q, w in enumerate(widths)],
            out_specs=[pl.BlockSpec((block, spots), lambda i, order: (order[i], 0)), cell],
        ),
        out_shape=[
            jax.ShapeDtypeStruct((cells, spots), f32),
            jax.ShapeDtypeStruct((cells // 128, 128), f32),
        ],
        compiler_params=params(26),
        cost_estimate=cost(2 * cells * spots * genes, cells * 8 * spots, cells * spots),
        name="backward",
    )(order, logits, enable, retain, col, turned, *[in_hbm(p) if q in streamed else p for q, p in enumerate(panels)])


def join_kernel(*refs):
    at = 0
    for ref in refs[:-1]:
        refs[-1][at : at + ref.shape[0], :] = ref[...]
        at += ref.shape[0]


def join(*parts):
    rows = sum(p.shape[0] for p in parts)
    return pl.pallas_call(
        join_kernel,
        in_specs=[VMEM] * len(parts),
        out_specs=VMEM,
        out_shape=jax.ShapeDtypeStruct((rows, parts[0].shape[1]), bf16),
        compiler_params=params(12),
        cost_estimate=cost(0, 4 * rows * parts[0].shape[1]),
        name="join",
    )(*parts)


def select_kernel(inside_ref, b_ref, e_ref, c_ref, f_ref, *out_refs):
    rows = b_ref.shape[0]
    cut = out_refs[0].shape[1]
    for k, out in enumerate(out_refs):
        cols = slice(k * cut, (k + 1) * cut)
        for flag, refs in ((1, (b_ref, c_ref)), (0, (e_ref, f_ref))):

            @pl.when(inside_ref[0] == flag)
            def _(out=out, refs=refs, cols=cols):
                out[0:rows, :] = refs[0][:, cols]
                out[rows : 2 * rows, :] = refs[1][:, cols]


def select(inside, b, e, c, f, parts=1):
    rows, wide = b.shape
    return pl.pallas_call(
        select_kernel,
        in_specs=[pl.BlockSpec(memory_space=pltpu.SMEM)] + [VMEM] * 4,
        out_specs=[VMEM] * parts,
        out_shape=[jax.ShapeDtypeStruct((2 * rows, wide // parts), bf16)] * parts,
        compiler_params=params(12),
        cost_estimate=cost(0, 8 * rows * wide),
        name="select",
    )(inside, b, e, c, f)


def lay_kernel(core_ref, *refs):
    out_ref = refs[-1]
    n = (len(refs) - 1) // 2
    for mine, parts in ((True, refs[:n]), (False, refs[n : 2 * n])):

        @pl.when((pl.program_id(0) == core_ref[0]) == mine)
        def _(parts=parts):
            at = 0
            for ref in parts:
                out_ref[:, at : at + ref.shape[1]] = ref[...]
                at += ref.shape[1]


def lay(core, preds, theirs, half, column, begun=None):
    spots = preds[0].shape[0]
    wide = sum(p.shape[1] for p in theirs)
    return pl.pallas_call(
        lay_kernel,
        grid_spec=pltpu.PrefetchScalarGridSpec(
            num_scalar_prefetch=1,
            grid=(2,),
            in_specs=[pl.BlockSpec((spots, p.shape[1]), lambda i, core: (0, core[0])) for p in theirs]
            + [pl.BlockSpec((spots, p.shape[1]), lambda i, core: (0, 0)) for p in theirs]
            + ([] if begun is None else [pl.BlockSpec(memory_space=pl.ANY)]),
            out_specs=pl.BlockSpec((spots, wide), lambda i, core: (i, column)),
        ),
        out_shape=jax.ShapeDtypeStruct((2 * spots, half), f32),
        input_output_aliases={} if begun is None else {1 + 2 * len(preds): 0},
        compiler_params=params(24),
        cost_estimate=cost(0, spots * half * 16),
        name="lay",
    )(core, *[in_hbm(x) for x in (*preds, *theirs)], *(() if begun is None else (begun,)))


def swap_cells(x):
    return lax.ppermute(x, "cells", [(0, 1), (1, 0)])


def swap_genes(x):
    return lax.ppermute(x, "genes", [(0, 1), (1, 0)])


def sum_spots_genes(x, meanwhile=()):
    if lax.axis_size("spots") != 8:
        return lax.psum(x, ("spots", "genes")), meanwhile
    moved = [lax.ppermute(x, "spots", [(i, i ^ d) for i in range(8)]) for d in (2, 4, 6)]
    moved[0], moved[1], moved[2], *meanwhile = hold(*moved, *meanwhile)
    x = (x + moved[0]) + (moved[1] + moved[2])
    pairs = [lax.ppermute(x, ("spots", "genes"), [(i, i ^ d) for i in range(16)]) for d in (1, 2, 3)]
    return (x + pairs[0]) + (pairs[1] + pairs[2]), meanwhile


class Step:
    def __init__(self, logits, filter_logits, expression, spot_expression, cell_mask):
        self.logits = pltpu.with_memory_space_constraint(logits, pltpu.HBM)
        self.expression = expression
        self.core = lax.axis_index("genes")
        self.enable = cell_mask.astype(f32).reshape(-1, 128)
        self.retain = jax.nn.sigmoid(filter_logits).reshape(-1, 128)
        self.spots = logits.shape[1]
        self.core_flag = self.core.astype(jnp.int32).reshape(1)
        self.half = expression.shape[1]
        self.target = spot_expression
        sent = lax.dynamic_slice_in_dim(spot_expression, (1 - self.core) * self.spots, self.spots, 0)
        quarter = self.half // 4
        self.target_sent = [sent[:, :quarter], sent[:, quarter : 2 * quarter], sent[:, 2 * quarter :]]

    def local_stats(self):
        part = col_stats(self.logits, self.enable, self.retain)
        count = jnp.broadcast_to(jnp.sum(self.enable * self.retain), (1, self.spots))
        return jnp.concatenate([part, count], axis=0)

    def merge_stats(self, part, away):
        top = jnp.maximum(part[0], away[0])
        here, there = jnp.exp(part[0] - top), jnp.exp(away[0] - top)
        total = part[1] * here + away[1] * there
        self.density = (part[2] * here + away[2] * there) / total
        self.cell_count = part[3, 0] + away[3, 0]
        self.shift = (top + jnp.log(total))[None, :]

    def turned(self, order, shift, logits):
        return mapped_turned(order, logits, self.enable, self.retain, shift)

    def stats(self, parts, other, at, wide):
        begin = self.half - other.shape[1] if other.shape[1] > self.half // 4 else at // (self.half // 4) * (self.half // 4)
        return pred_stats(self.core_flag, parts, self.target, other, at // wide, (at - begin) // wide, wide)

    def gathered_whole(self):
        own = lax.all_gather(self.expression, "spots", axis=0, tiled=True)
        other = swap_genes(own)
        part = self.local_stats()
        self.target_other = [swap_genes(x) for x in self.target_sent]
        self.merge_stats(part, swap_cells(part))
        order = jnp.arange(PIECES, dtype=jnp.int32)
        mapped = self.turned(order, self.shift, self.logits)
        wide = self.half // 4
        table = tuple((0, r) for r in range(PIECES))
        chunks = []
        for q in range(4):
            partial, panel = forward(self.core_flag, mapped, [(own, other)], table, [q], wide)
            chunks.append((wide, panel) + tuple(self.stats([lax.psum(partial, "cells")], self.target_other[min(q, 2)], q * wide, wide)))
        return order, chunks

    def gathered_line(self):
        near_pairs = [(2 * z + y, 2 * (z ^ 1) + y) for z in range(4) for y in range(2)]
        middle_pairs = [(2 * z + y, 2 * (3 - z) + y) for z in (1, 2) for y in range(2)]
        across_pairs = [(i, i ^ 1) for i in range(8)]

        def near(x):
            return lax.ppermute(x, "spots", near_pairs)

        def middle(x):
            return lax.ppermute(x, "spots", middle_pairs)

        def across(x):
            return lax.ppermute(x, "spots", across_pairs)

        spot = lax.axis_index("spots")
        z, y = spot // 2, spot % 2
        inside = (z == 1) | (z == 2)
        inside_flag = inside.astype(jnp.int32).reshape(1)
        column = jnp.stack([z, z ^ 1, jnp.where(z < 2, 2, 1), jnp.where(z < 2, 3, 0)])
        order = jnp.concatenate([2 * column + y, 2 * column + (1 - y)]).astype(jnp.int32)
        unit = self.half // 8
        expr = self.expression

        def cut(x, at, wide):
            return x[:, at * unit : (at + wide) * unit]

        def pick(b, e, c, f, parts=1):
            return select(inside_flag, b, e, c, f, parts)

        first = ((0, 0), (1, 0), (2, 0), (2, 1), (3, 0), (4, 0), (5, 0), (5, 1))
        early = ((0, 0), (1, 0), (2, 0), (2, 2), (3, 0), (1, 1), (2, 1), (2, 3))
        core = self.core_flag

        def run(sources, table, columns, wide):
            return forward(core, mapped, sources, table, columns, wide * unit)

        s01 = cut(expr, 0, 4)
        beside = across(expr)
        a01 = near(s01)
        b01 = middle(s01)
        expr_o = swap_genes(expr)
        target_0 = swap_genes(self.target_sent[0])
        part = self.local_stats()
        a01, b01, part, target_0, sv, target_1 = hold(
            a01, b01, part, target_0, cut(expr, 4, 3), self.target_sent[1]
        )
        c01 = middle(a01)
        e01 = near(b01)
        away = swap_cells(part)
        target_1 = swap_genes(target_1)
        self.merge_stats(part, away)
        mapped = self.turned(order, self.shift, self.logits)
        beside, e01, c01, expr_o, mapped, a01, sv, target_1 = hold(
            beside, e01, c01, expr_o, mapped, a01, sv, target_1
        )
        yn = across(a01)
        f01 = near(c01)
        beside_o = swap_genes(beside)
        a01_o = swap_genes(a01)
        bv = middle(sv)
        yn, f01, a01_o, sv, beside = hold(yn, f01, a01_o, sv, beside)
        mf0, mf1 = pick(b01, e01, c01, f01, 2)
        ymf0 = across(mf0)
        av = near(sv)
        mf0_o, yn_o = swap_genes(mf0), swap_genes(yn)
        sf = join(cut(expr, 7, 1), cut(beside, 7, 1))
        ymf0, av, mf0_o, yn_o, beside_o, mf1, bv, mapped = hold(ymf0, av, mf0_o, yn_o, beside_o, mf1, bv, mapped)
        ymf1 = across(mf1)
        ev = near(bv)
        cv = middle(av)
        ymf0_o, mf1_o = swap_genes(ymf0), swap_genes(mf1)
        expr_2, a01_2, beside_2, yn_2 = (expr, expr_o), (a01, a01_o), (beside, beside_o), (yn, yn_o)
        partial0, panel0 = run(
            [expr_2, a01_2, (mf0, mf0_o), beside_2, yn_2, (ymf0, ymf0_o)], first, (0, 0, 0, 0, 0, 0), 2
        )
        ymf1, ev, cv, partial0, mf1_o, av, mapped = hold(ymf1, ev, cv, partial0, mf1_o, av, mapped)
        ynv = across(av)
        fv = near(cv)
        ymf1_o = swap_genes(ymf1)
        away0 = swap_cells(partial0)
        av_o = swap_genes(av)
        partial1, panel1 = run(
            [expr_2, a01_2, (mf1, mf1_o), beside_2, yn_2, (ymf1, ymf1_o)], first, (1, 1, 0, 1, 1, 0), 2
        )
        ynv, fv, partial1, av_o, sf = hold(ynv, fv, partial1, av_o, sf)
        m2, m3, m4 = pick(bv, ev, cv, fv, 3)
        ym2 = across(m2)
        af = near(sf)
        away1 = swap_cells(partial1)
        ynv_o = swap_genes(ynv)
        ym2, af, ynv_o, away0, m2, m3, sf, mapped = hold(ym2, af, ynv_o, away0, m2, m3, sf, mapped)
        ym3 = across(m3)
        bf = middle(sf)
        ym2_o, m2_o = swap_genes(ym2), swap_genes(m2)
        av_2, ynv_2 = (av, av_o), (ynv, ynv_o)
        partial2, panel2 = run([expr_2, av_2, (m2, m2_o), beside_2, ynv_2, (ym2, ym2_o)], first, (4, 0, 0, 4, 0, 0), 1)
        stats0 = self.stats([partial0, away0], target_0, 0, 2 * unit)
        ym3, bf, partial2, away1, m3, m4, af, mapped, *stats0 = hold(
            ym3, bf, partial2, away1, m3, m4, af, mapped, *stats0
        )
        ym4 = across(m4)
        ef, cf = near(bf), middle(af)
        ym3_o, m3_o = swap_genes(ym3), swap_genes(m3)
        partial3, panel3 = run([expr_2, av_2, (m3, m3_o), beside_2, ynv_2, (ym3, ym3_o)], first, (5, 1, 0, 5, 1, 0), 1)
        stats1 = self.stats([partial1, away1], target_1, 2 * unit, 2 * unit)
        ym4, ef, cf, partial3, partial2, m4, mapped, *stats1 = hold(
            ym4, ef, cf, partial3, partial2, m4, mapped, *stats1
        )
        ff = near(cf)
        ym4_o, m4_o = swap_genes(ym4), swap_genes(m4)
        away2 = swap_cells(partial2)
        away3 = swap_cells(partial3)
        partial4, panel4 = run([expr_2, av_2, (m4, m4_o), beside_2, ynv_2, (ym4, ym4_o)], first, (6, 2, 0, 6, 2, 0), 1)
        ff, partial4, away2, af, mapped, target_2 = hold(ff, partial4, away2, af, mapped, self.target_sent[2])
        away4 = swap_cells(partial4)
        (mff,) = pick(bf, ef, cf, ff)
        mff_o, af_o = swap_genes(mff), swap_genes(af)
        target_2 = swap_genes(target_2)
        self.target_other = (target_0, target_1, target_2)
        partialf, panelf = run([expr_2, (af, af_o), (mff, mff_o), beside_2], early, (7, 0, 0, 7), 1)
        stats2 = self.stats([partial2, away2], target_2, 4 * unit, unit)
        partialf, away3, *stats2 = hold(partialf, away3, *stats2)
        stats3 = self.stats([partial3, away3], target_2, 5 * unit, unit)
        awayf = swap_cells(partialf)
        stats4 = self.stats([partial4, away4], target_2, 6 * unit, unit)
        statsf = self.stats([partialf, awayf], target_2, 7 * unit, unit)
        return order, [
            (2 * unit, panel0, *stats0),
            (2 * unit, panel1, *stats1),
            (unit, panel2, *stats2),
            (unit, panel3, *stats3),
            (unit, panel4, *stats4),
            (unit, panelf, *statsf),
        ]


def body(logits, filter_logits, expression, spot_expression, cell_mask, spot_counts):
    cells_total = logits.shape[0] * lax.axis_size("cells")
    spots = logits.shape[1]
    spots_total = spots * lax.axis_size("spots") * lax.axis_size("genes")
    genes_total = expression.shape[1] * lax.axis_size("genes")
    step = Step(logits, filter_logits, expression, spot_expression, cell_mask)
    order, chunks = step.gathered_line() if lax.axis_size("spots") == 8 else step.gathered_whole()
    widths, panels, preds, gene_stats, spot_stats, sent = zip(*chunks)
    density = step.density

    counts = spot_counts.astype(f32)
    kl_parts = jnp.stack([jnp.sum(density), jnp.sum(counts * (jnp.log(counts) - jnp.log(density))), jnp.sum(counts)])

    kl_block = jnp.broadcast_to(kl_parts[:, None], (3, 128))
    theirs = [swap_genes(x) for x in sent]
    half = expression.shape[1]
    split = len(widths) - 2
    predicted = lay(step.core_flag, preds[:split], theirs[:split], half, 0)
    gene, (predicted,) = sum_spots_genes(jnp.concatenate(gene_stats + (kl_block,), axis=1), (predicted,))
    dens_total, kl_part, count_total = gene[0, -1], gene[1, -1], gene[2, -1]
    kl_term = kl_part / count_total - jnp.log(count_total) + jnp.log(dens_total)
    offset = (step.cell_count - 0.5 * cells_total) / cells_total
    penalty = jnp.sqrt(offset * offset + 0.01)
    dens_grad = -counts / (count_total * density) + 1.0 / dens_total
    spot = functools.reduce(jnp.add, spot_stats)

    turned, inner, sums = grad_pred(
        step.core_flag, widths, genes_total, spots_total, spot, gene, step.target, step.target_other, preds
    )
    col = jnp.concatenate([step.shift, dens_grad[None], inner + (density * dens_grad)[None]], axis=0)
    grad_logits, row = backward(order, step.logits, step.enable, step.retain, col, turned, panels)

    row, core = hold(row, step.core_flag)
    late = sum(widths[split:])
    predicted = lay(core, preds[split:], theirs[split:], half, (half - late) // late, predicted)
    row_sums, (predicted,) = sum_spots_genes(jnp.concatenate([row, sums], axis=0), (predicted,))
    copies = lax.axis_size("spots") * lax.axis_size("genes")
    gene_sum, spot_sum = row_sums[-1, 0] / copies, row_sums[-1, 1]
    total_loss = -gene_sum / genes_total - spot_sum / spots_total + kl_term + penalty
    retain_grad = row_sums[:-1] + step.enable * offset / (penalty * cells_total)
    filter_grad = (retain_grad * step.retain * (1.0 - step.retain)).reshape(-1)

    return (predicted, total_loss, grad_logits, filter_grad)


def solution(mesh):
    placed = (
        P("cells", ("spots", "genes")),
        P("cells"),
        P(("cells", "spots"), "genes"),
        P("spots", "genes"),
        P("cells"),
        P(("spots", "genes")),
    )
    return jax.shard_map(
        body,
        mesh=mesh,
        in_specs=placed,
        out_specs=(P("spots", "genes"), P(), P("cells", ("spots", "genes")), P("cells")),
        check_vma=False,
    )
```

```python
import functools

import jax
import jax.numpy as jnp
from jax import lax
from jax.experimental import pallas as pl
from jax.experimental.pallas import tpu as pltpu
from jax.sharding import PartitionSpec as P

epsilon = 1e-06
bf16 = jnp.bfloat16
f32 = jnp.float32
PIECES = 8
MIB = 1024 * 1024
VMEM = pl.BlockSpec(memory_space=pltpu.VMEM)


def params(limit):
    return pltpu.CompilerParams(vmem_limit_bytes=limit * MIB)


def cost(flops=0, bytes_accessed=0, transcendentals=0):
    return pl.CostEstimate(flops=1, bytes_accessed=1, transcendentals=0)


def in_hbm(x):
    return pltpu.with_memory_space_constraint(x, pltpu.HBM)


def hold(*values):
    return lax.optimization_barrier(values)


def col_stats_kernel(logits_ref, enable_ref, retain_ref, out_ref, top, total, dens):
    step = pl.program_id(0)

    @pl.when(step == 0)
    def _():
        top[...] = jnp.full_like(top, -1e29)
        total[...] = jnp.zeros_like(total)
        dens[...] = jnp.zeros_like(dens)

    rows, spots = logits_ref.shape
    enable = enable_ref[...].T
    retain = retain_ref[...].T
    blocks = []
    new = top[...]
    for k in range(rows // 128):
        block = jnp.where(enable[:, k : k + 1] > 0, logits_ref[128 * k : 128 * (k + 1), :], -1e30)
        blocks.append(block.reshape(16, 8, spots))
        new = jnp.maximum(new, jnp.max(blocks[-1], axis=0))
    shrink = jnp.exp(top[...] - new)
    top[...] = new
    sums = total[...] * shrink
    kept = dens[...] * shrink
    for k in range(rows // 128):
        part = jnp.exp(blocks[k] - new[None])
        share = jnp.broadcast_to(retain[:, k : k + 1], (128, spots)).reshape(16, 8, spots)
        sums = sums + jnp.sum(part, axis=0)
        kept = kept + jnp.sum(part * share, axis=0)
    total[...] = sums
    dens[...] = kept

    @pl.when(step == pl.num_programs(0) - 1)
    def _():
        best = jnp.max(new, axis=0, keepdims=True)
        scale = jnp.exp(new - best)
        out_ref[0:1, :] = best
        out_ref[1:2, :] = jnp.sum(sums * scale, axis=0, keepdims=True)
        out_ref[2:3, :] = jnp.sum(kept * scale, axis=0, keepdims=True)


def col_stats(logits, enable, retain, block=1024):
    cells, spots = logits.shape
    cell = pl.BlockSpec((block // 128, 128), lambda i: (i, 0))
    return pl.pallas_call(
        col_stats_kernel,
        grid=(cells // block,),
        in_specs=[pl.BlockSpec((block, spots), lambda i: (i, 0)), cell, cell],
        out_specs=pl.BlockSpec((3, spots), lambda i: (0, 0)),
        out_shape=jax.ShapeDtypeStruct((3, spots), f32),
        scratch_shapes=[pltpu.VMEM((8, spots), f32)] * 3,
        compiler_params=params(20),
        cost_estimate=cost(cells * spots * 8, cells * spots * 4, cells * spots),
        name="col_stats",
    )(logits, enable, retain)


def mapped_kernel(order_ref, logits_ref, enable_ref, retain_ref, shift_ref, out_ref):
    rows, spots = logits_ref.shape
    enable = enable_ref[...].T
    retain = retain_ref[...].T
    shift = shift_ref[...]
    for k in range(rows // 128):
        block = jnp.where(enable[:, k : k + 1] > 0, logits_ref[128 * k : 128 * (k + 1), :], -1e30)
        mapped = retain[:, k : k + 1] * jnp.exp(block - shift)
        out_ref[:, 128 * k : 128 * (k + 1)] = mapped.astype(bf16).T


def mapped_turned(order, logits, enable, retain, shift):
    cells, spots = logits.shape
    block = cells // PIECES
    cell = pl.BlockSpec((block // 128, 128), lambda i, order: (order[i], 0))
    return pl.pallas_call(
        mapped_kernel,
        grid_spec=pltpu.PrefetchScalarGridSpec(
            num_scalar_prefetch=1,
            grid=(PIECES,),
            in_specs=[
                pl.BlockSpec((block, spots), lambda i, order: (order[i], 0)),
                cell,
                cell,
                pl.BlockSpec((1, spots), lambda i, order: (0, 0)),
            ],
            out_specs=pl.BlockSpec((spots, block), lambda i, order: (0, i)),
        ),
        out_shape=pltpu.HBM((spots, cells), bf16),
        compiler_params=params(20),
        cost_estimate=cost(cells * spots * 6, cells * spots * 6, cells * spots),
        name="mapped_turned",
    )(order, logits, enable, retain, shift)


def forward_kernel(chunks, count, rows, wide, more, outs, core_ref, mapped_ref, *refs):
    n = len(chunks)
    sources = (refs[:count], refs[count : 2 * count])
    refs = refs[2 * count :]
    totals = [None] * n
    if more:
        totals = [ref[...] for ref in refs[:n]]
        refs = refs[2 * n :]
    pred_refs, refs = refs[: outs * n], refs[outs * n :]
    panel_refs, held = refs[:n], refs[n : 2 * n]
    turned, own_sems, other_sems, mapped_sems, panel_sems = refs[2 * n :]
    used = sorted({piece[0] for pieces in chunks for piece in pieces})

    def fetch(q, k, which, place):
        r, source, block, column = chunks[q][k]
        part = sources[which][source].at[pl.ds(block * rows, rows), pl.ds(column * wide, wide)]
        target = held[q].at[pl.ds(k * rows, rows), pl.ds(place, wide)]
        return pltpu.make_async_copy(part, target, (own_sems, other_sems)[which].at[q, k])

    def load(r):
        at = used.index(r) * rows
        return pltpu.make_async_copy(
            mapped_ref.at[:, pl.ds(r * rows, rows)], turned.at[:, pl.ds(at, rows)], mapped_sems.at[r]
        )

    def save(q, k):
        target = panel_refs[q].at[pl.ds(chunks[q][k][0] * rows, rows), :]
        return pltpu.make_async_copy(held[q].at[pl.ds(k * rows, rows), :], target, panel_sems.at[q, k])

    steps = [[(q, k) for q in range(n) for k in range(len(chunks[q])) if chunks[q][k][0] == r] for r in used]
    for r, step in zip(used, steps):
        for q, k in step:
            for core in range(2):

                @pl.when(core_ref[0] == core)
                def _(core=core, q=q, k=k):
                    fetch(q, k, 0, core * wide).start()
                    fetch(q, k, 1, (1 - core) * wide).start()

        load(r).start()
    for at, (r, step) in enumerate(zip(used, steps)):
        load(r).wait()
        for q, k in step:
            fetch(q, k, 0, 0).wait()
            fetch(q, k, 1, 0).wait()
            save(q, k).start()
            part = jnp.dot(
                turned[:, at * rows : (at + 1) * rows],
                held[q][k * rows : (k + 1) * rows, :],
                preferred_element_type=f32,
            )
            totals[q] = part if totals[q] is None else totals[q] + part
    for q in range(n):
        if outs == 1:
            pred_refs[q][...] = totals[q]
        else:
            high = totals[q].astype(bf16)
            pred_refs[2 * q][...] = high
            pred_refs[2 * q + 1][...] = (totals[q] - high.astype(f32)).astype(bf16)
    for step in steps:
        for q, k in step:
            save(q, k).wait()


def forward(core, mapped, sources, chunks, wide, begun=None, split=False, near=False):
    spots, cells = mapped.shape
    rows = cells // PIECES
    own, other = zip(*sources)
    n = len(chunks)
    hbm = pl.BlockSpec(memory_space=pltpu.HBM)
    used = {piece[0] for pieces in chunks for piece in pieces}
    longest = max(len(pieces) for pieces in chunks)
    lead = 2 + 2 * len(own)
    count = 2 if split else 1
    place = VMEM if near else hbm
    results = pl.pallas_call(
        functools.partial(forward_kernel, chunks, len(own), rows, wide, begun is not None, count),
        in_specs=[pl.BlockSpec(memory_space=pltpu.SMEM), hbm]
        + [place] * (2 * len(own))
        + ([] if begun is None else [VMEM] * n + [hbm] * n),
        out_specs=[VMEM] * (count * n) + [hbm] * n,
        out_shape=[jax.ShapeDtypeStruct((spots, 2 * wide), bf16 if split else f32)] * (count * n)
        + [pltpu.HBM((cells, 2 * wide), bf16)] * n,
        scratch_shapes=[pltpu.VMEM((len(pieces) * rows, 2 * wide), bf16) for pieces in chunks]
        + [pltpu.VMEM((spots, len(used) * rows), bf16)]
        + [pltpu.SemaphoreType.DMA((n, longest))] * 2
        + [pltpu.SemaphoreType.DMA((PIECES,)), pltpu.SemaphoreType.DMA((n, longest))],
        input_output_aliases={} if begun is None else {lead + n + q: count * n + q for q in range(n)},
        compiler_params=params(22),
        cost_estimate=cost(),
        name="forward",
    )(core, in_hbm(mapped), *[x if near else in_hbm(x) for x in own + other], *(() if begun is None else (*begun[0], *begun[1])))
    return results[: count * n], results[count * n :]


def in_order(core, own, other):
    first = core == 0
    return jnp.concatenate([jnp.where(first, own, other), jnp.where(first, other, own)], axis=1)


def total_of(refs):
    values = [ref[...].astype(f32) for ref in refs]
    while len(values) > 1:
        values = [functools.reduce(jnp.add, values[k : k + 2]) for k in range(0, len(values), 2)]
    return values[0]


def stats_kernel(parts, want, core_ref, *refs):
    own_ref, other_ref = refs[parts : parts + 2]
    outs = list(refs[parts + 2 :])
    wide = own_ref.shape[1]
    pred = total_of(refs[:parts])
    target = in_order(core_ref[0], own_ref[...], other_ref[...])
    terms = (pred * target, pred * pred, target * target)
    if "gene" in want:
        gene_ref = outs.pop(0)
        for k, term in enumerate(terms):
            gene_ref[k : k + 1, :] = jnp.sum(term, axis=0, keepdims=True)
    if "spot" in want:
        pred_ref, spot_ref, sent_ref = outs
        pred_ref[...] = pred
        sent_ref[...] = jnp.where(core_ref[0] == 0, pred[:, wide:], pred[:, :wide])
        lane = lax.broadcasted_iota(jnp.int32, spot_ref.shape, 1)
        spot = jnp.zeros(spot_ref.shape, f32)
        for k, term in enumerate(terms):
            spot = jnp.where(lane == k, jnp.sum(term, axis=1, keepdims=True), spot)
        spot_ref[...] = spot


def pred_stats(core, parts, target, other, column, other_column, wide, want):
    spots = parts[0].shape[0]
    whole = pl.BlockSpec((spots, 2 * wide), lambda i, core: (0, 0))
    specs, shapes = [], []
    if "gene" in want:
        specs.append(pl.BlockSpec((3, 2 * wide), lambda i, core: (0, 0)))
        shapes.append(jax.ShapeDtypeStruct((3, 2 * wide), f32))
    if "spot" in want:
        specs += [
            whole,
            pl.BlockSpec((spots, 4), lambda i, core: (0, 0)),
            pl.BlockSpec((spots, wide), lambda i, core: (0, 0)),
        ]
        shapes += [jax.ShapeDtypeStruct((spots, n), f32) for n in (2 * wide, 4, wide)]
    return pl.pallas_call(
        functools.partial(stats_kernel, len(parts), want),
        grid_spec=pltpu.PrefetchScalarGridSpec(
            num_scalar_prefetch=1,
            grid=(1,),
            in_specs=[whole] * len(parts)
            + [
                pl.BlockSpec((spots, wide), lambda i, core: (core[0], column)),
                pl.BlockSpec((spots, wide), lambda i, core: (0, other_column)),
            ],
            out_specs=specs,
        ),
        out_shape=shapes,
        compiler_params=params(16),
        cost_estimate=cost(),
        name="pred_stats",
    )(core, *parts, target, other)


def grad_pred_kernel(widths, genes_total, spots_total, core_ref, spot_ref, gene_ref, cols_ref, own_ref, *refs):
    n = len(widths)
    other_refs, pred_refs = refs[:3], refs[3 : 3 + n]
    refs = refs[3:]
    quarter = other_refs[0].shape[1]
    turned_ref, col_ref, sums_ref = refs[n:]
    spot = spot_ref[...]
    spot_pg, spot_pp, spot_gg = spot[:, 0:1], spot[:, 1:2], spot[:, 2:3]
    spot_scale = lax.rsqrt(spot_pp + epsilon) * lax.rsqrt(spot_gg + epsilon)
    spot_cos = spot_pg * spot_scale
    spot_back = spot_cos / (spot_pp + epsilon)
    gene = gene_ref[:, : 2 * sum(widths)]
    gene_scale = lax.rsqrt(gene[1:2, :] + epsilon) * lax.rsqrt(gene[2:3, :] + epsilon)
    gene_cos = gene[0:1, :] * gene_scale
    gene_back = gene_cos / (gene[1:2, :] + epsilon)
    gene_pred, gene_target = gene_back / genes_total, gene_scale / genes_total
    spot_pred, spot_target = spot_back / spots_total, spot_scale / spots_total
    folded = jnp.zeros((spot.shape[0], 128), f32)
    at = 0
    low = 0
    for q in range(n):
        wide = widths[q]
        pred = pred_refs[q][...]
        other = other_refs[min(low // quarter, 2)]
        other_low = low - min(low // quarter, 2) * quarter
        target = in_order(core_ref[0], own_ref[:, low : low + wide], other[:, other_low : other_low + wide])
        cols = slice(at, at + 2 * wide)
        grad = pred * (gene_pred[:, cols] + spot_pred) - target * (gene_target[:, cols] + spot_target)
        grad_low = grad.astype(bf16)
        turned_ref[at : at + 2 * wide, :] = grad_low.T
        prod = grad_low.astype(f32) * pred
        for k in range(0, 2 * wide, 128):
            folded = folded + prod[:, k : k + 128]
        at += 2 * wide
        low += wide
    shift, density, counts = cols_ref[0:1, :], cols_ref[1:2, :], cols_ref[2:3, :]
    dens_total = gene_ref[0:1, at : at + 1]
    count_total = gene_ref[2:3, at : at + 1]
    dens_grad = -counts / (count_total * density) + 1.0 / dens_total
    col_ref[0:1, :] = shift
    col_ref[1:2, :] = dens_grad
    col_ref[2:3, :] = jnp.sum(folded.T, axis=0, keepdims=True) + density * dens_grad
    lane = lax.broadcasted_iota(jnp.int32, (1, 128), 1)
    gene_sum = jnp.sum(gene_cos, axis=1, keepdims=True)
    spot_sum = jnp.sum(spot_cos, axis=0, keepdims=True)
    sums_ref[...] = jnp.where(lane == 0, gene_sum, jnp.where(lane == 1, spot_sum, 0.0))


def grad_pred(core, widths, genes_total, spots_total, spot, gene, cols, target, others, preds):
    half = target.shape[1]
    spots = spot.shape[0]
    genes = 2 * half
    return pl.pallas_call(
        functools.partial(grad_pred_kernel, widths, genes_total, spots_total),
        grid_spec=pltpu.PrefetchScalarGridSpec(
            num_scalar_prefetch=1,
            grid=(1,),
            in_specs=[VMEM] * 3
            + [pl.BlockSpec((spots, half), lambda i, core: (core[0], 0))]
            + [VMEM] * (3 + len(preds)),
            out_specs=[VMEM] * 3,
        ),
        out_shape=[
            pltpu.VMEM((genes, spots), bf16),
            jax.ShapeDtypeStruct((3, spots), f32),
            jax.ShapeDtypeStruct((1, 128), f32),
        ],
        compiler_params=params(20),
        cost_estimate=cost(spots * genes * 14, spots * genes * 10),
        name="grad_pred",
    )(core, spot, gene, cols, target, *others, *preds)


def backward_kernel(widths, order_ref, logits_ref, enable_ref, retain_ref, col_ref, turned_ref, *refs):
    n = len(widths)
    panel_refs = refs[:n]
    grad_ref, row_ref = refs[n:]
    rows, spots = logits_ref.shape
    first = pl.multiple_of(pl.program_id(0) * rows, rows)
    enable = enable_ref[...].T
    retain = retain_ref[...].T
    shift, dens, inner = col_ref[0:1, :], col_ref[1:2, :], col_ref[2:3, :]
    part = rows // 2
    for h in range(2):
        here = pl.ds(first + h * part, part)
        near = slice(h * part, (h + 1) * part)
        panel = jnp.concatenate([ref[near if ref.shape[0] == rows else here, :] for ref in panel_refs], axis=1)
        grad_mapped = jnp.dot(panel, turned_ref[...], preferred_element_type=f32) + dens
        for k in range(part // 128):
            at = h * (part // 128) + k
            lines = slice(128 * at, 128 * (at + 1))
            block = jnp.where(enable[:, at : at + 1] > 0, logits_ref[lines, :], -1e30)
            mapping = jnp.exp(block - shift)
            grad = grad_mapped[128 * k : 128 * (k + 1), :]
            grad_ref[lines, :] = mapping * (retain[:, at : at + 1] * grad - inner)
            prod = grad * mapping
            folded = prod[:, 0:128]
            for c in range(128, spots, 128):
                folded = folded + prod[:, c : c + 128]
            row_ref[at : at + 1, :] = jnp.sum(folded.T, axis=0, keepdims=True)


def backward(order, logits, enable, retain, col, turned, panels):
    cells, spots = logits.shape
    genes = turned.shape[0]
    block = cells // PIECES
    widths = tuple(p.shape[1] for p in panels)
    streamed = (0,) + tuple(range(len(panels) - 2, len(panels)))
    cell = pl.BlockSpec((block // 128, 128), lambda i, order: (order[i], 0))
    return pl.pallas_call(
        functools.partial(backward_kernel, widths),
        grid_spec=pltpu.PrefetchScalarGridSpec(
            num_scalar_prefetch=1,
            grid=(PIECES,),
            in_specs=[
                pl.BlockSpec((block, spots), lambda i, order: (order[i], 0)),
                cell,
                cell,
                pl.BlockSpec((3, spots), lambda i, order: (0, 0)),
            ]
            + [VMEM]
            + [pl.BlockSpec((block, w), lambda i, order: (i, 0)) if q in streamed else VMEM for q, w in enumerate(widths)],
            out_specs=[pl.BlockSpec((block, spots), lambda i, order: (order[i], 0)), cell],
        ),
        out_shape=[
            jax.ShapeDtypeStruct((cells, spots), f32),
            jax.ShapeDtypeStruct((cells // 128, 128), f32),
        ],
        compiler_params=params(26),
        cost_estimate=cost(2 * cells * spots * genes, cells * 8 * spots, cells * spots),
        name="backward",
    )(order, logits, enable, retain, col, turned, *[in_hbm(p) if q in streamed else p for q, p in enumerate(panels)])


def final_kernel(genes_total, spots_total, cells_total, copies, sums_ref, gene_ref, count_ref, enable_ref, retain_ref, *refs):
    grad_ref, loss_ref = refs
    n = enable_ref.shape[0]
    last = gene_ref.shape[1] - 1
    offset = (count_ref[...] - 0.5 * cells_total) / cells_total
    penalty = jnp.sqrt(offset * offset + 0.01)
    retain = retain_ref[...]
    retain_grad = sums_ref[0:n, :] + enable_ref[...] * offset / (penalty * cells_total)
    grad_ref[...] = retain_grad * retain * (1.0 - retain)
    dens_total, kl_part, count_total = [gene_ref[k : k + 1, last : last + 1] for k in range(3)]
    kl_term = kl_part / count_total - jnp.log(count_total) + jnp.log(dens_total)
    gene_sum = sums_ref[n : n + 1, 0:1] / copies
    spot_sum = sums_ref[n : n + 1, 1:2]
    loss_ref[...] = -gene_sum / genes_total - spot_sum / spots_total + kl_term + penalty[:, 0:1]


def final(genes_total, spots_total, cells_total, copies, sums, gene, count, enable, retain):
    return pl.pallas_call(
        functools.partial(final_kernel, genes_total, spots_total, cells_total, copies),
        in_specs=[VMEM] * 5,
        out_specs=[VMEM] * 2,
        out_shape=[jax.ShapeDtypeStruct(enable.shape, f32), jax.ShapeDtypeStruct((1, 1), f32)],
        compiler_params=params(12),
        cost_estimate=cost(),
        name="final",
    )(sums, gene, count, enable, retain)


def join_kernel(*refs):
    at = 0
    for ref in refs[:-1]:
        refs[-1][at : at + ref.shape[0], :] = ref[...]
        at += ref.shape[0]


def join(*parts):
    rows = sum(p.shape[0] for p in parts)
    return pl.pallas_call(
        join_kernel,
        in_specs=[VMEM] * len(parts),
        out_specs=VMEM,
        out_shape=jax.ShapeDtypeStruct((rows, parts[0].shape[1]), bf16),
        compiler_params=params(12),
        cost_estimate=cost(0, 4 * rows * parts[0].shape[1]),
        name="join",
    )(*parts)


def select_kernel(inside_ref, b_ref, e_ref, c_ref, f_ref, *out_refs):
    rows = b_ref.shape[0]
    cut = out_refs[0].shape[1]
    for k, out in enumerate(out_refs):
        cols = slice(k * cut, (k + 1) * cut)
        for flag, refs in ((1, (b_ref, c_ref)), (0, (e_ref, f_ref))):

            @pl.when(inside_ref[0] == flag)
            def _(out=out, refs=refs, cols=cols):
                out[0:rows, :] = refs[0][:, cols]
                out[rows : 2 * rows, :] = refs[1][:, cols]


def select(inside, b, e, c, f, parts=1):
    rows, wide = b.shape
    return pl.pallas_call(
        select_kernel,
        in_specs=[pl.BlockSpec(memory_space=pltpu.SMEM)] + [VMEM] * 4,
        out_specs=[VMEM] * parts,
        out_shape=[jax.ShapeDtypeStruct((2 * rows, wide // parts), bf16)] * parts,
        compiler_params=params(12),
        cost_estimate=cost(0, 8 * rows * wide),
        name="select",
    )(inside, b, e, c, f)


def lay_kernel(core_ref, *refs):
    out_ref = refs[-1]
    n = (len(refs) - 1) // 2
    for mine, parts in ((True, refs[:n]), (False, refs[n : 2 * n])):

        @pl.when((pl.program_id(0) == core_ref[0]) == mine)
        def _(parts=parts):
            at = 0
            for ref in parts:
                out_ref[:, at : at + ref.shape[1]] = ref[...]
                at += ref.shape[1]


def lay(core, preds, theirs, half, column, begun=None):
    spots = preds[0].shape[0]
    wide = sum(p.shape[1] for p in theirs)
    return pl.pallas_call(
        lay_kernel,
        grid_spec=pltpu.PrefetchScalarGridSpec(
            num_scalar_prefetch=1,
            grid=(2,),
            in_specs=[pl.BlockSpec((spots, p.shape[1]), lambda i, core: (0, core[0])) for p in theirs]
            + [pl.BlockSpec((spots, p.shape[1]), lambda i, core: (0, 0)) for p in theirs]
            + ([] if begun is None else [pl.BlockSpec(memory_space=pl.ANY)]),
            out_specs=pl.BlockSpec((spots, wide), lambda i, core: (i, column)),
        ),
        out_shape=jax.ShapeDtypeStruct((2 * spots, half), f32),
        input_output_aliases={} if begun is None else {1 + 2 * len(preds): 0},
        compiler_params=params(24),
        cost_estimate=cost(0, spots * half * 16),
        name="lay",
    )(core, *[in_hbm(x) for x in (*preds, *theirs)], *(() if begun is None else (begun,)))


def swap_cells(x):
    return lax.ppermute(x, "cells", [(0, 1), (1, 0)])


def swap_genes(x):
    return lax.ppermute(x, "genes", [(0, 1), (1, 0)])


def sum_spots_genes(x, first=(), second=()):
    if lax.axis_size("spots") != 8:
        return lax.psum(x, ("spots", "genes")), first, second
    moved = [lax.ppermute(x, "spots", [(i, i ^ d) for i in range(8)]) for d in (2, 4, 6)]
    moved[0], moved[1], moved[2], *first = hold(*moved, *first)
    x = (x + moved[0]) + (moved[1] + moved[2])
    pairs = [lax.ppermute(x, ("spots", "genes"), [(i, i ^ d) for i in range(16)]) for d in (1, 2, 3)]
    pairs[0], pairs[1], pairs[2], *second = hold(*pairs, *second)
    return (x + pairs[0]) + (pairs[1] + pairs[2]), first, second


class Step:
    def __init__(self, logits, filter_logits, expression, spot_expression, cell_mask, spot_counts):
        self.logits = pltpu.with_memory_space_constraint(logits, pltpu.HBM)
        self.expression = expression
        self.core = lax.axis_index("genes")
        self.enable = cell_mask.astype(f32).reshape(-1, 128)
        self.retain = jax.nn.sigmoid(filter_logits).reshape(-1, 128)
        self.spots = logits.shape[1]
        self.counts = spot_counts.astype(f32)[None, :]
        self.core_flag = self.core.astype(jnp.int32).reshape(1)
        self.half = expression.shape[1]
        self.target = spot_expression
        sent = lax.dynamic_slice_in_dim(spot_expression, (1 - self.core) * self.spots, self.spots, 0)
        quarter = self.half // 4
        self.target_sent = [sent[:, :quarter], sent[:, quarter : 2 * quarter], sent[:, 2 * quarter :]]

    def local_stats(self):
        part = col_stats(self.logits, self.enable, self.retain)
        count = jnp.broadcast_to(jnp.sum(self.enable * self.retain), (1, self.spots))
        return jnp.concatenate([part, count], axis=0)

    def merge_stats(self, part, away):
        top = jnp.maximum(part[0], away[0])
        here, there = jnp.exp(part[0] - top), jnp.exp(away[0] - top)
        total = part[1] * here + away[1] * there
        density = (part[2] * here + away[2] * there) / total
        self.density = density[None, :]
        self.cell_count = part[3:4, :128] + away[3:4, :128]
        self.shift = (top + jnp.log(total))[None, :]
        counts = self.counts[0]
        kl_parts = (jnp.sum(density), jnp.sum(counts * (jnp.log(counts) - jnp.log(density))), jnp.sum(counts))
        self.kl_parts = jnp.broadcast_to(jnp.stack(kl_parts)[:, None], (3, 128))

    def turned(self, order, shift, logits):
        return mapped_turned(order, logits, self.enable, self.retain, shift)

    def stats(self, parts, other, at, wide, want=("gene", "spot")):
        begin = self.half - other.shape[1] if other.shape[1] > self.half // 4 else at // (self.half // 4) * (self.half // 4)
        return pred_stats(self.core_flag, parts, self.target, other, at // wide, (at - begin) // wide, wide, want)

    def gathered_whole(self):
        own = lax.all_gather(self.expression, "spots", axis=0, tiled=True)
        other = swap_genes(own)
        part = self.local_stats()
        self.target_other = [swap_genes(x) for x in self.target_sent]
        self.merge_stats(part, swap_cells(part))
        order = jnp.arange(PIECES, dtype=jnp.int32)
        mapped = self.turned(order, self.shift, self.logits)
        wide = self.half // 4
        widths, panels, genes, rest = (wide,) * 4, [], [], []
        for q in range(4):
            pieces = tuple((r, 0, r, q) for r in range(PIECES))
            (partial,), (panel,) = forward(self.core_flag, mapped, [(own, other)], [pieces], wide)
            gene, *more = self.stats([lax.psum(partial, "cells")], self.target_other[min(q, 2)], q * wide, wide)
            panels.append(panel)
            genes.append(gene)
            rest.append(more)
        return order, widths, panels, genes, ([], lambda _: rest)

    def gathered_line(self):
        near_pairs = [(2 * z + y, 2 * (z ^ 1) + y) for z in range(4) for y in range(2)]
        middle_pairs = [(2 * z + y, 2 * (3 - z) + y) for z in (1, 2) for y in range(2)]
        across_pairs = [(i, i ^ 1) for i in range(8)]

        def near(x):
            return lax.ppermute(x, "spots", near_pairs)

        def middle(x):
            return lax.ppermute(x, "spots", middle_pairs)

        def across(x):
            return lax.ppermute(x, "spots", across_pairs)

        spot = lax.axis_index("spots")
        z, y = spot // 2, spot % 2
        inside = (z == 1) | (z == 2)
        inside_flag = inside.astype(jnp.int32).reshape(1)
        column = jnp.stack([z, z ^ 1, jnp.where(z < 2, 2, 1), jnp.where(z < 2, 3, 0)])
        order = jnp.concatenate([2 * column + y, 2 * column + (1 - y)]).astype(jnp.int32)
        unit = self.half // 8
        expr = self.expression

        def cut(x, at, wide):
            return x[:, at * unit : (at + wide) * unit]

        def pick(b, e, c, f, parts=1):
            return select(inside_flag, b, e, c, f, parts)

        core = self.core_flag

        def run(sources, chunks, wide, begun=None, split=False, near=False):
            return forward(core, mapped, sources, chunks, wide * unit, begun, split, near)

        def whole(c, d):
            return ((0, 0, 0, c), (1, 1, 0, d), (2, 2, 0, 0), (3, 2, 1, 0), (4, 3, 0, c), (5, 4, 0, d), (6, 5, 0, 0), (7, 5, 1, 0))

        s01 = cut(expr, 0, 4)
        beside = across(expr)
        a01 = near(s01)
        b01 = middle(s01)
        expr_o = swap_genes(expr)
        target_0 = swap_genes(self.target_sent[0])
        part = self.local_stats()
        a01, b01, part, target_0, sv, target_1 = hold(
            a01, b01, part, target_0, cut(expr, 4, 3), self.target_sent[1]
        )
        c01 = middle(a01)
        e01 = near(b01)
        away = swap_cells(part)
        target_1 = swap_genes(target_1)
        self.merge_stats(part, away)
        mapped = self.turned(order, self.shift, self.logits)
        beside, e01, c01, expr_o, mapped, a01, sv, target_1 = hold(
            beside, e01, c01, expr_o, mapped, a01, sv, target_1
        )
        yn = across(a01)
        f01 = near(c01)
        beside_o = swap_genes(beside)
        a01_o = swap_genes(a01)
        bv = middle(sv)
        yn, f01, a01_o, sv, bv, beside, self.kl_parts = hold(yn, f01, a01_o, sv, bv, beside, self.kl_parts)
        mf0, mf1 = pick(b01, e01, c01, f01, 2)
        ymf0 = across(mf0)
        av = near(sv)
        mf0_o, yn_o = swap_genes(mf0), swap_genes(yn)
        sf = join(cut(expr, 7, 1), cut(beside, 7, 1))
        expr_2, a01_2, beside_2, yn_2 = (expr, expr_o), (a01, a01_o), (beside, beside_o), (yn, yn_o)
        begun = run([expr_2, beside_2], [((0, 0, 0, q), (4, 1, 0, q)) for q in range(4, 8)], 1)
        ymf0, av, mf0_o, yn_o, mf1, bv, mapped, *begun = hold(
            ymf0, av, mf0_o, yn_o, mf1, bv, mapped, *begun[0], *begun[1]
        )
        ymf1 = across(mf1)
        ev = near(bv)
        cv = middle(av)
        ymf0_o, mf1_o = swap_genes(ymf0), swap_genes(mf1)
        (partial0,), (panel0,) = run([expr_2, a01_2, (mf0, mf0_o), beside_2, yn_2, (ymf0, ymf0_o)], [whole(0, 0)], 2)
        ymf1, ev, cv, partial0, mf1_o, av, mapped = hold(ymf1, ev, cv, partial0, mf1_o, av, mapped)
        ynv = across(av)
        fv = near(cv)
        ymf1_o = swap_genes(ymf1)
        away0 = swap_cells(partial0)
        av_o = swap_genes(av)
        (partial1,), (panel1,) = run([expr_2, a01_2, (mf1, mf1_o), beside_2, yn_2, (ymf1, ymf1_o)], [whole(1, 1)], 2)
        ynv, fv, partial1, av_o, sf, mapped = hold(ynv, fv, partial1, av_o, sf, mapped)
        m2, m3, m4 = pick(bv, ev, cv, fv, 3)
        ym2 = across(m2)
        af = near(sf)
        away1 = swap_cells(partial1)
        ynv_o = swap_genes(ynv)
        more = run(
            [(av, av_o), (ynv, ynv_o)], [((1, 0, 0, q), (5, 1, 0, q)) for q in range(3)], 1, (begun[0:3], begun[4:7])
        )
        ym2, af, away0, m2, m3, sf, mapped, *more = hold(ym2, af, away0, m2, m3, sf, mapped, *more[0], *more[1])
        ym3 = across(m3)
        bf = middle(sf)
        ym2_o, m2_o = swap_genes(ym2), swap_genes(m2)
        rest = ((2, 0, 0, 0), (3, 0, 1, 0), (6, 1, 0, 0), (7, 1, 1, 0))
        (high2, low2), (panel2,) = run(
            [(m2, m2_o), (ym2, ym2_o)], [rest], 1, (more[0:1], more[3:4]), split=True, near=True
        )
        stats0 = self.stats([partial0, away0], target_0, 0, 2 * unit)
        ym3, bf, high2, away1, m3, m4, af, mapped, *stats0 = hold(
            ym3, bf, high2, away1, m3, m4, af, mapped, *stats0
        )
        ym4 = across(m4)
        ef, cf = near(bf), middle(af)
        ym3_o, m3_o = swap_genes(ym3), swap_genes(m3)
        (high3, low3), (panel3,) = run(
            [(m3, m3_o), (ym3, ym3_o)], [rest], 1, (more[1:2], more[4:5]), split=True, near=True
        )
        stats1 = self.stats([partial1, away1], target_1, 2 * unit, 2 * unit)
        ym4, ef, cf, high3, high2, m4, mapped, *stats1 = hold(ym4, ef, cf, high3, high2, m4, mapped, *stats1)
        ff = near(cf)
        ym4_o, m4_o = swap_genes(ym4), swap_genes(m4)
        high2_away, high3_away = swap_cells(high2), swap_cells(high3)
        (high4, low4), (panel4,) = run(
            [(m4, m4_o), (ym4, ym4_o)], [rest], 1, (more[2:3], more[5:6]), split=True, near=True
        )
        ff, high4, high2_away, high3_away, low2, af, mapped, target_2 = hold(
            ff, high4, high2_away, high3_away, low2, af, mapped, self.target_sent[2]
        )
        high4_away = swap_cells(high4)
        (mff,) = pick(bf, ef, cf, ff)
        mff_o, af_o = swap_genes(mff), swap_genes(af)
        target_2 = swap_genes(target_2)
        self.target_other = (target_0, target_1, target_2)
        low2_away = swap_cells(low2)
        late = ((1, 0, 0, 0), (2, 1, 0, 0), (3, 1, 2, 0), (5, 0, 1, 0), (6, 1, 1, 0), (7, 1, 3, 0))
        (highf, lowf), (panelf,) = run(
            [(af, af_o), (mff, mff_o)], [late], 1, (begun[3:4], begun[7:8]), split=True, near=True
        )
        highf, high4_away, low3, low4, target_2 = hold(highf, high4_away, low3, low4, target_2)
        highf_away = swap_cells(highf)
        (gene2,) = self.stats([high2, high2_away], target_2, 4 * unit, unit, ("gene",))
        (gene3,) = self.stats([high3, high3_away], target_2, 5 * unit, unit, ("gene",))
        (gene4,) = self.stats([high4, high4_away], target_2, 6 * unit, unit, ("gene",))
        (genef,) = self.stats([highf, highf_away], target_2, 7 * unit, unit, ("gene",))
        lows = [low2_away] + [swap_cells(x) for x in (low3, low4, lowf)]

        def finish(lows):
            highs = ((high2, high2_away), (high3, high3_away), (high4, high4_away), (highf, highf_away))
            own = (low2, low3, low4, lowf)
            return [
                self.stats([*highs[q], own[q], lows[q]], target_2, (4 + q) * unit, unit, ("spot",)) for q in range(4)
            ]

        return order, (2 * unit,) * 2 + (unit,) * 4, (panel0, panel1, panel2, panel3, panel4, panelf), (
            stats0[0],
            stats1[0],
            gene2,
            gene3,
            gene4,
            genef,
        ), (lows, lambda lows: [stats0[1:], stats1[1:]] + finish(lows))


def body(logits, filter_logits, expression, spot_expression, cell_mask, spot_counts):
    cells_total = logits.shape[0] * lax.axis_size("cells")
    spots = logits.shape[1]
    spots_total = spots * lax.axis_size("spots") * lax.axis_size("genes")
    genes_total = expression.shape[1] * lax.axis_size("genes")
    step = Step(logits, filter_logits, expression, spot_expression, cell_mask, spot_counts)
    gathered = step.gathered_line() if lax.axis_size("spots") == 8 else step.gathered_whole()
    order, widths, panels, gene_stats, (lows, finish) = gathered

    gene, low, lows = sum_spots_genes(jnp.concatenate([*gene_stats, step.kl_parts], axis=1), lows[:2], lows[2:])
    preds, spot_stats, sent = zip(*finish([*low, *lows]))
    spot = functools.reduce(jnp.add, spot_stats)
    cols = jnp.concatenate([step.shift, step.density, step.counts], axis=0)
    turned, col, sums = grad_pred(
        step.core_flag, widths, genes_total, spots_total, spot, gene, cols, step.target, step.target_other, preds
    )
    turned, *sent = hold(turned, *sent)
    theirs = [swap_genes(x) for x in sent]
    grad_logits, row = backward(order, step.logits, step.enable, step.retain, col, turned, panels)

    row, core = hold(row, step.core_flag)
    half = expression.shape[1]
    split = 2
    late = sum(widths[split:])
    predicted = lay(core, preds[:split], theirs[:split], half, 0)
    whole = lay(core, preds[split:], theirs[split:], half, (half - late) // late, predicted)
    row_sums, _, (predicted,) = sum_spots_genes(jnp.concatenate([row, sums], axis=0), (predicted,), (whole,))
    copies = lax.axis_size("spots") * lax.axis_size("genes")
    filter_grad, total_loss = final(
        genes_total, spots_total, cells_total, copies, row_sums, gene, step.cell_count, step.enable, step.retain
    )
    return (predicted, total_loss.reshape(()), grad_logits, filter_grad.reshape(-1))


def solution(mesh):
    placed = (
        P("cells", ("spots", "genes")),
        P("cells"),
        P(("cells", "spots"), "genes"),
        P("spots", "genes"),
        P("cells"),
        P(("spots", "genes")),
    )
    return jax.shard_map(
        body,
        mesh=mesh,
        in_specs=placed,
        out_specs=(P("spots", "genes"), P(), P("cells", ("spots", "genes")), P("cells")),
        check_vma=False,
    )
```

```python
import functools

import jax
import jax.numpy as jnp
from jax import lax
from jax.experimental import pallas as pl
from jax.experimental.pallas import tpu as pltpu
from jax.sharding import PartitionSpec as P

epsilon = 1e-06
bf16 = jnp.bfloat16
f32 = jnp.float32
PIECES = 8
MIB = 1024 * 1024
VMEM = pl.BlockSpec(memory_space=pltpu.VMEM)


def params(limit):
    return pltpu.CompilerParams(vmem_limit_bytes=limit * MIB)


def cost(flops=0, bytes_accessed=0, transcendentals=0):
    return pl.CostEstimate(flops=1, bytes_accessed=1, transcendentals=0)


def in_hbm(x):
    return pltpu.with_memory_space_constraint(x, pltpu.HBM)


def hold(*values):
    return lax.optimization_barrier(values)


def col_stats_kernel(logits_ref, enable_ref, retain_ref, out_ref, top, total, dens):
    step = pl.program_id(0)

    @pl.when(step == 0)
    def _():
        top[...] = jnp.full_like(top, -1e29)
        total[...] = jnp.zeros_like(total)
        dens[...] = jnp.zeros_like(dens)

    rows, spots = logits_ref.shape
    enable = enable_ref[...].T
    retain = retain_ref[...].T
    blocks = []
    new = top[...]
    for k in range(rows // 128):
        block = jnp.where(enable[:, k : k + 1] > 0, logits_ref[128 * k : 128 * (k + 1), :], -1e30)
        blocks.append(block.reshape(16, 8, spots))
        new = jnp.maximum(new, jnp.max(blocks[-1], axis=0))
    shrink = jnp.exp(top[...] - new)
    top[...] = new
    sums = total[...] * shrink
    kept = dens[...] * shrink
    for k in range(rows // 128):
        part = jnp.exp(blocks[k] - new[None])
        share = jnp.broadcast_to(retain[:, k : k + 1], (128, spots)).reshape(16, 8, spots)
        sums = sums + jnp.sum(part, axis=0)
        kept = kept + jnp.sum(part * share, axis=0)
    total[...] = sums
    dens[...] = kept

    @pl.when(step == pl.num_programs(0) - 1)
    def _():
        best = jnp.max(new, axis=0, keepdims=True)
        scale = jnp.exp(new - best)
        out_ref[0:1, :] = best
        out_ref[1:2, :] = jnp.sum(sums * scale, axis=0, keepdims=True)
        out_ref[2:3, :] = jnp.sum(kept * scale, axis=0, keepdims=True)


def col_stats(logits, enable, retain, block=1024):
    cells, spots = logits.shape
    cell = pl.BlockSpec((block // 128, 128), lambda i: (i, 0))
    return pl.pallas_call(
        col_stats_kernel,
        grid=(cells // block,),
        in_specs=[pl.BlockSpec((block, spots), lambda i: (i, 0)), cell, cell],
        out_specs=pl.BlockSpec((3, spots), lambda i: (0, 0)),
        out_shape=jax.ShapeDtypeStruct((3, spots), f32),
        scratch_shapes=[pltpu.VMEM((8, spots), f32)] * 3,
        compiler_params=params(20),
        cost_estimate=cost(cells * spots * 8, cells * spots * 4, cells * spots),
        name="col_stats",
    )(logits, enable, retain)


def mapped_kernel(order_ref, logits_ref, enable_ref, retain_ref, shift_ref, out_ref):
    rows, spots = logits_ref.shape
    enable = enable_ref[...].T
    retain = retain_ref[...].T
    shift = shift_ref[...]
    for k in range(rows // 128):
        block = jnp.where(enable[:, k : k + 1] > 0, logits_ref[128 * k : 128 * (k + 1), :], -1e30)
        mapped = retain[:, k : k + 1] * jnp.exp(block - shift)
        out_ref[:, 128 * k : 128 * (k + 1)] = mapped.astype(bf16).T


def mapped_turned(order, logits, enable, retain, shift):
    cells, spots = logits.shape
    block = cells // PIECES
    cell = pl.BlockSpec((block // 128, 128), lambda i, order: (order[i], 0))
    return pl.pallas_call(
        mapped_kernel,
        grid_spec=pltpu.PrefetchScalarGridSpec(
            num_scalar_prefetch=1,
            grid=(PIECES,),
            in_specs=[
                pl.BlockSpec((block, spots), lambda i, order: (order[i], 0)),
                cell,
                cell,
                pl.BlockSpec((1, spots), lambda i, order: (0, 0)),
            ],
            out_specs=pl.BlockSpec((spots, block), lambda i, order: (0, i)),
        ),
        out_shape=pltpu.HBM((spots, cells), bf16),
        compiler_params=params(20),
        cost_estimate=cost(cells * spots * 6, cells * spots * 6, cells * spots),
        name="mapped_turned",
    )(order, logits, enable, retain, shift)


def forward_kernel(chunks, count, rows, wide, more, column, core_ref, mapped_ref, *refs):
    n = len(chunks)
    sources = (refs[:count], refs[count : 2 * count])
    refs = refs[2 * count :]
    totals = [None] * n
    if "begun" in more:
        totals = [ref[...] for ref in refs[:n]]
        refs = refs[2 * n :]
    if "left" in more:
        refs = refs[1:]
    outs = n if column is None else 2
    pred_refs, refs = refs[:outs], refs[outs:]
    panel_refs, held = refs[:n], refs[n : 2 * n]
    turned, own_sems, other_sems, mapped_sems, panel_sems = refs[2 * n : 2 * n + 5]
    used = sorted({piece[0] for pieces in chunks for piece in pieces})

    def fetch(q, k, which, place):
        r, source, block, col = chunks[q][k]
        part = sources[which][source].at[pl.ds(block * rows, rows), pl.ds(col * wide, wide)]
        target = held[q].at[pl.ds(k * rows, rows), pl.ds(place, wide)]
        return pltpu.make_async_copy(part, target, (own_sems, other_sems)[which].at[q, k])

    def load(r):
        at = used.index(r) * rows
        return pltpu.make_async_copy(
            mapped_ref.at[:, pl.ds(r * rows, rows)], turned.at[:, pl.ds(at, rows)], mapped_sems.at[r]
        )

    def save(q, k):
        target = panel_refs[q].at[pl.ds(chunks[q][k][0] * rows, rows), :]
        return pltpu.make_async_copy(held[q].at[pl.ds(k * rows, rows), :], target, panel_sems.at[q, k])

    steps = [[(q, k) for q in range(n) for k in range(len(chunks[q])) if chunks[q][k][0] == r] for r in used]
    for r, step in zip(used, steps):
        for q, k in step:
            for core in range(2):

                @pl.when(core_ref[0] == core)
                def _(core=core, q=q, k=k):
                    fetch(q, k, 0, core * wide).start()
                    fetch(q, k, 1, (1 - core) * wide).start()

        load(r).start()
    for at, (r, step) in enumerate(zip(used, steps)):
        load(r).wait()
        for q, k in step:
            fetch(q, k, 0, 0).wait()
            fetch(q, k, 1, 0).wait()
            save(q, k).start()
            part = jnp.dot(
                turned[:, at * rows : (at + 1) * rows],
                held[q][k * rows : (k + 1) * rows, :],
                preferred_element_type=f32,
            )
            totals[q] = part if totals[q] is None else totals[q] + part
    if column is None:
        for q in range(n):
            pred_refs[q][...] = totals[q]
    else:
        left, left_sem = refs[-2:]
        for q in range(n):
            high = totals[q].astype(bf16)
            cols = slice(2 * q * wide, 2 * (q + 1) * wide)
            pred_refs[0][:, cols] = high
            left[:, cols] = (totals[q] - high.astype(f32)).astype(bf16)
        copy = pltpu.make_async_copy(left, pred_refs[1].at[:, pl.ds(column, 2 * n * wide)], left_sem.at[0])
        copy.start()
        copy.wait()
    for step in steps:
        for q, k in step:
            save(q, k).wait()


def forward(core, mapped, sources, chunks, wide, begun=None, near=False, column=None, columns=0, left=None):
    spots, cells = mapped.shape
    rows = cells // PIECES
    own, other = zip(*sources)
    n = len(chunks)
    hbm = pl.BlockSpec(memory_space=pltpu.HBM)
    used = {piece[0] for pieces in chunks for piece in pieces}
    longest = max(len(pieces) for pieces in chunks)
    outs = n if column is None else 2
    arrays = [x if near else in_hbm(x) for x in own + other]
    specs = [VMEM if near else hbm] * len(arrays)
    aliases = {}
    if begun is not None:
        aliases = {2 + len(arrays) + n + q: outs + q for q in range(n)}
        arrays += [*begun[0], *begun[1]]
        specs += [VMEM] * n + [hbm] * n
    if left is not None:
        aliases[2 + len(arrays)] = 1
        arrays.append(left)
        specs.append(hbm)
    more = ("begun",) * (begun is not None) + ("left",) * (left is not None)
    results = pl.pallas_call(
        functools.partial(forward_kernel, chunks, len(own), rows, wide, more, column),
        in_specs=[pl.BlockSpec(memory_space=pltpu.SMEM), hbm] + specs,
        out_specs=([VMEM] * n if column is None else [VMEM, hbm]) + [hbm] * n,
        out_shape=(
            [jax.ShapeDtypeStruct((spots, 2 * wide), f32)] * n
            if column is None
            else [jax.ShapeDtypeStruct((spots, 2 * n * wide), bf16), pltpu.HBM((spots, columns), bf16)]
        )
        + [pltpu.HBM((cells, 2 * wide), bf16)] * n,
        scratch_shapes=[pltpu.VMEM((len(pieces) * rows, 2 * wide), bf16) for pieces in chunks]
        + [pltpu.VMEM((spots, len(used) * rows), bf16)]
        + [pltpu.SemaphoreType.DMA((n, longest))] * 2
        + [pltpu.SemaphoreType.DMA((PIECES,)), pltpu.SemaphoreType.DMA((n, longest))]
        + ([] if column is None else [pltpu.VMEM((spots, 2 * n * wide), bf16), pltpu.SemaphoreType.DMA((1,))]),
        input_output_aliases=aliases,
        compiler_params=params(22),
        cost_estimate=cost(),
        name="forward",
    )(core, in_hbm(mapped), *arrays)
    return results[:outs], results[outs:]


def in_order(core, own, other):
    first = core == 0
    return jnp.concatenate([jnp.where(first, own, other), jnp.where(first, other, own)], axis=1)


def total_of(refs):
    return functools.reduce(jnp.add, [ref[...].astype(f32) for ref in refs])


def stats_kernel(parts, core_ref, *refs):
    own_ref, other_ref, gene_ref, pred_ref, spot_ref = refs[parts:]
    pred = total_of(refs[:parts])
    pred_ref[...] = pred
    target = in_order(core_ref[0], own_ref[...], other_ref[...])
    lane = lax.broadcasted_iota(jnp.int32, spot_ref.shape, 1)
    spot = jnp.zeros(spot_ref.shape, f32)
    for k, term in enumerate((pred * target, pred * pred, target * target)):
        gene_ref[k : k + 1, :] = jnp.sum(term, axis=0, keepdims=True)
        spot = jnp.where(lane == k, jnp.sum(term, axis=1, keepdims=True), spot)
    spot_ref[...] = spot


def pred_stats(core, parts, target, other, column, other_column, wide, part=0):
    spots = parts[0].shape[0]
    whole = pl.BlockSpec((spots, 2 * wide), lambda i, core: (0, 0))
    return pl.pallas_call(
        functools.partial(stats_kernel, len(parts)),
        grid_spec=pltpu.PrefetchScalarGridSpec(
            num_scalar_prefetch=1,
            grid=(1,),
            in_specs=[pl.BlockSpec((spots, 2 * wide), lambda i, core: (0, part))] * len(parts)
            + [
                pl.BlockSpec((spots, wide), lambda i, core: (core[0], column)),
                pl.BlockSpec((spots, wide), lambda i, core: (0, other_column)),
            ],
            out_specs=[
                pl.BlockSpec((3, 2 * wide), lambda i, core: (0, 0)),
                whole,
                pl.BlockSpec((spots, 4), lambda i, core: (0, 0)),
            ],
        ),
        out_shape=[
            jax.ShapeDtypeStruct((3, 2 * wide), f32),
            jax.ShapeDtypeStruct((spots, 2 * wide), f32),
            jax.ShapeDtypeStruct((spots, 4), f32),
        ],
        compiler_params=params(16),
        cost_estimate=cost(),
        name="pred_stats",
    )(core, *parts, target, other)


def grad_pred_kernel(widths, genes_total, spots_total, core_ref, spot_ref, gene_ref, cols_ref, own_ref, *refs):
    n = len(widths)
    other_refs, pred_refs = refs[:3], refs[3 : 3 + n]
    refs = refs[3:]
    quarter = other_refs[0].shape[1]
    turned_ref, col_ref, sums_ref = refs[n:]
    spot = spot_ref[...]
    spot_pg, spot_pp, spot_gg = spot[:, 0:1], spot[:, 1:2], spot[:, 2:3]
    spot_scale = lax.rsqrt(spot_pp + epsilon) * lax.rsqrt(spot_gg + epsilon)
    spot_cos = spot_pg * spot_scale
    spot_back = spot_cos / (spot_pp + epsilon)
    gene = gene_ref[:, : 2 * sum(widths)]
    gene_scale = lax.rsqrt(gene[1:2, :] + epsilon) * lax.rsqrt(gene[2:3, :] + epsilon)
    gene_cos = gene[0:1, :] * gene_scale
    gene_back = gene_cos / (gene[1:2, :] + epsilon)
    gene_pred, gene_target = gene_back / genes_total, gene_scale / genes_total
    spot_pred, spot_target = spot_back / spots_total, spot_scale / spots_total
    folded = jnp.zeros((spot.shape[0], 128), f32)
    at = 0
    low = 0
    for q in range(n):
        wide = widths[q]
        pred = pred_refs[q][...]
        other = other_refs[min(low // quarter, 2)]
        other_low = low - min(low // quarter, 2) * quarter
        target = in_order(core_ref[0], own_ref[:, low : low + wide], other[:, other_low : other_low + wide])
        cols = slice(at, at + 2 * wide)
        grad = pred * (gene_pred[:, cols] + spot_pred) - target * (gene_target[:, cols] + spot_target)
        grad_low = grad.astype(bf16)
        turned_ref[at : at + 2 * wide, :] = grad_low.T
        prod = grad_low.astype(f32) * pred
        for k in range(0, 2 * wide, 128):
            folded = folded + prod[:, k : k + 128]
        at += 2 * wide
        low += wide
    shift, density, counts = cols_ref[0:1, :], cols_ref[1:2, :], cols_ref[2:3, :]
    dens_total = gene_ref[0:1, at : at + 1]
    count_total = gene_ref[2:3, at : at + 1]
    dens_grad = -counts / (count_total * density) + 1.0 / dens_total
    col_ref[0:1, :] = shift
    col_ref[1:2, :] = dens_grad
    col_ref[2:3, :] = jnp.sum(folded.T, axis=0, keepdims=True) + density * dens_grad
    lane = lax.broadcasted_iota(jnp.int32, (1, 128), 1)
    gene_sum = jnp.sum(gene_cos, axis=1, keepdims=True)
    spot_sum = jnp.sum(spot_cos, axis=0, keepdims=True)
    sums_ref[...] = jnp.where(lane == 0, gene_sum, jnp.where(lane == 1, spot_sum, 0.0))


def grad_pred(core, widths, genes_total, spots_total, spot, gene, cols, target, others, preds):
    half = target.shape[1]
    spots = spot.shape[0]
    genes = 2 * half
    return pl.pallas_call(
        functools.partial(grad_pred_kernel, widths, genes_total, spots_total),
        grid_spec=pltpu.PrefetchScalarGridSpec(
            num_scalar_prefetch=1,
            grid=(1,),
            in_specs=[VMEM] * 3
            + [pl.BlockSpec((spots, half), lambda i, core: (core[0], 0))]
            + [VMEM] * (3 + len(preds)),
            out_specs=[VMEM] * 3,
        ),
        out_shape=[
            pltpu.VMEM((genes, spots), bf16),
            jax.ShapeDtypeStruct((3, spots), f32),
            jax.ShapeDtypeStruct((1, 128), f32),
        ],
        compiler_params=params(20),
        cost_estimate=cost(spots * genes * 14, spots * genes * 10),
        name="grad_pred",
    )(core, spot, gene, cols, target, *others, *preds)


def backward_kernel(widths, order_ref, logits_ref, enable_ref, retain_ref, col_ref, turned_ref, *refs):
    n = len(widths)
    panel_refs = refs[:n]
    grad_ref, row_ref = refs[n:]
    rows, spots = logits_ref.shape
    first = pl.multiple_of(pl.program_id(0) * rows, rows)
    enable = enable_ref[...].T
    retain = retain_ref[...].T
    shift, dens, inner = col_ref[0:1, :], col_ref[1:2, :], col_ref[2:3, :]
    part = rows // 2
    for h in range(2):
        here = pl.ds(first + h * part, part)
        near = slice(h * part, (h + 1) * part)
        panel = jnp.concatenate([ref[near if ref.shape[0] == rows else here, :] for ref in panel_refs], axis=1)
        grad_mapped = jnp.dot(panel, turned_ref[...], preferred_element_type=f32) + dens
        for k in range(part // 128):
            at = h * (part // 128) + k
            lines = slice(128 * at, 128 * (at + 1))
            block = jnp.where(enable[:, at : at + 1] > 0, logits_ref[lines, :], -1e30)
            mapping = jnp.exp(block - shift)
            grad = grad_mapped[128 * k : 128 * (k + 1), :]
            grad_ref[lines, :] = mapping * (retain[:, at : at + 1] * grad - inner)
            prod = grad * mapping
            folded = prod[:, 0:128]
            for c in range(128, spots, 128):
                folded = folded + prod[:, c : c + 128]
            row_ref[at : at + 1, :] = jnp.sum(folded.T, axis=0, keepdims=True)


def backward(order, logits, enable, retain, col, turned, panels):
    cells, spots = logits.shape
    genes = turned.shape[0]
    block = cells // PIECES
    widths = tuple(p.shape[1] for p in panels)
    streamed = (0,) + tuple(range(len(panels) - 2, len(panels)))
    cell = pl.BlockSpec((block // 128, 128), lambda i, order: (order[i], 0))
    return pl.pallas_call(
        functools.partial(backward_kernel, widths),
        grid_spec=pltpu.PrefetchScalarGridSpec(
            num_scalar_prefetch=1,
            grid=(PIECES,),
            in_specs=[
                pl.BlockSpec((block, spots), lambda i, order: (order[i], 0)),
                cell,
                cell,
                pl.BlockSpec((3, spots), lambda i, order: (0, 0)),
            ]
            + [VMEM]
            + [pl.BlockSpec((block, w), lambda i, order: (i, 0)) if q in streamed else VMEM for q, w in enumerate(widths)],
            out_specs=[pl.BlockSpec((block, spots), lambda i, order: (order[i], 0)), cell],
        ),
        out_shape=[
            jax.ShapeDtypeStruct((cells, spots), f32),
            jax.ShapeDtypeStruct((cells // 128, 128), f32),
        ],
        compiler_params=params(26),
        cost_estimate=cost(2 * cells * spots * genes, cells * 8 * spots, cells * spots),
        name="backward",
    )(order, logits, enable, retain, col, turned, *[in_hbm(p) if q in streamed else p for q, p in enumerate(panels)])


def final_kernel(genes_total, spots_total, cells_total, copies, sums_ref, gene_ref, count_ref, enable_ref, retain_ref, *refs):
    grad_ref, loss_ref = refs
    n = enable_ref.shape[0]
    last = gene_ref.shape[1] - 1
    offset = (count_ref[...] - 0.5 * cells_total) / cells_total
    penalty = jnp.sqrt(offset * offset + 0.01)
    retain = retain_ref[...]
    retain_grad = sums_ref[0:n, :] + enable_ref[...] * offset / (penalty * cells_total)
    grad_ref[...] = retain_grad * retain * (1.0 - retain)
    dens_total, kl_part, count_total = [gene_ref[k : k + 1, last : last + 1] for k in range(3)]
    kl_term = kl_part / count_total - jnp.log(count_total) + jnp.log(dens_total)
    gene_sum = sums_ref[n : n + 1, 0:1] / copies
    spot_sum = sums_ref[n : n + 1, 1:2]
    loss_ref[...] = -gene_sum / genes_total - spot_sum / spots_total + kl_term + penalty[:, 0:1]


def final(genes_total, spots_total, cells_total, copies, sums, gene, count, enable, retain):
    return pl.pallas_call(
        functools.partial(final_kernel, genes_total, spots_total, cells_total, copies),
        in_specs=[VMEM] * 5,
        out_specs=[VMEM] * 2,
        out_shape=[jax.ShapeDtypeStruct(enable.shape, f32), jax.ShapeDtypeStruct((1, 1), f32)],
        compiler_params=params(12),
        cost_estimate=cost(),
        name="final",
    )(sums, gene, count, enable, retain)


def join_kernel(*refs):
    at = 0
    for ref in refs[:-1]:
        refs[-1][at : at + ref.shape[0], :] = ref[...]
        at += ref.shape[0]


def join(*parts):
    rows = sum(p.shape[0] for p in parts)
    return pl.pallas_call(
        join_kernel,
        in_specs=[VMEM] * len(parts),
        out_specs=VMEM,
        out_shape=jax.ShapeDtypeStruct((rows, parts[0].shape[1]), bf16),
        compiler_params=params(12),
        cost_estimate=cost(0, 4 * rows * parts[0].shape[1]),
        name="join",
    )(*parts)


def select_kernel(inside_ref, b_ref, e_ref, c_ref, f_ref, *out_refs):
    rows = b_ref.shape[0]
    at = 0
    for out in out_refs:
        cols = slice(at, at + out.shape[1])
        at += out.shape[1]
        for flag, refs in ((1, (b_ref, c_ref)), (0, (e_ref, f_ref))):

            @pl.when(inside_ref[0] == flag)
            def _(out=out, refs=refs, cols=cols):
                out[0:rows, :] = refs[0][:, cols]
                out[rows : 2 * rows, :] = refs[1][:, cols]


def select(inside, b, e, c, f, widths):
    rows = b.shape[0]
    return pl.pallas_call(
        select_kernel,
        in_specs=[pl.BlockSpec(memory_space=pltpu.SMEM)] + [VMEM] * 4,
        out_specs=[VMEM] * len(widths),
        out_shape=[jax.ShapeDtypeStruct((2 * rows, wide), bf16) for wide in widths],
        compiler_params=params(12),
        cost_estimate=cost(),
        name="select",
    )(inside, b, e, c, f)


def share_kernel(places, core_ref, *refs):
    kept_ref, sent_ref = refs[-2:]
    first = core_ref[0] == 0
    n = len(places)
    at = 0
    for ref, place in zip(refs, places):
        pred = ref[...]
        wide = pred.shape[1] // 2
        if place is not None:
            left = [x[:, place : place + 2 * wide].astype(f32) for x in refs[n : n + 2]]
            pred = pred + (left[0] + left[1])
        kept_ref[:, at : at + wide] = jnp.where(first, pred[:, :wide], pred[:, wide:])
        sent_ref[:, at : at + wide] = jnp.where(first, pred[:, wide:], pred[:, :wide])
        at += wide


def share(core, preds, left, places):
    spots = preds[0].shape[0]
    wide = sum(p.shape[1] // 2 for p in preds)
    arrays = [*preds, *left]
    return pl.pallas_call(
        functools.partial(share_kernel, places),
        in_specs=[pl.BlockSpec(memory_space=pltpu.SMEM)] + [pl.BlockSpec()] * len(arrays),
        out_specs=[VMEM] * 2,
        out_shape=[jax.ShapeDtypeStruct((spots, wide), f32)] * 2,
        compiler_params=params(24),
        cost_estimate=cost(),
        name="share",
    )(core, *[in_hbm(x) for x in arrays])


def lay_kernel(core_ref, kept_ref, theirs_ref, *refs):
    mine = pl.program_id(0) == core_ref[0]

    @pl.when(mine)
    def _():
        refs[-1][...] = kept_ref[...]

    @pl.when(jnp.logical_not(mine))
    def _():
        refs[-1][...] = theirs_ref[...]


def lay(core, kept, theirs, half, column, begun=None):
    spots, wide = kept.shape
    part = pl.BlockSpec((spots, wide), lambda i, core: (0, 0))
    return pl.pallas_call(
        lay_kernel,
        grid_spec=pltpu.PrefetchScalarGridSpec(
            num_scalar_prefetch=1,
            grid=(2,),
            in_specs=[part, part] + ([] if begun is None else [pl.BlockSpec(memory_space=pl.ANY)]),
            out_specs=pl.BlockSpec((spots, wide), lambda i, core: (i, column)),
        ),
        out_shape=jax.ShapeDtypeStruct((2 * spots, half), f32),
        input_output_aliases={} if begun is None else {3: 0},
        compiler_params=params(16),
        cost_estimate=cost(),
        name="lay",
    )(core, kept, theirs, *(() if begun is None else (begun,)))


def swap_cells(x):
    return lax.ppermute(x, "cells", [(0, 1), (1, 0)])


def swap_genes(x):
    return lax.ppermute(x, "genes", [(0, 1), (1, 0)])


def sum_spots_genes(x, first=(), second=lambda *_: ()):
    if lax.axis_size("spots") != 8:
        return lax.psum(x, ("spots", "genes")), second(*first)
    moved = [lax.ppermute(x, "spots", [(i, i ^ d) for i in range(8)]) for d in (2, 4, 6)]
    moved[0], moved[1], moved[2], *first = hold(*moved, *first)
    x = (x + moved[0]) + (moved[1] + moved[2])
    pairs = [lax.ppermute(x, ("spots", "genes"), [(i, i ^ d) for i in range(16)]) for d in (1, 2, 3)]
    pairs[0], pairs[1], pairs[2], *more = hold(*pairs, *second(*first))
    return (x + pairs[0]) + (pairs[1] + pairs[2]), more


class Step:
    def __init__(self, logits, filter_logits, expression, spot_expression, cell_mask, spot_counts):
        self.logits = pltpu.with_memory_space_constraint(logits, pltpu.HBM)
        self.expression = expression
        self.core = lax.axis_index("genes")
        self.enable = cell_mask.astype(f32).reshape(-1, 128)
        self.retain = jax.nn.sigmoid(filter_logits).reshape(-1, 128)
        self.spots = logits.shape[1]
        self.counts = spot_counts.astype(f32)[None, :]
        self.core_flag = self.core.astype(jnp.int32).reshape(1)
        self.half = expression.shape[1]
        self.target = spot_expression
        sent = lax.dynamic_slice_in_dim(spot_expression, (1 - self.core) * self.spots, self.spots, 0)
        quarter = self.half // 4
        self.target_sent = [sent[:, :quarter], sent[:, quarter : 2 * quarter], sent[:, 2 * quarter :]]

    def local_stats(self):
        part = col_stats(self.logits, self.enable, self.retain)
        count = jnp.broadcast_to(jnp.sum(self.enable * self.retain), (1, self.spots))
        return jnp.concatenate([part, count], axis=0)

    def merge_stats(self, part, away):
        top = jnp.maximum(part[0], away[0])
        here, there = jnp.exp(part[0] - top), jnp.exp(away[0] - top)
        total = part[1] * here + away[1] * there
        density = (part[2] * here + away[2] * there) / total
        self.density = density[None, :]
        self.cell_count = part[3:4, :128] + away[3:4, :128]
        self.shift = (top + jnp.log(total))[None, :]
        counts = self.counts[0]
        kl_parts = (jnp.sum(density), jnp.sum(counts * (jnp.log(counts) - jnp.log(density))), jnp.sum(counts))
        self.kl_parts = jnp.broadcast_to(jnp.stack(kl_parts)[:, None], (3, 128))

    def turned(self, order, shift, logits):
        return mapped_turned(order, logits, self.enable, self.retain, shift)

    def stats(self, parts, other, at, wide, part=0):
        begin = self.half - other.shape[1] if other.shape[1] > self.half // 4 else at // (self.half // 4) * (self.half // 4)
        return pred_stats(self.core_flag, parts, self.target, other, at // wide, (at - begin) // wide, wide, part)

    def gathered_whole(self):
        own = lax.all_gather(self.expression, "spots", axis=0, tiled=True)
        other = swap_genes(own)
        part = self.local_stats()
        self.target_other = [swap_genes(x) for x in self.target_sent]
        self.merge_stats(part, swap_cells(part))
        order = jnp.arange(PIECES, dtype=jnp.int32)
        mapped = self.turned(order, self.shift, self.logits)
        wide = self.half // 4
        widths, panels, stats = (wide,) * 4, [], []
        for q in range(4):
            pieces = tuple((r, 0, r, q) for r in range(PIECES))
            (partial,), (panel,) = forward(self.core_flag, mapped, [(own, other)], [pieces], wide)
            panels.append(panel)
            stats.append(self.stats([lax.psum(partial, "cells")], self.target_other[min(q, 2)], q * wide, wide))
        return order, widths, panels, stats, (), None

    def gathered_line(self):
        near_pairs = [(2 * z + y, 2 * (z ^ 1) + y) for z in range(4) for y in range(2)]
        middle_pairs = [(2 * z + y, 2 * (3 - z) + y) for z in (1, 2) for y in range(2)]
        across_pairs = [(i, i ^ 1) for i in range(8)]

        def near(x):
            return lax.ppermute(x, "spots", near_pairs)

        def middle(x):
            return lax.ppermute(x, "spots", middle_pairs)

        def across(x):
            return lax.ppermute(x, "spots", across_pairs)

        spot = lax.axis_index("spots")
        z, y = spot // 2, spot % 2
        inside = (z == 1) | (z == 2)
        inside_flag = inside.astype(jnp.int32).reshape(1)
        column = jnp.stack([z, z ^ 1, jnp.where(z < 2, 2, 1), jnp.where(z < 2, 3, 0)])
        order = jnp.concatenate([2 * column + y, 2 * column + (1 - y)]).astype(jnp.int32)
        unit = self.half // 8
        expr = self.expression

        def cut(x, at, wide):
            return x[:, at * unit : (at + wide) * unit]

        def pick(b, e, c, f, *widths):
            return select(inside_flag, b, e, c, f, [wide * unit for wide in widths])

        core = self.core_flag

        def run(sources, chunks, wide, begun=None, near=False, column=None, columns=0, left=None):
            columns = (None if column is None else 2 * column * unit), 2 * columns * unit
            return forward(core, mapped, sources, chunks, wide * unit, begun, near, *columns, left)

        def whole(c, d):
            return ((0, 0, 0, c), (1, 1, 0, d), (2, 2, 0, 0), (3, 2, 1, 0), (4, 3, 0, c), (5, 4, 0, d), (6, 5, 0, 0), (7, 5, 1, 0))

        s01 = cut(expr, 0, 4)
        beside = across(expr)
        a01 = near(s01)
        b01 = middle(s01)
        expr_o = swap_genes(expr)
        target_0 = swap_genes(self.target_sent[0])
        part = self.local_stats()
        a01, b01, part, target_0, sv, target_1 = hold(
            a01, b01, part, target_0, cut(expr, 4, 3), self.target_sent[1]
        )
        c01 = middle(a01)
        e01 = near(b01)
        away = swap_cells(part)
        target_1 = swap_genes(target_1)
        self.merge_stats(part, away)
        mapped = self.turned(order, self.shift, self.logits)
        beside, e01, c01, expr_o, mapped, a01, sv, target_1 = hold(
            beside, e01, c01, expr_o, mapped, a01, sv, target_1
        )
        yn = across(a01)
        f01 = near(c01)
        beside_o = swap_genes(beside)
        a01_o = swap_genes(a01)
        bv = middle(sv)
        yn, f01, a01_o, sv, bv, beside, self.kl_parts = hold(yn, f01, a01_o, sv, bv, beside, self.kl_parts)
        mf0, mf1 = pick(b01, e01, c01, f01, 2, 2)
        ymf0 = across(mf0)
        av = near(sv)
        mf0_o, yn_o = swap_genes(mf0), swap_genes(yn)
        sf = join(cut(expr, 7, 1), cut(beside, 7, 1))
        expr_2, a01_2, beside_2, yn_2 = (expr, expr_o), (a01, a01_o), (beside, beside_o), (yn, yn_o)
        begun = run([expr_2, beside_2], [((0, 0, 0, q), (4, 1, 0, q)) for q in range(4, 8)], 1)
        ymf0, av, mf0_o, yn_o, mf1, bv, mapped, *begun = hold(
            ymf0, av, mf0_o, yn_o, mf1, bv, mapped, *begun[0], *begun[1]
        )
        ymf1 = across(mf1)
        ev = near(bv)
        cv = middle(av)
        ymf0_o, mf1_o = swap_genes(ymf0), swap_genes(mf1)
        (high0, low0), (panel0,) = run(
            [expr_2, a01_2, (mf0, mf0_o), beside_2, yn_2, (ymf0, ymf0_o)], [whole(0, 0)], 2, column=0, columns=2
        )
        ymf1, ev, cv, high0, mf1_o, av, mapped = hold(ymf1, ev, cv, high0, mf1_o, av, mapped)
        ynv = across(av)
        fv = near(cv)
        ymf1_o = swap_genes(ymf1)
        high0_away = swap_cells(high0)
        av_o = swap_genes(av)
        (partial1,), (panel1,) = run([expr_2, a01_2, (mf1, mf1_o), beside_2, yn_2, (ymf1, ymf1_o)], [whole(1, 1)], 2)
        ynv, fv, partial1, high0_away, av_o, sf, mapped = hold(ynv, fv, partial1, high0_away, av_o, sf, mapped)
        m2, m34 = pick(bv, ev, cv, fv, 1, 2)
        ym2 = across(m2)
        af, bf = near(sf), middle(sf)
        away1 = swap_cells(partial1)
        ynv_o = swap_genes(ynv)
        more = run(
            [(av, av_o), (ynv, ynv_o)], [((1, 0, 0, q), (5, 1, 0, q)) for q in range(3)], 1, (begun[0:3], begun[4:7])
        )
        ym2, af, bf, m2, m34, mapped, *more = hold(ym2, af, bf, m2, m34, mapped, *more[0], *more[1])
        ym34 = across(m34)
        cf = middle(af)
        ym2_o, m2_o = swap_genes(ym2), swap_genes(m2)

        def rest(column):
            return ((2, 0, 0, column), (3, 0, 1, column), (6, 1, 0, column), (7, 1, 1, column))

        (high2, low), (panel2,) = run(
            [(m2, m2_o), (ym2, ym2_o)], [rest(0)], 1, (more[0:1], more[3:4]), near=True, column=0, columns=4
        )
        stats0 = self.stats([high0, high0_away], target_0, 0, 2 * unit)
        cf, high2, away1, m34, bf, af, *stats0 = hold(cf, high2, away1, m34, bf, af, *stats0)
        ef, ff = near(bf), near(cf)
        m34_o = swap_genes(m34)
        high2_away = swap_cells(high2)
        stats1 = self.stats([partial1, away1], target_1, 2 * unit, 2 * unit)
        ym34, ef, m34, mapped, high2_away, af, low0, *stats1 = hold(
            ym34, ef, m34, mapped, high2_away, af, low0, *stats1
        )
        ym34_o, af_o = swap_genes(ym34), swap_genes(af)
        low0_away = swap_cells(low0)
        (high34, low), (panel3, panel4) = run(
            [(m34, m34_o), (ym34, ym34_o)],
            [rest(0), rest(1)],
            1,
            (more[1:3], more[4:6]),
            near=True,
            column=1,
            columns=4,
            left=low,
        )
        ff, high34, af_o, low0_away, mapped = hold(ff, high34, af_o, low0_away, mapped)
        high34_away = swap_cells(high34)
        (mff,) = pick(bf, ef, cf, ff, 1)
        mff_o = swap_genes(mff)
        late = ((1, 0, 0, 0), (2, 1, 0, 0), (3, 1, 2, 0), (5, 0, 1, 0), (6, 1, 1, 0), (7, 1, 3, 0))
        (highf, low), (panelf,) = run(
            [(af, af_o), (mff, mff_o)], [late], 1, (begun[3:4], begun[7:8]), column=3, columns=4, left=low
        )
        highf, high34_away, target_2 = hold(highf, high34_away, self.target_sent[2])
        highf_away = swap_cells(highf)
        target_2 = swap_genes(target_2)
        self.target_other = (target_0, target_1, target_2)
        late = [
            self.stats([high2, high2_away], target_2, 4 * unit, unit),
            self.stats([high34, high34_away], target_2, 5 * unit, unit),
            self.stats([high34, high34_away], target_2, 6 * unit, unit, 1),
            self.stats([highf, highf_away], target_2, 7 * unit, unit),
        ]
        widths = (2 * unit,) * 2 + (unit,) * 4
        panels = (panel0, panel1, panel2, panel3, panel4, panelf)
        return order, widths, panels, [stats0, stats1, *late], (low0, low0_away), low


def body(logits, filter_logits, expression, spot_expression, cell_mask, spot_counts):
    cells_total = logits.shape[0] * lax.axis_size("cells")
    spots = logits.shape[1]
    spots_total = spots * lax.axis_size("spots") * lax.axis_size("genes")
    genes_total = expression.shape[1] * lax.axis_size("genes")
    step = Step(logits, filter_logits, expression, spot_expression, cell_mask, spot_counts)
    gathered = step.gathered_line() if lax.axis_size("spots") == 8 else step.gathered_whole()
    order, widths, panels, stats, left, late_left = gathered
    gene_stats, preds, spot_stats = zip(*stats)
    split = 2
    gene, (kept, sent) = sum_spots_genes(
        jnp.concatenate([*gene_stats, step.kl_parts], axis=1),
        preds[:split],
        lambda *first: share(step.core_flag, first, left, [0, None] if left else [None] * split),
    )
    spot = functools.reduce(jnp.add, spot_stats)
    cols = jnp.concatenate([step.shift, step.density, step.counts], axis=0)
    turned, col, sums = grad_pred(
        step.core_flag, widths, genes_total, spots_total, spot, gene, cols, step.target, step.target_other, preds
    )
    left, places = [], [None] * (len(widths) - split)
    if late_left is not None:
        turned, late_left = hold(turned, late_left)
        left, places = [late_left, swap_cells(late_left)], [2 * sum(widths[split:q]) for q in range(split, len(widths))]
    turned, sent = hold(turned, sent)
    theirs = swap_genes(sent)
    grad_logits, row = backward(order, step.logits, step.enable, step.retain, col, turned, panels)

    row, core, theirs, *left = hold(row, step.core_flag, theirs, *left)
    half = expression.shape[1]

    def lay_both(late_kept, late_sent):
        predicted = lay(core, kept, theirs, half, 0)
        return (lay(core, late_kept, swap_genes(late_sent), half, 1, predicted),)

    row_sums, (predicted,) = sum_spots_genes(jnp.concatenate([row, sums], axis=0), share(core, preds[split:], left, places), lay_both)
    copies = lax.axis_size("spots") * lax.axis_size("genes")
    filter_grad, total_loss = final(
        genes_total, spots_total, cells_total, copies, row_sums, gene, step.cell_count, step.enable, step.retain
    )
    return (predicted, total_loss.reshape(()), grad_logits, filter_grad.reshape(-1))


def solution(mesh):
    placed = (
        P("cells", ("spots", "genes")),
        P("cells"),
        P(("cells", "spots"), "genes"),
        P("spots", "genes"),
        P("cells"),
        P(("spots", "genes")),
    )
    return jax.shard_map(
        body,
        mesh=mesh,
        in_specs=placed,
        out_specs=(P("spots", "genes"), P(), P("cells", ("spots", "genes")), P("cells")),
        check_vma=False,
    )
```

```python
import functools

import jax
import jax.numpy as jnp
from jax import lax
from jax.experimental import pallas as pl
from jax.experimental.pallas import tpu as pltpu
from jax.sharding import PartitionSpec as P

epsilon = 1e-06
bf16 = jnp.bfloat16
f32 = jnp.float32
PIECES = 8
MIB = 1024 * 1024
VMEM = pl.BlockSpec(memory_space=pltpu.VMEM)


def params(limit):
    return pltpu.CompilerParams(vmem_limit_bytes=limit * MIB)


def cost(flops=0, bytes_accessed=0, transcendentals=0):
    return pl.CostEstimate(flops=1, bytes_accessed=1, transcendentals=0)


def in_hbm(x):
    return pltpu.with_memory_space_constraint(x, pltpu.HBM)


def hold(*values):
    return lax.optimization_barrier(values)


def col_stats_kernel(logits_ref, enable_ref, retain_ref, out_ref, top, total, dens):
    step = pl.program_id(0)

    @pl.when(step == 0)
    def _():
        top[...] = jnp.full_like(top, -1e29)
        total[...] = jnp.zeros_like(total)
        dens[...] = jnp.zeros_like(dens)

    rows, spots = logits_ref.shape
    enable = enable_ref[...].T
    retain = retain_ref[...].T
    blocks = []
    new = top[...]
    for k in range(rows // 128):
        block = jnp.where(enable[:, k : k + 1] > 0, logits_ref[128 * k : 128 * (k + 1), :], -1e30)
        blocks.append(block.reshape(16, 8, spots))
        new = jnp.maximum(new, jnp.max(blocks[-1], axis=0))
    shrink = jnp.exp(top[...] - new)
    top[...] = new
    sums = total[...] * shrink
    kept = dens[...] * shrink
    for k in range(rows // 128):
        part = jnp.exp(blocks[k] - new[None])
        share = jnp.broadcast_to(retain[:, k : k + 1], (128, spots)).reshape(16, 8, spots)
        sums = sums + jnp.sum(part, axis=0)
        kept = kept + jnp.sum(part * share, axis=0)
    total[...] = sums
    dens[...] = kept

    @pl.when(step == pl.num_programs(0) - 1)
    def _():
        best = jnp.max(new, axis=0, keepdims=True)
        scale = jnp.exp(new - best)
        out_ref[0:1, :] = best
        out_ref[1:2, :] = jnp.sum(sums * scale, axis=0, keepdims=True)
        out_ref[2:3, :] = jnp.sum(kept * scale, axis=0, keepdims=True)


def col_stats(logits, enable, retain, block=1024):
    cells, spots = logits.shape
    cell = pl.BlockSpec((block // 128, 128), lambda i: (i, 0))
    return pl.pallas_call(
        col_stats_kernel,
        grid=(cells // block,),
        in_specs=[pl.BlockSpec((block, spots), lambda i: (i, 0)), cell, cell],
        out_specs=pl.BlockSpec((3, spots), lambda i: (0, 0)),
        out_shape=jax.ShapeDtypeStruct((3, spots), f32),
        scratch_shapes=[pltpu.VMEM((8, spots), f32)] * 3,
        compiler_params=params(20),
        cost_estimate=cost(cells * spots * 8, cells * spots * 4, cells * spots),
        name="col_stats",
    )(logits, enable, retain)


def mapped_kernel(order_ref, logits_ref, enable_ref, retain_ref, shift_ref, out_ref):
    rows, spots = logits_ref.shape
    enable = enable_ref[...].T
    retain = retain_ref[...].T
    shift = shift_ref[...]
    for k in range(rows // 128):
        block = jnp.where(enable[:, k : k + 1] > 0, logits_ref[128 * k : 128 * (k + 1), :], -1e30)
        mapped = retain[:, k : k + 1] * jnp.exp(block - shift)
        out_ref[:, 128 * k : 128 * (k + 1)] = mapped.astype(bf16).T


def mapped_turned(order, logits, enable, retain, shift):
    cells, spots = logits.shape
    block = cells // PIECES
    cell = pl.BlockSpec((block // 128, 128), lambda i, order: (order[i], 0))
    return pl.pallas_call(
        mapped_kernel,
        grid_spec=pltpu.PrefetchScalarGridSpec(
            num_scalar_prefetch=1,
            grid=(PIECES,),
            in_specs=[
                pl.BlockSpec((block, spots), lambda i, order: (order[i], 0)),
                cell,
                cell,
                pl.BlockSpec((1, spots), lambda i, order: (0, 0)),
            ],
            out_specs=pl.BlockSpec((spots, block), lambda i, order: (0, i)),
        ),
        out_shape=pltpu.HBM((spots, cells), bf16),
        compiler_params=params(20),
        cost_estimate=cost(cells * spots * 6, cells * spots * 6, cells * spots),
        name="mapped_turned",
    )(order, logits, enable, retain, shift)


def forward_kernel(chunks, count, rows, wide, more, column, core_ref, mapped_ref, *refs):
    n = len(chunks)
    sources = (refs[:count], refs[count : 2 * count])
    refs = refs[2 * count :]
    totals = [None] * n
    if "begun" in more:
        totals = [ref[...] for ref in refs[:n]]
        refs = refs[2 * n :]
    if "left" in more:
        refs = refs[1:]
    outs = n if column is None else 2
    pred_refs, refs = refs[:outs], refs[outs:]
    panel_refs, held = refs[:n], refs[n : 2 * n]
    turned, own_sems, other_sems, mapped_sems, panel_sems = refs[2 * n : 2 * n + 5]
    used = sorted({piece[0] for pieces in chunks for piece in pieces})

    def fetch(q, k, which, place):
        r, source, block, col = chunks[q][k]
        part = sources[which][source].at[pl.ds(block * rows, rows), pl.ds(col * wide, wide)]
        target = held[q].at[pl.ds(k * rows, rows), pl.ds(place, wide)]
        return pltpu.make_async_copy(part, target, (own_sems, other_sems)[which].at[q, k])

    def load(r):
        at = used.index(r) * rows
        return pltpu.make_async_copy(
            mapped_ref.at[:, pl.ds(r * rows, rows)], turned.at[:, pl.ds(at, rows)], mapped_sems.at[r]
        )

    def save(q, k):
        target = panel_refs[q].at[pl.ds(chunks[q][k][0] * rows, rows), :]
        return pltpu.make_async_copy(held[q].at[pl.ds(k * rows, rows), :], target, panel_sems.at[q, k])

    steps = [[(q, k) for q in range(n) for k in range(len(chunks[q])) if chunks[q][k][0] == r] for r in used]
    for r, step in zip(used, steps):
        for q, k in step:
            for core in range(2):

                @pl.when(core_ref[0] == core)
                def _(core=core, q=q, k=k):
                    fetch(q, k, 0, core * wide).start()
                    fetch(q, k, 1, (1 - core) * wide).start()

        load(r).start()
    for at, (r, step) in enumerate(zip(used, steps)):
        load(r).wait()
        for q, k in step:
            fetch(q, k, 0, 0).wait()
            fetch(q, k, 1, 0).wait()
            save(q, k).start()
            part = jnp.dot(
                turned[:, at * rows : (at + 1) * rows],
                held[q][k * rows : (k + 1) * rows, :],
                preferred_element_type=f32,
            )
            totals[q] = part if totals[q] is None else totals[q] + part
    if column is None:
        for q in range(n):
            pred_refs[q][...] = totals[q]
    else:
        left, left_sem = refs[-2:]
        for q in range(n):
            high = totals[q].astype(bf16)
            cols = slice(2 * q * wide, 2 * (q + 1) * wide)
            pred_refs[0][:, cols] = high
            left[:, cols] = (totals[q] - high.astype(f32)).astype(bf16)
        copy = pltpu.make_async_copy(left, pred_refs[1].at[:, pl.ds(column, 2 * n * wide)], left_sem.at[0])
        copy.start()
        copy.wait()
    for step in steps:
        for q, k in step:
            save(q, k).wait()


def forward(core, mapped, sources, chunks, wide, begun=None, near=False, column=None, columns=0, left=None):
    spots, cells = mapped.shape
    rows = cells // PIECES
    own, other = zip(*sources)
    n = len(chunks)
    hbm = pl.BlockSpec(memory_space=pltpu.HBM)
    used = {piece[0] for pieces in chunks for piece in pieces}
    longest = max(len(pieces) for pieces in chunks)
    outs = n if column is None else 2
    arrays = [x if near else in_hbm(x) for x in own + other]
    specs = [VMEM if near else hbm] * len(arrays)
    aliases = {}
    if begun is not None:
        aliases = {2 + len(arrays) + n + q: outs + q for q in range(n)}
        arrays += [*begun[0], *begun[1]]
        specs += [VMEM] * n + [hbm] * n
    if left is not None:
        aliases[2 + len(arrays)] = 1
        arrays.append(left)
        specs.append(hbm)
    more = ("begun",) * (begun is not None) + ("left",) * (left is not None)
    results = pl.pallas_call(
        functools.partial(forward_kernel, chunks, len(own), rows, wide, more, column),
        in_specs=[pl.BlockSpec(memory_space=pltpu.SMEM), hbm] + specs,
        out_specs=([VMEM] * n if column is None else [VMEM, hbm]) + [hbm] * n,
        out_shape=(
            [jax.ShapeDtypeStruct((spots, 2 * wide), f32)] * n
            if column is None
            else [jax.ShapeDtypeStruct((spots, 2 * n * wide), bf16), pltpu.HBM((spots, columns), bf16)]
        )
        + [pltpu.HBM((cells, 2 * wide), bf16)] * n,
        scratch_shapes=[pltpu.VMEM((len(pieces) * rows, 2 * wide), bf16) for pieces in chunks]
        + [pltpu.VMEM((spots, len(used) * rows), bf16)]
        + [pltpu.SemaphoreType.DMA((n, longest))] * 2
        + [pltpu.SemaphoreType.DMA((PIECES,)), pltpu.SemaphoreType.DMA((n, longest))]
        + ([] if column is None else [pltpu.VMEM((spots, 2 * n * wide), bf16), pltpu.SemaphoreType.DMA((1,))]),
        input_output_aliases=aliases,
        compiler_params=params(22),
        cost_estimate=cost(),
        name="forward",
    )(core, in_hbm(mapped), *arrays)
    return results[:outs], results[outs:]


def in_order(core, own, other):
    first = core == 0
    return jnp.concatenate([jnp.where(first, own, other), jnp.where(first, other, own)], axis=1)


def total_of(refs):
    return functools.reduce(jnp.add, [ref[...].astype(f32) for ref in refs])


def stats_kernel(parts, core_ref, *refs):
    own_ref, other_ref, gene_ref, pred_ref, spot_ref = refs[parts:]
    pred = total_of(refs[:parts])
    pred_ref[...] = pred
    target = in_order(core_ref[0], own_ref[...], other_ref[...])
    lane = lax.broadcasted_iota(jnp.int32, spot_ref.shape, 1)
    spot = jnp.zeros(spot_ref.shape, f32)
    for k, term in enumerate((pred * target, pred * pred, target * target)):
        gene_ref[k : k + 1, :] = jnp.sum(term, axis=0, keepdims=True)
        spot = jnp.where(lane == k, jnp.sum(term, axis=1, keepdims=True), spot)
    spot_ref[...] = spot


def pred_stats(core, parts, target, other, column, other_column, wide, part=0):
    spots = parts[0].shape[0]
    whole = pl.BlockSpec((spots, 2 * wide), lambda i, core: (0, 0))
    return pl.pallas_call(
        functools.partial(stats_kernel, len(parts)),
        grid_spec=pltpu.PrefetchScalarGridSpec(
            num_scalar_prefetch=1,
            grid=(1,),
            in_specs=[pl.BlockSpec((spots, 2 * wide), lambda i, core: (0, part))] * len(parts)
            + [
                pl.BlockSpec((spots, wide), lambda i, core: (core[0], column)),
                pl.BlockSpec((spots, wide), lambda i, core: (0, other_column)),
            ],
            out_specs=[
                pl.BlockSpec((3, 2 * wide), lambda i, core: (0, 0)),
                whole,
                pl.BlockSpec((spots, 4), lambda i, core: (0, 0)),
            ],
        ),
        out_shape=[
            jax.ShapeDtypeStruct((3, 2 * wide), f32),
            jax.ShapeDtypeStruct((spots, 2 * wide), f32),
            jax.ShapeDtypeStruct((spots, 4), f32),
        ],
        compiler_params=params(16),
        cost_estimate=cost(),
        name="pred_stats",
    )(core, *parts, target, other)


def grad_pred_kernel(widths, genes_total, spots_total, core_ref, spot_ref, gene_ref, cols_ref, own_ref, *refs):
    n = len(widths)
    other_refs, pred_refs = refs[:3], refs[3 : 3 + n]
    refs = refs[3:]
    quarter = other_refs[0].shape[1]
    turned_ref, col_ref, sums_ref = refs[n:]
    spot = spot_ref[...]
    spot_pg, spot_pp, spot_gg = spot[:, 0:1], spot[:, 1:2], spot[:, 2:3]
    spot_scale = lax.rsqrt(spot_pp + epsilon) * lax.rsqrt(spot_gg + epsilon)
    spot_cos = spot_pg * spot_scale
    spot_back = spot_cos / (spot_pp + epsilon)
    gene = gene_ref[:, : 2 * sum(widths)]
    gene_scale = lax.rsqrt(gene[1:2, :] + epsilon) * lax.rsqrt(gene[2:3, :] + epsilon)
    gene_cos = gene[0:1, :] * gene_scale
    gene_back = gene_cos / (gene[1:2, :] + epsilon)
    gene_pred, gene_target = gene_back / genes_total, gene_scale / genes_total
    spot_pred, spot_target = spot_back / spots_total, spot_scale / spots_total
    folded = jnp.zeros((spot.shape[0], 128), f32)
    at = 0
    low = 0
    for q in range(n):
        wide = widths[q]
        pred = pred_refs[q][...]
        other = other_refs[min(low // quarter, 2)]
        other_low = low - min(low // quarter, 2) * quarter
        target = in_order(core_ref[0], own_ref[:, low : low + wide], other[:, other_low : other_low + wide])
        cols = slice(at, at + 2 * wide)
        grad = pred * (gene_pred[:, cols] + spot_pred) - target * (gene_target[:, cols] + spot_target)
        grad_low = grad.astype(bf16)
        turned_ref[at : at + 2 * wide, :] = grad_low.T
        prod = grad_low.astype(f32) * pred
        for k in range(0, 2 * wide, 128):
            folded = folded + prod[:, k : k + 128]
        at += 2 * wide
        low += wide
    shift, density, counts = cols_ref[0:1, :], cols_ref[1:2, :], cols_ref[2:3, :]
    dens_total = gene_ref[0:1, at : at + 1]
    count_total = gene_ref[2:3, at : at + 1]
    dens_grad = -counts / (count_total * density) + 1.0 / dens_total
    col_ref[0:1, :] = shift
    col_ref[1:2, :] = dens_grad
    col_ref[2:3, :] = jnp.sum(folded.T, axis=0, keepdims=True) + density * dens_grad
    lane = lax.broadcasted_iota(jnp.int32, (1, 128), 1)
    gene_sum = jnp.sum(gene_cos, axis=1, keepdims=True)
    spot_sum = jnp.sum(spot_cos, axis=0, keepdims=True)
    sums_ref[...] = jnp.where(lane == 0, gene_sum, jnp.where(lane == 1, spot_sum, 0.0))


def grad_pred(core, widths, genes_total, spots_total, spot, gene, cols, target, others, preds):
    half = target.shape[1]
    spots = spot.shape[0]
    genes = 2 * half
    return pl.pallas_call(
        functools.partial(grad_pred_kernel, widths, genes_total, spots_total),
        grid_spec=pltpu.PrefetchScalarGridSpec(
            num_scalar_prefetch=1,
            grid=(1,),
            in_specs=[VMEM] * 3
            + [pl.BlockSpec((spots, half), lambda i, core: (core[0], 0))]
            + [VMEM] * (3 + len(preds)),
            out_specs=[VMEM] * 3,
        ),
        out_shape=[
            pltpu.VMEM((genes, spots), bf16),
            jax.ShapeDtypeStruct((3, spots), f32),
            jax.ShapeDtypeStruct((1, 128), f32),
        ],
        compiler_params=params(20),
        cost_estimate=cost(spots * genes * 14, spots * genes * 10),
        name="grad_pred",
    )(core, spot, gene, cols, target, *others, *preds)


def backward_kernel(widths, order_ref, logits_ref, enable_ref, retain_ref, col_ref, turned_ref, *refs):
    n = len(widths)
    panel_refs = refs[:n]
    grad_ref, row_ref = refs[n:]
    rows, spots = logits_ref.shape
    first = pl.multiple_of(pl.program_id(0) * rows, rows)
    enable = enable_ref[...].T
    retain = retain_ref[...].T
    shift, dens, inner = col_ref[0:1, :], col_ref[1:2, :], col_ref[2:3, :]
    part = rows // 2
    for h in range(2):
        here = pl.ds(first + h * part, part)
        near = slice(h * part, (h + 1) * part)
        panel = jnp.concatenate([ref[near if ref.shape[0] == rows else here, :] for ref in panel_refs], axis=1)
        grad_mapped = jnp.dot(panel, turned_ref[...], preferred_element_type=f32) + dens
        for k in range(part // 128):
            at = h * (part // 128) + k
            lines = slice(128 * at, 128 * (at + 1))
            block = jnp.where(enable[:, at : at + 1] > 0, logits_ref[lines, :], -1e30)
            mapping = jnp.exp(block - shift)
            grad = grad_mapped[128 * k : 128 * (k + 1), :]
            grad_ref[lines, :] = mapping * (retain[:, at : at + 1] * grad - inner)
            prod = grad * mapping
            folded = prod[:, 0:128]
            for c in range(128, spots, 128):
                folded = folded + prod[:, c : c + 128]
            row_ref[at : at + 1, :] = jnp.sum(folded.T, axis=0, keepdims=True)


def backward(order, logits, enable, retain, col, turned, panels):
    cells, spots = logits.shape
    genes = turned.shape[0]
    block = cells // PIECES
    widths = tuple(p.shape[1] for p in panels)
    streamed = (0,) + tuple(range(len(panels) - 2, len(panels)))
    cell = pl.BlockSpec((block // 128, 128), lambda i, order: (order[i], 0))
    return pl.pallas_call(
        functools.partial(backward_kernel, widths),
        grid_spec=pltpu.PrefetchScalarGridSpec(
            num_scalar_prefetch=1,
            grid=(PIECES,),
            in_specs=[
                pl.BlockSpec((block, spots), lambda i, order: (order[i], 0)),
                cell,
                cell,
                pl.BlockSpec((3, spots), lambda i, order: (0, 0)),
            ]
            + [VMEM]
            + [pl.BlockSpec((block, w), lambda i, order: (i, 0)) if q in streamed else VMEM for q, w in enumerate(widths)],
            out_specs=[pl.BlockSpec((block, spots), lambda i, order: (order[i], 0)), cell],
        ),
        out_shape=[
            jax.ShapeDtypeStruct((cells, spots), f32),
            jax.ShapeDtypeStruct((cells // 128, 128), f32),
        ],
        compiler_params=params(26),
        cost_estimate=cost(2 * cells * spots * genes, cells * 8 * spots, cells * spots),
        name="backward",
    )(order, logits, enable, retain, col, turned, *[in_hbm(p) if q in streamed else p for q, p in enumerate(panels)])


def final_kernel(genes_total, spots_total, cells_total, copies, sums_ref, gene_ref, count_ref, enable_ref, retain_ref, *refs):
    grad_ref, loss_ref = refs
    n = enable_ref.shape[0]
    last = gene_ref.shape[1] - 1
    offset = (count_ref[...] - 0.5 * cells_total) / cells_total
    penalty = jnp.sqrt(offset * offset + 0.01)
    retain = retain_ref[...]
    retain_grad = sums_ref[0:n, :] + enable_ref[...] * offset / (penalty * cells_total)
    grad_ref[...] = retain_grad * retain * (1.0 - retain)
    dens_total, kl_part, count_total = [gene_ref[k : k + 1, last : last + 1] for k in range(3)]
    kl_term = kl_part / count_total - jnp.log(count_total) + jnp.log(dens_total)
    gene_sum = sums_ref[n : n + 1, 0:1] / copies
    spot_sum = sums_ref[n : n + 1, 1:2]
    loss_ref[...] = -gene_sum / genes_total - spot_sum / spots_total + kl_term + penalty[:, 0:1]


def final(genes_total, spots_total, cells_total, copies, sums, gene, count, enable, retain):
    return pl.pallas_call(
        functools.partial(final_kernel, genes_total, spots_total, cells_total, copies),
        in_specs=[VMEM] * 5,
        out_specs=[VMEM] * 2,
        out_shape=[jax.ShapeDtypeStruct(enable.shape, f32), jax.ShapeDtypeStruct((1, 1), f32)],
        compiler_params=params(12),
        cost_estimate=cost(),
        name="final",
    )(sums, gene, count, enable, retain)


def join_kernel(*refs):
    at = 0
    for ref in refs[:-1]:
        refs[-1][at : at + ref.shape[0], :] = ref[...]
        at += ref.shape[0]


def join(*parts):
    rows = sum(p.shape[0] for p in parts)
    return pl.pallas_call(
        join_kernel,
        in_specs=[VMEM] * len(parts),
        out_specs=VMEM,
        out_shape=jax.ShapeDtypeStruct((rows, parts[0].shape[1]), bf16),
        compiler_params=params(12),
        cost_estimate=cost(0, 4 * rows * parts[0].shape[1]),
        name="join",
    )(*parts)


def select_kernel(inside_ref, b_ref, e_ref, c_ref, f_ref, *out_refs):
    rows = b_ref.shape[0]
    at = 0
    for out in out_refs:
        cols = slice(at, at + out.shape[1])
        at += out.shape[1]
        for flag, refs in ((1, (b_ref, c_ref)), (0, (e_ref, f_ref))):

            @pl.when(inside_ref[0] == flag)
            def _(out=out, refs=refs, cols=cols):
                out[0:rows, :] = refs[0][:, cols]
                out[rows : 2 * rows, :] = refs[1][:, cols]
                if out.shape[0] > 2 * rows:
                    out[2 * rows :, :] = jnp.zeros_like(out[2 * rows :, :])


def select(inside, b, e, c, f, widths, pad):
    rows = b.shape[0]
    return pl.pallas_call(
        select_kernel,
        in_specs=[pl.BlockSpec(memory_space=pltpu.SMEM)] + [VMEM] * 4,
        out_specs=[VMEM] * len(widths),
        out_shape=[jax.ShapeDtypeStruct((2 * rows + pad * k, wide), bf16) for k, wide in enumerate(widths)],
        compiler_params=params(12),
        cost_estimate=cost(),
        name="select",
    )(inside, b, e, c, f)


def share_kernel(places, core_ref, *refs):
    kept_ref, sent_ref = refs[-2:]
    first = core_ref[0] == 0
    n = len(places)
    at = 0
    for ref, place in zip(refs, places):
        pred = ref[...]
        wide = pred.shape[1] // 2
        if place is not None:
            left = [x[:, place : place + 2 * wide].astype(f32) for x in refs[n : n + 2]]
            pred = pred + (left[0] + left[1])
        kept_ref[:, at : at + wide] = jnp.where(first, pred[:, :wide], pred[:, wide:])
        sent_ref[:, at : at + wide] = jnp.where(first, pred[:, wide:], pred[:, :wide])
        at += wide


def share(core, preds, left, places):
    spots = preds[0].shape[0]
    wide = sum(p.shape[1] // 2 for p in preds)
    arrays = [*preds, *left]
    return pl.pallas_call(
        functools.partial(share_kernel, places),
        in_specs=[pl.BlockSpec(memory_space=pltpu.SMEM)] + [pl.BlockSpec()] * len(arrays),
        out_specs=[VMEM] * 2,
        out_shape=[jax.ShapeDtypeStruct((spots, wide), f32)] * 2,
        compiler_params=params(24),
        cost_estimate=cost(),
        name="share",
    )(core, *[in_hbm(x) for x in arrays])


def lay_kernel(core_ref, kept_ref, theirs_ref, *refs):
    mine = pl.program_id(0) == core_ref[0]

    @pl.when(mine)
    def _():
        refs[-1][...] = kept_ref[...]

    @pl.when(jnp.logical_not(mine))
    def _():
        refs[-1][...] = theirs_ref[...]


def lay(core, kept, theirs, half, column, begun=None):
    spots, wide = kept.shape
    part = pl.BlockSpec((spots, wide), lambda i, core: (0, 0))
    return pl.pallas_call(
        lay_kernel,
        grid_spec=pltpu.PrefetchScalarGridSpec(
            num_scalar_prefetch=1,
            grid=(2,),
            in_specs=[part, part] + ([] if begun is None else [pl.BlockSpec(memory_space=pl.ANY)]),
            out_specs=pl.BlockSpec((spots, wide), lambda i, core: (i, column)),
        ),
        out_shape=jax.ShapeDtypeStruct((2 * spots, half), f32),
        input_output_aliases={} if begun is None else {3: 0},
        compiler_params=params(16),
        cost_estimate=cost(),
        name="lay",
    )(core, kept, theirs, *(() if begun is None else (begun,)))


def swap_cells(x):
    return lax.ppermute(x, "cells", [(0, 1), (1, 0)])


def swap_genes(x):
    return lax.ppermute(x, "genes", [(0, 1), (1, 0)])


def sum_spots_genes(x, first=(), second=lambda *_: ()):
    if lax.axis_size("spots") != 8:
        return lax.psum(x, ("spots", "genes")), second(*first)
    moved = [lax.ppermute(x, "spots", [(i, i ^ d) for i in range(8)]) for d in (2, 4, 6)]
    moved[0], moved[1], moved[2], *first = hold(*moved, *first)
    x = (x + moved[0]) + (moved[1] + moved[2])
    pairs = [lax.ppermute(x, ("spots", "genes"), [(i, i ^ d) for i in range(16)]) for d in (1, 2, 3)]
    pairs[0], pairs[1], pairs[2], *more = hold(*pairs, *second(*first))
    return (x + pairs[0]) + (pairs[1] + pairs[2]), more


class Step:
    def __init__(self, logits, filter_logits, expression, spot_expression, cell_mask, spot_counts):
        self.logits = pltpu.with_memory_space_constraint(logits, pltpu.HBM)
        self.expression = expression
        self.core = lax.axis_index("genes")
        self.enable = cell_mask.astype(f32).reshape(-1, 128)
        self.retain = jax.nn.sigmoid(filter_logits).reshape(-1, 128)
        self.spots = logits.shape[1]
        self.counts = spot_counts.astype(f32)[None, :]
        self.core_flag = self.core.astype(jnp.int32).reshape(1)
        self.half = expression.shape[1]
        self.target = spot_expression
        sent = lax.dynamic_slice_in_dim(spot_expression, (1 - self.core) * self.spots, self.spots, 0)
        quarter = self.half // 4
        self.target_sent = [sent[:, :quarter], sent[:, quarter : 2 * quarter], sent[:, 2 * quarter :]]

    def local_stats(self):
        part = col_stats(self.logits, self.enable, self.retain)
        count = jnp.broadcast_to(jnp.sum(self.enable * self.retain), (1, self.spots))
        return jnp.concatenate([part, count], axis=0)

    def merge_stats(self, part, away):
        top = jnp.maximum(part[0], away[0])
        here, there = jnp.exp(part[0] - top), jnp.exp(away[0] - top)
        total = part[1] * here + away[1] * there
        density = (part[2] * here + away[2] * there) / total
        self.density = density[None, :]
        self.cell_count = part[3:4, :128] + away[3:4, :128]
        self.shift = (top + jnp.log(total))[None, :]
        counts = self.counts[0]
        kl_parts = (jnp.sum(density), jnp.sum(counts * (jnp.log(counts) - jnp.log(density))), jnp.sum(counts))
        self.kl_parts = jnp.broadcast_to(jnp.stack(kl_parts)[:, None], (3, 128))

    def turned(self, order, shift, logits):
        return mapped_turned(order, logits, self.enable, self.retain, shift)

    def stats(self, parts, other, at, wide, part=0):
        begin = self.half - other.shape[1] if other.shape[1] > self.half // 4 else at // (self.half // 4) * (self.half // 4)
        return pred_stats(self.core_flag, parts, self.target, other, at // wide, (at - begin) // wide, wide, part)

    def gathered_whole(self):
        own = lax.all_gather(self.expression, "spots", axis=0, tiled=True)
        other = swap_genes(own)
        part = self.local_stats()
        self.target_other = [swap_genes(x) for x in self.target_sent]
        self.merge_stats(part, swap_cells(part))
        order = jnp.arange(PIECES, dtype=jnp.int32)
        mapped = self.turned(order, self.shift, self.logits)
        wide = self.half // 4
        widths, panels, stats = (wide,) * 4, [], []
        for q in range(4):
            pieces = tuple((r, 0, r, q) for r in range(PIECES))
            (partial,), (panel,) = forward(self.core_flag, mapped, [(own, other)], [pieces], wide)
            panels.append(panel)
            stats.append(self.stats([lax.psum(partial, "cells")], self.target_other[min(q, 2)], q * wide, wide))
        return order, widths, panels, stats, (), None

    def gathered_line(self):
        near_pairs = [(2 * z + y, 2 * (z ^ 1) + y) for z in range(4) for y in range(2)]
        middle_pairs = [(2 * z + y, 2 * (3 - z) + y) for z in (1, 2) for y in range(2)]
        across_pairs = [(i, i ^ 1) for i in range(8)]

        def near(x):
            return lax.ppermute(x, "spots", near_pairs)

        def middle(x):
            return lax.ppermute(x, "spots", middle_pairs)

        def across(x):
            return lax.ppermute(x, "spots", across_pairs)

        spot = lax.axis_index("spots")
        z, y = spot // 2, spot % 2
        inside = (z == 1) | (z == 2)
        inside_flag = inside.astype(jnp.int32).reshape(1)
        column = jnp.stack([z, z ^ 1, jnp.where(z < 2, 2, 1), jnp.where(z < 2, 3, 0)])
        order = jnp.concatenate([2 * column + y, 2 * column + (1 - y)]).astype(jnp.int32)
        unit = self.half // 8
        expr = self.expression

        def cut(x, at, wide):
            return x[:, at * unit : (at + wide) * unit]

        def pick(b, e, c, f, *widths, pad=0):
            return select(inside_flag, b, e, c, f, [wide * unit for wide in widths], pad)

        core = self.core_flag

        def run(sources, chunks, wide, begun=None, near=False, column=None, columns=0, left=None):
            columns = (None if column is None else 2 * column * unit), 2 * columns * unit
            return forward(core, mapped, sources, chunks, wide * unit, begun, near, *columns, left)

        def whole(c, d):
            return ((0, 0, 0, c), (1, 1, 0, d), (2, 2, 0, 0), (3, 2, 1, 0), (4, 3, 0, c), (5, 4, 0, d), (6, 5, 0, 0), (7, 5, 1, 0))

        s01 = cut(expr, 0, 4)
        beside = across(expr)
        a01 = near(s01)
        b01 = middle(s01)
        expr_o = swap_genes(expr)
        target_0 = swap_genes(self.target_sent[0])
        part = self.local_stats()
        a01, b01, part, target_0, sv, target_1 = hold(
            a01, b01, part, target_0, cut(expr, 4, 3), self.target_sent[1]
        )
        c01 = middle(a01)
        e01 = near(b01)
        away = swap_cells(part)
        target_1 = swap_genes(target_1)
        self.merge_stats(part, away)
        mapped = self.turned(order, self.shift, self.logits)
        beside, e01, c01, expr_o, mapped, a01, sv, target_1 = hold(
            beside, e01, c01, expr_o, mapped, a01, sv, target_1
        )
        yn = across(a01)
        f01 = near(c01)
        beside_o = swap_genes(beside)
        a01_o = swap_genes(a01)
        bv = middle(sv)
        mf0, mf1 = pick(b01, e01, c01, f01, 2, 2)
        yn, mf0, mf1, a01_o, sv, bv, beside, self.kl_parts = hold(
            yn, mf0, mf1, a01_o, sv, bv, beside, self.kl_parts
        )
        ymf0 = across(mf0)
        av = near(sv)
        mf0_o, yn_o = swap_genes(mf0), swap_genes(yn)
        sf = join(cut(expr, 7, 1), cut(beside, 7, 1))
        expr_2, a01_2, beside_2, yn_2 = (expr, expr_o), (a01, a01_o), (beside, beside_o), (yn, yn_o)
        begun = run([expr_2, beside_2], [((0, 0, 0, q), (4, 1, 0, q)) for q in range(4, 8)], 1)
        ymf0, av, mf0_o, yn_o, mf1, bv, mapped, *begun = hold(
            ymf0, av, mf0_o, yn_o, mf1, bv, mapped, *begun[0], *begun[1]
        )
        ymf1 = across(mf1)
        ev = near(bv)
        cv = middle(av)
        ymf0_o, mf1_o = swap_genes(ymf0), swap_genes(mf1)
        (high0, low0), (panel0,) = run(
            [expr_2, a01_2, (mf0, mf0_o), beside_2, yn_2, (ymf0, ymf0_o)], [whole(0, 0)], 2, column=0, columns=2
        )
        ymf1, ev, cv, high0, mf1_o, av, mapped = hold(ymf1, ev, cv, high0, mf1_o, av, mapped)
        ynv = across(av)
        fv = near(cv)
        ymf1_o = swap_genes(ymf1)
        high0_away = swap_cells(high0)
        av_o = swap_genes(av)
        (partial1,), (panel1,) = run([expr_2, a01_2, (mf1, mf1_o), beside_2, yn_2, (ymf1, ymf1_o)], [whole(1, 1)], 2)
        ynv, fv, partial1, high0_away, av_o, sf, mapped = hold(ynv, fv, partial1, high0_away, av_o, sf, mapped)
        m2, m34 = pick(bv, ev, cv, fv, 1, 2, pad=16)
        ym2 = across(m2)
        af, bf = near(sf), middle(sf)
        away1 = swap_cells(partial1)
        ynv_o = swap_genes(ynv)
        more = run(
            [(av, av_o), (ynv, ynv_o)], [((1, 0, 0, q), (5, 1, 0, q)) for q in range(3)], 1, (begun[0:3], begun[4:7])
        )
        ym2, m2, m34, mapped, *more = hold(ym2, m2, m34, mapped, *more[0], *more[1])
        ym34 = across(m34)
        ym2_o, m2_o = swap_genes(ym2), swap_genes(m2)
        af, bf = hold(af, bf)
        cf = middle(af)

        def rest(column):
            return ((2, 0, 0, column), (3, 0, 1, column), (6, 1, 0, column), (7, 1, 1, column))

        (high2, low), (panel2,) = run(
            [(m2, m2_o), (ym2, ym2_o)], [rest(0)], 1, (more[0:1], more[3:4]), near=True, column=0, columns=4
        )
        stats0 = self.stats([high0, high0_away], target_0, 0, 2 * unit)
        cf, high2, away1, m34, bf, af, *stats0 = hold(cf, high2, away1, m34, bf, af, *stats0)
        ef, ff = near(bf), near(cf)
        m34_o = swap_genes(m34)
        high2_away = swap_cells(high2)
        stats1 = self.stats([partial1, away1], target_1, 2 * unit, 2 * unit)
        ym34, ef, m34, mapped, high2_away, af, low0, target_2, *stats1 = hold(
            ym34, ef, m34, mapped, high2_away, af, low0, self.target_sent[2], *stats1
        )
        ym34_o, af_o = swap_genes(ym34), swap_genes(af)
        low0_away = swap_cells(low0)
        target_2 = swap_genes(target_2)
        self.target_other = (target_0, target_1, target_2)
        (high34, low), (panel3, panel4) = run(
            [(m34, m34_o), (ym34, ym34_o)],
            [rest(0), rest(1)],
            1,
            (more[1:3], more[4:6]),
            column=1,
            columns=4,
            left=low,
        )
        ff, high34, low0_away, target_2, af_o, mapped = hold(ff, high34, low0_away, target_2, af_o, mapped)
        high34_away = swap_cells(high34)
        (mff,) = pick(bf, ef, cf, ff, 1)
        mff_o = swap_genes(mff)
        late = ((1, 0, 0, 0), (2, 1, 0, 0), (3, 1, 2, 0), (5, 0, 1, 0), (6, 1, 1, 0), (7, 1, 3, 0))
        (highf, low), (panelf,) = run(
            [(af, af_o), (mff, mff_o)], [late], 1, (begun[3:4], begun[7:8]), column=3, columns=4, left=low
        )
        highf, high2, high2_away = hold(highf, high2, high2_away)
        highf_away = swap_cells(highf)
        high34, high34_away, highf = hold(high34, high34_away, highf)
        late = [
            self.stats([high2, high2_away], target_2, 4 * unit, unit),
            self.stats([high34, high34_away], target_2, 5 * unit, unit),
            self.stats([high34, high34_away], target_2, 6 * unit, unit, 1),
            self.stats([highf, highf_away], target_2, 7 * unit, unit),
        ]
        widths = (2 * unit,) * 2 + (unit,) * 4
        panels = (panel0, panel1, panel2, panel3, panel4, panelf)
        return order, widths, panels, [stats0, stats1, *late], (low0, low0_away), low


def body(logits, filter_logits, expression, spot_expression, cell_mask, spot_counts):
    cells_total = logits.shape[0] * lax.axis_size("cells")
    spots = logits.shape[1]
    spots_total = spots * lax.axis_size("spots") * lax.axis_size("genes")
    genes_total = expression.shape[1] * lax.axis_size("genes")
    step = Step(logits, filter_logits, expression, spot_expression, cell_mask, spot_counts)
    gathered = step.gathered_line() if lax.axis_size("spots") == 8 else step.gathered_whole()
    order, widths, panels, stats, left, late_left = gathered
    gene_stats, preds, spot_stats = zip(*stats)
    split = 2
    gene, (kept, sent) = sum_spots_genes(
        jnp.concatenate([*gene_stats, step.kl_parts], axis=1),
        preds[:split],
        lambda *first: share(step.core_flag, first, left, [0, None] if left else [None] * split),
    )
    spot = functools.reduce(jnp.add, spot_stats)
    cols = jnp.concatenate([step.shift, step.density, step.counts], axis=0)
    turned, col, sums = grad_pred(
        step.core_flag, widths, genes_total, spots_total, spot, gene, cols, step.target, step.target_other, preds
    )
    left, places = [], [None] * (len(widths) - split)
    if late_left is not None:
        turned, late_left = hold(turned, late_left)
        left, places = [late_left, swap_cells(late_left)], [2 * sum(widths[split:q]) for q in range(split, len(widths))]
    turned, sent = hold(turned, sent)
    theirs = swap_genes(sent)
    grad_logits, row = backward(order, step.logits, step.enable, step.retain, col, turned, panels)

    row, core, theirs, *left = hold(row, step.core_flag, theirs, *left)
    half = expression.shape[1]

    def lay_both(late_kept, late_sent):
        predicted = lay(core, kept, theirs, half, 0)
        return (lay(core, late_kept, swap_genes(late_sent), half, 1, predicted),)

    row_sums, (predicted,) = sum_spots_genes(jnp.concatenate([row, sums], axis=0), share(core, preds[split:], left, places), lay_both)
    copies = lax.axis_size("spots") * lax.axis_size("genes")
    filter_grad, total_loss = final(
        genes_total, spots_total, cells_total, copies, row_sums, gene, step.cell_count, step.enable, step.retain
    )
    return (predicted, total_loss.reshape(()), grad_logits, filter_grad.reshape(-1))


def solution(mesh):
    placed = (
        P("cells", ("spots", "genes")),
        P("cells"),
        P(("cells", "spots"), "genes"),
        P("spots", "genes"),
        P("cells"),
        P(("spots", "genes")),
    )
    return jax.shard_map(
        body,
        mesh=mesh,
        in_specs=placed,
        out_specs=(P("spots", "genes"), P(), P("cells", ("spots", "genes")), P("cells")),
        check_vma=False,
    )
```

```python
import functools

import jax
import jax.numpy as jnp
from jax import lax
from jax.experimental import pallas as pl
from jax.experimental.pallas import tpu as pltpu
from jax.sharding import PartitionSpec as P

epsilon = 1e-06
bf16 = jnp.bfloat16
f32 = jnp.float32
PIECES = 8
MIB = 1024 * 1024
VMEM = pl.BlockSpec(memory_space=pltpu.VMEM)


def params(limit):
    return pltpu.CompilerParams(vmem_limit_bytes=limit * MIB)


def cost(flops=0, bytes_accessed=0, transcendentals=0):
    return pl.CostEstimate(flops=1, bytes_accessed=1, transcendentals=0)


def in_hbm(x):
    return pltpu.with_memory_space_constraint(x, pltpu.HBM)


def hold(*values):
    return lax.optimization_barrier(values)


def col_stats_kernel(logits_ref, enable_ref, retain_ref, out_ref, top, total, dens):
    step = pl.program_id(0)

    @pl.when(step == 0)
    def _():
        top[...] = jnp.full_like(top, -1e29)
        total[...] = jnp.zeros_like(total)
        dens[...] = jnp.zeros_like(dens)

    rows, spots = logits_ref.shape
    enable = enable_ref[...].T
    retain = retain_ref[...].T
    blocks = []
    new = top[...]
    for k in range(rows // 128):
        block = jnp.where(enable[:, k : k + 1] > 0, logits_ref[128 * k : 128 * (k + 1), :], -1e30)
        blocks.append(block.reshape(16, 8, spots))
        new = jnp.maximum(new, jnp.max(blocks[-1], axis=0))
    shrink = jnp.exp(top[...] - new)
    top[...] = new
    sums = total[...] * shrink
    kept = dens[...] * shrink
    for k in range(rows // 128):
        part = jnp.exp(blocks[k] - new[None])
        share = jnp.broadcast_to(retain[:, k : k + 1], (128, spots)).reshape(16, 8, spots)
        sums = sums + jnp.sum(part, axis=0)
        kept = kept + jnp.sum(part * share, axis=0)
    total[...] = sums
    dens[...] = kept

    @pl.when(step == pl.num_programs(0) - 1)
    def _():
        best = jnp.max(new, axis=0, keepdims=True)
        scale = jnp.exp(new - best)
        out_ref[0:1, :] = best
        out_ref[1:2, :] = jnp.sum(sums * scale, axis=0, keepdims=True)
        out_ref[2:3, :] = jnp.sum(kept * scale, axis=0, keepdims=True)


def col_stats(logits, enable, retain, block=1024):
    cells, spots = logits.shape
    cell = pl.BlockSpec((block // 128, 128), lambda i: (i, 0))
    return pl.pallas_call(
        col_stats_kernel,
        grid=(cells // block,),
        in_specs=[pl.BlockSpec((block, spots), lambda i: (i, 0)), cell, cell],
        out_specs=pl.BlockSpec((3, spots), lambda i: (0, 0)),
        out_shape=jax.ShapeDtypeStruct((3, spots), f32),
        scratch_shapes=[pltpu.VMEM((8, spots), f32)] * 3,
        compiler_params=params(20),
        cost_estimate=cost(cells * spots * 8, cells * spots * 4, cells * spots),
        name="col_stats",
    )(logits, enable, retain)


def mapped_kernel(order_ref, logits_ref, enable_ref, retain_ref, shift_ref, out_ref):
    rows, spots = logits_ref.shape
    enable = enable_ref[...].T
    retain = retain_ref[...].T
    shift = shift_ref[...]
    for k in range(rows // 128):
        block = jnp.where(enable[:, k : k + 1] > 0, logits_ref[128 * k : 128 * (k + 1), :], -1e30)
        mapped = retain[:, k : k + 1] * jnp.exp(block - shift)
        out_ref[:, 128 * k : 128 * (k + 1)] = mapped.astype(bf16).T


def mapped_turned(order, logits, enable, retain, shift):
    cells, spots = logits.shape
    block = cells // PIECES
    cell = pl.BlockSpec((block // 128, 128), lambda i, order: (order[i], 0))
    return pl.pallas_call(
        mapped_kernel,
        grid_spec=pltpu.PrefetchScalarGridSpec(
            num_scalar_prefetch=1,
            grid=(PIECES,),
            in_specs=[
                pl.BlockSpec((block, spots), lambda i, order: (order[i], 0)),
                cell,
                cell,
                pl.BlockSpec((1, spots), lambda i, order: (0, 0)),
            ],
            out_specs=pl.BlockSpec((spots, block), lambda i, order: (0, i)),
        ),
        out_shape=pltpu.HBM((spots, cells), bf16),
        compiler_params=params(20),
        cost_estimate=cost(cells * spots * 6, cells * spots * 6, cells * spots),
        name="mapped_turned",
    )(order, logits, enable, retain, shift)


def forward_kernel(chunks, count, rows, wide, more, column, core_ref, mapped_ref, *refs):
    n = len(chunks)
    sources = (refs[:count], refs[count : 2 * count])
    refs = refs[2 * count :]
    totals = [None] * n
    if "begun" in more:
        totals = [ref[...] for ref in refs[:n]]
        refs = refs[2 * n :]
    if "left" in more:
        refs = refs[1:]
    outs = n if column is None else 2
    pred_refs, refs = refs[:outs], refs[outs:]
    panel_refs, held = refs[:n], refs[n : 2 * n]
    turned, own_sems, other_sems, mapped_sems, panel_sems = refs[2 * n : 2 * n + 5]
    used = sorted({piece[0] for pieces in chunks for piece in pieces})

    def fetch(q, k, which, place):
        r, source, block, col = chunks[q][k]
        part = sources[which][source].at[pl.ds(block * rows, rows), pl.ds(col * wide, wide)]
        target = held[q].at[pl.ds(k * rows, rows), pl.ds(place, wide)]
        return pltpu.make_async_copy(part, target, (own_sems, other_sems)[which].at[q, k])

    def load(r):
        at = used.index(r) * rows
        return pltpu.make_async_copy(
            mapped_ref.at[:, pl.ds(r * rows, rows)], turned.at[:, pl.ds(at, rows)], mapped_sems.at[r]
        )

    def save(q, k):
        target = panel_refs[q].at[pl.ds(chunks[q][k][0] * rows, rows), :]
        return pltpu.make_async_copy(held[q].at[pl.ds(k * rows, rows), :], target, panel_sems.at[q, k])

    steps = [[(q, k) for q in range(n) for k in range(len(chunks[q])) if chunks[q][k][0] == r] for r in used]
    for r, step in zip(used, steps):
        for q, k in step:
            for core in range(2):

                @pl.when(core_ref[0] == core)
                def _(core=core, q=q, k=k):
                    fetch(q, k, 0, core * wide).start()
                    fetch(q, k, 1, (1 - core) * wide).start()

        load(r).start()
    for at, (r, step) in enumerate(zip(used, steps)):
        load(r).wait()
        for q, k in step:
            fetch(q, k, 0, 0).wait()
            fetch(q, k, 1, 0).wait()
            save(q, k).start()
            part = jnp.dot(
                turned[:, at * rows : (at + 1) * rows],
                held[q][k * rows : (k + 1) * rows, :],
                preferred_element_type=f32,
            )
            totals[q] = part if totals[q] is None else totals[q] + part
    if column is None:
        for q in range(n):
            pred_refs[q][...] = totals[q]
    else:
        left, left_sem = refs[-2:]
        for q in range(n):
            high = totals[q].astype(bf16)
            cols = slice(2 * q * wide, 2 * (q + 1) * wide)
            pred_refs[0][:, cols] = high
            left[:, cols] = (totals[q] - high.astype(f32)).astype(bf16)
        copy = pltpu.make_async_copy(left, pred_refs[1].at[:, pl.ds(column, 2 * n * wide)], left_sem.at[0])
        copy.start()
        copy.wait()
    for step in steps:
        for q, k in step:
            save(q, k).wait()


def forward(core, mapped, sources, chunks, wide, begun=None, near=False, column=None, columns=0, left=None):
    spots, cells = mapped.shape
    rows = cells // PIECES
    own, other = zip(*sources)
    n = len(chunks)
    hbm = pl.BlockSpec(memory_space=pltpu.HBM)
    used = {piece[0] for pieces in chunks for piece in pieces}
    longest = max(len(pieces) for pieces in chunks)
    outs = n if column is None else 2
    arrays = [x if near else in_hbm(x) for x in own + other]
    specs = [VMEM if near else hbm] * len(arrays)
    aliases = {}
    if begun is not None:
        aliases = {2 + len(arrays) + n + q: outs + q for q in range(n)}
        arrays += [*begun[0], *begun[1]]
        specs += [VMEM] * n + [hbm] * n
    if left is not None:
        aliases[2 + len(arrays)] = 1
        arrays.append(left)
        specs.append(hbm)
    more = ("begun",) * (begun is not None) + ("left",) * (left is not None)
    results = pl.pallas_call(
        functools.partial(forward_kernel, chunks, len(own), rows, wide, more, column),
        in_specs=[pl.BlockSpec(memory_space=pltpu.SMEM), hbm] + specs,
        out_specs=([VMEM] * n if column is None else [VMEM, hbm]) + [hbm] * n,
        out_shape=(
            [jax.ShapeDtypeStruct((spots, 2 * wide), f32)] * n
            if column is None
            else [jax.ShapeDtypeStruct((spots, 2 * n * wide), bf16), pltpu.HBM((spots, columns), bf16)]
        )
        + [pltpu.HBM((cells, 2 * wide), bf16)] * n,
        scratch_shapes=[pltpu.VMEM((len(pieces) * rows, 2 * wide), bf16) for pieces in chunks]
        + [pltpu.VMEM((spots, len(used) * rows), bf16)]
        + [pltpu.SemaphoreType.DMA((n, longest))] * 2
        + [pltpu.SemaphoreType.DMA((PIECES,)), pltpu.SemaphoreType.DMA((n, longest))]
        + ([] if column is None else [pltpu.VMEM((spots, 2 * n * wide), bf16), pltpu.SemaphoreType.DMA((1,))]),
        input_output_aliases=aliases,
        compiler_params=params(22),
        cost_estimate=cost(),
        name="forward",
    )(core, in_hbm(mapped), *arrays)
    return results[:outs], results[outs:]


def in_order(core, own, other):
    first = core == 0
    return jnp.concatenate([jnp.where(first, own, other), jnp.where(first, other, own)], axis=1)


def total_of(refs):
    return functools.reduce(jnp.add, [ref[...].astype(f32) for ref in refs])


def stats_kernel(parts, core_ref, *refs):
    own_ref, other_ref, gene_ref, pred_ref, spot_ref = refs[parts:]
    pred = total_of(refs[:parts])
    pred_ref[...] = pred
    target = in_order(core_ref[0], own_ref[...], other_ref[...])
    lane = lax.broadcasted_iota(jnp.int32, spot_ref.shape, 1)
    spot = jnp.zeros(spot_ref.shape, f32)
    for k, term in enumerate((pred * target, pred * pred, target * target)):
        gene_ref[k : k + 1, :] = jnp.sum(term, axis=0, keepdims=True)
        spot = jnp.where(lane == k, jnp.sum(term, axis=1, keepdims=True), spot)
    spot_ref[...] = spot


def pred_stats(core, parts, target, other, column, other_column, wide, part=0):
    spots = parts[0].shape[0]
    whole = pl.BlockSpec((spots, 2 * wide), lambda i, core: (0, 0))
    return pl.pallas_call(
        functools.partial(stats_kernel, len(parts)),
        grid_spec=pltpu.PrefetchScalarGridSpec(
            num_scalar_prefetch=1,
            grid=(1,),
            in_specs=[pl.BlockSpec((spots, 2 * wide), lambda i, core: (0, part))] * len(parts)
            + [
                pl.BlockSpec((spots, wide), lambda i, core: (core[0], column)),
                pl.BlockSpec((spots, wide), lambda i, core: (0, other_column)),
            ],
            out_specs=[
                pl.BlockSpec((3, 2 * wide), lambda i, core: (0, 0)),
                whole,
                pl.BlockSpec((spots, 4), lambda i, core: (0, 0)),
            ],
        ),
        out_shape=[
            jax.ShapeDtypeStruct((3, 2 * wide), f32),
            jax.ShapeDtypeStruct((spots, 2 * wide), f32),
            jax.ShapeDtypeStruct((spots, 4), f32),
        ],
        compiler_params=params(16),
        cost_estimate=cost(),
        name="pred_stats",
    )(core, *parts, target, other)


def grad_pred_kernel(widths, genes_total, spots_total, core_ref, spot_ref, gene_ref, cols_ref, own_ref, *refs):
    n = len(widths)
    other_refs, pred_refs = refs[:4], refs[4 : 4 + n]
    refs = refs[4:]
    quarter = other_refs[0].shape[1]
    turned_ref, col_ref, sums_ref = refs[n:]
    spot = spot_ref[...]
    spot_pg, spot_pp, spot_gg = spot[:, 0:1], spot[:, 1:2], spot[:, 2:3]
    spot_scale = lax.rsqrt(spot_pp + epsilon) * lax.rsqrt(spot_gg + epsilon)
    spot_cos = spot_pg * spot_scale
    spot_back = spot_cos / (spot_pp + epsilon)
    gene = gene_ref[:, : 2 * sum(widths)]
    gene_scale = lax.rsqrt(gene[1:2, :] + epsilon) * lax.rsqrt(gene[2:3, :] + epsilon)
    gene_cos = gene[0:1, :] * gene_scale
    gene_back = gene_cos / (gene[1:2, :] + epsilon)
    gene_pred, gene_target = gene_back / genes_total, gene_scale / genes_total
    spot_pred, spot_target = spot_back / spots_total, spot_scale / spots_total
    folded = jnp.zeros((spot.shape[0], 128), f32)
    at = 0
    low = 0
    for q in range(n):
        wide = widths[q]
        pred = pred_refs[q][...]
        other = other_refs[low // quarter]
        other_low = low % quarter
        target = in_order(core_ref[0], own_ref[:, low : low + wide], other[:, other_low : other_low + wide])
        cols = slice(at, at + 2 * wide)
        grad = pred * (gene_pred[:, cols] + spot_pred) - target * (gene_target[:, cols] + spot_target)
        grad_low = grad.astype(bf16)
        turned_ref[at : at + 2 * wide, :] = grad_low.T
        prod = grad_low.astype(f32) * pred
        for k in range(0, 2 * wide, 128):
            folded = folded + prod[:, k : k + 128]
        at += 2 * wide
        low += wide
    shift, density, counts = cols_ref[0:1, :], cols_ref[1:2, :], cols_ref[2:3, :]
    dens_total = gene_ref[0:1, at : at + 1]
    count_total = gene_ref[2:3, at : at + 1]
    dens_grad = -counts / (count_total * density) + 1.0 / dens_total
    col_ref[0:1, :] = shift
    col_ref[1:2, :] = dens_grad
    col_ref[2:3, :] = jnp.sum(folded.T, axis=0, keepdims=True) + density * dens_grad
    lane = lax.broadcasted_iota(jnp.int32, (1, 128), 1)
    gene_sum = jnp.sum(gene_cos, axis=1, keepdims=True)
    spot_sum = jnp.sum(spot_cos, axis=0, keepdims=True)
    sums_ref[...] = jnp.where(lane == 0, gene_sum, jnp.where(lane == 1, spot_sum, 0.0))


def grad_pred(core, widths, genes_total, spots_total, spot, gene, cols, target, others, preds):
    half = target.shape[1]
    spots = spot.shape[0]
    genes = 2 * half
    return pl.pallas_call(
        functools.partial(grad_pred_kernel, widths, genes_total, spots_total),
        grid_spec=pltpu.PrefetchScalarGridSpec(
            num_scalar_prefetch=1,
            grid=(1,),
            in_specs=[VMEM] * 3
            + [pl.BlockSpec((spots, half), lambda i, core: (core[0], 0))]
            + [VMEM] * (4 + len(preds)),
            out_specs=[VMEM] * 3,
        ),
        out_shape=[
            pltpu.VMEM((genes, spots), bf16),
            jax.ShapeDtypeStruct((3, spots), f32),
            jax.ShapeDtypeStruct((1, 128), f32),
        ],
        compiler_params=params(20),
        cost_estimate=cost(spots * genes * 14, spots * genes * 10),
        name="grad_pred",
    )(core, spot, gene, cols, target, *others, *preds)


def backward_kernel(widths, order_ref, logits_ref, enable_ref, retain_ref, col_ref, turned_ref, *refs):
    n = len(widths)
    panel_refs = refs[:n]
    grad_ref, row_ref = refs[n:]
    rows, spots = logits_ref.shape
    first = pl.multiple_of(pl.program_id(0) * rows, rows)
    enable = enable_ref[...].T
    retain = retain_ref[...].T
    shift, dens, inner = col_ref[0:1, :], col_ref[1:2, :], col_ref[2:3, :]
    part = rows // 2
    for h in range(2):
        here = pl.ds(first + h * part, part)
        near = slice(h * part, (h + 1) * part)
        panel = jnp.concatenate([ref[near if ref.shape[0] == rows else here, :] for ref in panel_refs], axis=1)
        grad_mapped = jnp.dot(panel, turned_ref[...], preferred_element_type=f32) + dens
        for k in range(part // 128):
            at = h * (part // 128) + k
            lines = slice(128 * at, 128 * (at + 1))
            block = jnp.where(enable[:, at : at + 1] > 0, logits_ref[lines, :], -1e30)
            mapping = jnp.exp(block - shift)
            grad = grad_mapped[128 * k : 128 * (k + 1), :]
            grad_ref[lines, :] = mapping * (retain[:, at : at + 1] * grad - inner)
            prod = grad * mapping
            folded = prod[:, 0:128]
            for c in range(128, spots, 128):
                folded = folded + prod[:, c : c + 128]
            row_ref[at : at + 1, :] = jnp.sum(folded.T, axis=0, keepdims=True)


def backward(order, logits, enable, retain, col, turned, panels):
    cells, spots = logits.shape
    genes = turned.shape[0]
    block = cells // PIECES
    widths = tuple(p.shape[1] for p in panels)
    streamed = (0,) + tuple(range(len(panels) - 2, len(panels)))
    cell = pl.BlockSpec((block // 128, 128), lambda i, order: (order[i], 0))
    return pl.pallas_call(
        functools.partial(backward_kernel, widths),
        grid_spec=pltpu.PrefetchScalarGridSpec(
            num_scalar_prefetch=1,
            grid=(PIECES,),
            in_specs=[
                pl.BlockSpec((block, spots), lambda i, order: (order[i], 0)),
                cell,
                cell,
                pl.BlockSpec((3, spots), lambda i, order: (0, 0)),
            ]
            + [VMEM]
            + [pl.BlockSpec((block, w), lambda i, order: (i, 0)) if q in streamed else VMEM for q, w in enumerate(widths)],
            out_specs=[pl.BlockSpec((block, spots), lambda i, order: (order[i], 0)), cell],
        ),
        out_shape=[
            jax.ShapeDtypeStruct((cells, spots), f32),
            jax.ShapeDtypeStruct((cells // 128, 128), f32),
        ],
        compiler_params=params(26),
        cost_estimate=cost(2 * cells * spots * genes, cells * 8 * spots, cells * spots),
        name="backward",
    )(order, logits, enable, retain, col, turned, *[in_hbm(p) if q in streamed else p for q, p in enumerate(panels)])


def final_kernel(genes_total, spots_total, cells_total, copies, sums_ref, gene_ref, count_ref, enable_ref, retain_ref, *refs):
    grad_ref, loss_ref = refs
    n = enable_ref.shape[0]
    last = gene_ref.shape[1] - 1
    offset = (count_ref[...] - 0.5 * cells_total) / cells_total
    penalty = jnp.sqrt(offset * offset + 0.01)
    retain = retain_ref[...]
    retain_grad = sums_ref[0:n, :] + enable_ref[...] * offset / (penalty * cells_total)
    grad_ref[...] = retain_grad * retain * (1.0 - retain)
    dens_total, kl_part, count_total = [gene_ref[k : k + 1, last : last + 1] for k in range(3)]
    kl_term = kl_part / count_total - jnp.log(count_total) + jnp.log(dens_total)
    gene_sum = sums_ref[n : n + 1, 0:1] / copies
    spot_sum = sums_ref[n : n + 1, 1:2]
    loss_ref[...] = -gene_sum / genes_total - spot_sum / spots_total + kl_term + penalty[:, 0:1]


def final(genes_total, spots_total, cells_total, copies, sums, gene, count, enable, retain):
    return pl.pallas_call(
        functools.partial(final_kernel, genes_total, spots_total, cells_total, copies),
        in_specs=[VMEM] * 5,
        out_specs=[VMEM] * 2,
        out_shape=[jax.ShapeDtypeStruct(enable.shape, f32), jax.ShapeDtypeStruct((1, 1), f32)],
        compiler_params=params(12),
        cost_estimate=cost(),
        name="final",
    )(sums, gene, count, enable, retain)


def join_kernel(*refs):
    at = 0
    for ref in refs[:-1]:
        refs[-1][at : at + ref.shape[0], :] = ref[...]
        at += ref.shape[0]


def join(*parts):
    rows = sum(p.shape[0] for p in parts)
    return pl.pallas_call(
        join_kernel,
        in_specs=[VMEM] * len(parts),
        out_specs=VMEM,
        out_shape=jax.ShapeDtypeStruct((rows, parts[0].shape[1]), bf16),
        compiler_params=params(12),
        cost_estimate=cost(0, 4 * rows * parts[0].shape[1]),
        name="join",
    )(*parts)


def select_kernel(inside_ref, b_ref, e_ref, c_ref, f_ref, *out_refs):
    rows = b_ref.shape[0]
    at = 0
    for out in out_refs:
        cols = slice(at, at + out.shape[1])
        at += out.shape[1]
        for flag, refs in ((1, (b_ref, c_ref)), (0, (e_ref, f_ref))):

            @pl.when(inside_ref[0] == flag)
            def _(out=out, refs=refs, cols=cols):
                out[0:rows, :] = refs[0][:, cols]
                out[rows : 2 * rows, :] = refs[1][:, cols]
                if out.shape[0] > 2 * rows:
                    out[2 * rows :, :] = jnp.zeros_like(out[2 * rows :, :])


def select(inside, b, e, c, f, widths, pad):
    rows = b.shape[0]
    return pl.pallas_call(
        select_kernel,
        in_specs=[pl.BlockSpec(memory_space=pltpu.SMEM)] + [VMEM] * 4,
        out_specs=[VMEM] * len(widths),
        out_shape=[jax.ShapeDtypeStruct((2 * rows + pad * k, wide), bf16) for k, wide in enumerate(widths)],
        compiler_params=params(12),
        cost_estimate=cost(),
        name="select",
    )(inside, b, e, c, f)


def share_kernel(places, core_ref, *refs):
    kept_ref, sent_ref = refs[-2:]
    first = core_ref[0] == 0
    n = len(places)
    at = 0
    for ref, place in zip(refs, places):
        pred = ref[...]
        wide = pred.shape[1] // 2
        if place is not None:
            left = [x[:, place : place + 2 * wide].astype(f32) for x in refs[n : n + 2]]
            pred = pred + (left[0] + left[1])
        kept_ref[:, at : at + wide] = jnp.where(first, pred[:, :wide], pred[:, wide:])
        sent_ref[:, at : at + wide] = jnp.where(first, pred[:, wide:], pred[:, :wide])
        at += wide


def share(core, preds, left, places):
    spots = preds[0].shape[0]
    wide = sum(p.shape[1] // 2 for p in preds)
    arrays = [*preds, *left]
    return pl.pallas_call(
        functools.partial(share_kernel, places),
        in_specs=[pl.BlockSpec(memory_space=pltpu.SMEM)] + [pl.BlockSpec()] * len(arrays),
        out_specs=[VMEM] * 2,
        out_shape=[jax.ShapeDtypeStruct((spots, wide), f32)] * 2,
        compiler_params=params(24),
        cost_estimate=cost(),
        name="share",
    )(core, *[in_hbm(x) for x in arrays])


def lay_kernel(core_ref, kept_ref, theirs_ref, *refs):
    mine = pl.program_id(0) == core_ref[0]

    @pl.when(mine)
    def _():
        refs[-1][...] = kept_ref[...]

    @pl.when(jnp.logical_not(mine))
    def _():
        refs[-1][...] = theirs_ref[...]


def lay(core, kept, theirs, half, column, begun=None):
    spots, wide = kept.shape
    part = pl.BlockSpec((spots, wide), lambda i, core: (0, 0))
    return pl.pallas_call(
        lay_kernel,
        grid_spec=pltpu.PrefetchScalarGridSpec(
            num_scalar_prefetch=1,
            grid=(2,),
            in_specs=[part, part] + ([] if begun is None else [pl.BlockSpec(memory_space=pl.ANY)]),
            out_specs=pl.BlockSpec((spots, wide), lambda i, core: (i, column)),
        ),
        out_shape=jax.ShapeDtypeStruct((2 * spots, half), f32),
        input_output_aliases={} if begun is None else {3: 0},
        compiler_params=params(16),
        cost_estimate=cost(),
        name="lay",
    )(core, kept, theirs, *(() if begun is None else (begun,)))


def swap_cells(x):
    return lax.ppermute(x, "cells", [(0, 1), (1, 0)])


def swap_genes(x):
    return lax.ppermute(x, "genes", [(0, 1), (1, 0)])


def sum_spots_genes(x, first=(), second=lambda *_: ()):
    if lax.axis_size("spots") != 8:
        return lax.psum(x, ("spots", "genes")), second(*first)
    moved = [lax.ppermute(x, "spots", [(i, i ^ d) for i in range(8)]) for d in (2, 4, 6)]
    moved[0], moved[1], moved[2], *first = hold(*moved, *first)
    x = (x + moved[0]) + (moved[1] + moved[2])
    pairs = [lax.ppermute(x, ("spots", "genes"), [(i, i ^ d) for i in range(16)]) for d in (1, 2, 3)]
    pairs[0], pairs[1], pairs[2], *more = hold(*pairs, *second(*first))
    return (x + pairs[0]) + (pairs[1] + pairs[2]), more


class Step:
    def __init__(self, logits, filter_logits, expression, spot_expression, cell_mask, spot_counts):
        self.logits = pltpu.with_memory_space_constraint(logits, pltpu.HBM)
        self.expression = expression
        self.core = lax.axis_index("genes")
        self.enable = cell_mask.astype(f32).reshape(-1, 128)
        self.retain = jax.nn.sigmoid(filter_logits).reshape(-1, 128)
        self.spots = logits.shape[1]
        self.counts = spot_counts.astype(f32)[None, :]
        self.core_flag = self.core.astype(jnp.int32).reshape(1)
        self.half = expression.shape[1]
        self.target = spot_expression
        sent = lax.dynamic_slice_in_dim(spot_expression, (1 - self.core) * self.spots, self.spots, 0)
        quarter = self.half // 4
        self.target_sent = [sent[:, k * quarter : (k + 1) * quarter] for k in range(4)]

    def local_stats(self):
        part = col_stats(self.logits, self.enable, self.retain)
        count = jnp.broadcast_to(jnp.sum(self.enable * self.retain), (1, self.spots))
        return jnp.concatenate([part, count], axis=0)

    def merge_stats(self, part, away):
        top = jnp.maximum(part[0], away[0])
        here, there = jnp.exp(part[0] - top), jnp.exp(away[0] - top)
        total = part[1] * here + away[1] * there
        density = (part[2] * here + away[2] * there) / total
        self.density = density[None, :]
        self.cell_count = part[3:4, :128] + away[3:4, :128]
        self.shift = (top + jnp.log(total))[None, :]
        counts = self.counts[0]
        kl_parts = (jnp.sum(density), jnp.sum(counts * (jnp.log(counts) - jnp.log(density))), jnp.sum(counts))
        self.kl_parts = jnp.broadcast_to(jnp.stack(kl_parts)[:, None], (3, 128))

    def turned(self, order, shift, logits):
        return mapped_turned(order, logits, self.enable, self.retain, shift)

    def stats(self, parts, other, at, wide, part=0):
        column = at % (self.half // 4) // wide
        return pred_stats(self.core_flag, parts, self.target, other, at // wide, column, wide, part)

    def gathered_whole(self):
        own = lax.all_gather(self.expression, "spots", axis=0, tiled=True)
        other = swap_genes(own)
        part = self.local_stats()
        self.target_other = [swap_genes(x) for x in self.target_sent]
        self.merge_stats(part, swap_cells(part))
        order = jnp.arange(PIECES, dtype=jnp.int32)
        mapped = self.turned(order, self.shift, self.logits)
        wide = self.half // 4
        widths, panels, stats = (wide,) * 4, [], []
        for q in range(4):
            pieces = tuple((r, 0, r, q) for r in range(PIECES))
            (partial,), (panel,) = forward(self.core_flag, mapped, [(own, other)], [pieces], wide)
            panels.append(panel)
            stats.append(self.stats([lax.psum(partial, "cells")], self.target_other[q], q * wide, wide))
        return order, widths, panels, stats, (), None

    def gathered_line(self):
        near_pairs = [(2 * z + y, 2 * (z ^ 1) + y) for z in range(4) for y in range(2)]
        middle_pairs = [(2 * z + y, 2 * (3 - z) + y) for z in (1, 2) for y in range(2)]
        across_pairs = [(i, i ^ 1) for i in range(8)]

        def near(x):
            return lax.ppermute(x, "spots", near_pairs)

        def middle(x):
            return lax.ppermute(x, "spots", middle_pairs)

        def across(x):
            return lax.ppermute(x, "spots", across_pairs)

        spot = lax.axis_index("spots")
        z, y = spot // 2, spot % 2
        inside = (z == 1) | (z == 2)
        inside_flag = inside.astype(jnp.int32).reshape(1)
        column = jnp.stack([z, z ^ 1, jnp.where(z < 2, 2, 1), jnp.where(z < 2, 3, 0)])
        order = jnp.concatenate([2 * column + y, 2 * column + (1 - y)]).astype(jnp.int32)
        unit = self.half // 8
        expr = self.expression

        def cut(x, at, wide):
            return x[:, at * unit : (at + wide) * unit]

        def pick(b, e, c, f, *widths, pad=0):
            return select(inside_flag, b, e, c, f, [wide * unit for wide in widths], pad)

        core = self.core_flag

        def run(sources, chunks, wide, begun=None, near=False, column=None, columns=0, left=None):
            columns = (None if column is None else 2 * column * unit), 2 * columns * unit
            return forward(core, mapped, sources, chunks, wide * unit, begun, near, *columns, left)

        def whole(c, d):
            return ((0, 0, 0, c), (1, 1, 0, d), (2, 2, 0, 0), (3, 2, 1, 0), (4, 3, 0, c), (5, 4, 0, d), (6, 5, 0, 0), (7, 5, 1, 0))

        s01 = cut(expr, 0, 4)
        beside = across(expr)
        a01 = near(s01)
        b01 = middle(s01)
        expr_o = swap_genes(expr)
        target_0 = swap_genes(self.target_sent[0])
        part = self.local_stats()
        a01, b01, part, target_0, sv, target_1 = hold(
            a01, b01, part, target_0, cut(expr, 4, 3), self.target_sent[1]
        )
        c01 = middle(a01)
        e01 = near(b01)
        away = swap_cells(part)
        target_1 = swap_genes(target_1)
        self.merge_stats(part, away)
        mapped = self.turned(order, self.shift, self.logits)
        beside, e01, c01, expr_o, mapped, a01, sv, target_1 = hold(
            beside, e01, c01, expr_o, mapped, a01, sv, target_1
        )
        yn = across(a01)
        f01 = near(c01)
        beside_o = swap_genes(beside)
        a01_o = swap_genes(a01)
        bv = middle(sv)
        mf0, mf1 = pick(b01, e01, c01, f01, 2, 2)
        yn, mf0, mf1, a01_o, sv, bv, beside, self.kl_parts = hold(
            yn, mf0, mf1, a01_o, sv, bv, beside, self.kl_parts
        )
        ymf0 = across(mf0)
        av = near(sv)
        mf0_o, yn_o = swap_genes(mf0), swap_genes(yn)
        sf = join(cut(expr, 7, 1), cut(beside, 7, 1))
        expr_2, a01_2, beside_2, yn_2 = (expr, expr_o), (a01, a01_o), (beside, beside_o), (yn, yn_o)
        begun = run([expr_2, beside_2], [((0, 0, 0, q), (4, 1, 0, q)) for q in range(4, 8)], 1)
        ymf0, av, mf0_o, yn_o, mf1, bv, mapped, *begun = hold(
            ymf0, av, mf0_o, yn_o, mf1, bv, mapped, *begun[0], *begun[1]
        )
        ymf1 = across(mf1)
        ev = near(bv)
        cv = middle(av)
        ymf0_o, mf1_o = swap_genes(ymf0), swap_genes(mf1)
        (high0, low0), (panel0,) = run(
            [expr_2, a01_2, (mf0, mf0_o), beside_2, yn_2, (ymf0, ymf0_o)], [whole(0, 0)], 2, column=0, columns=2
        )
        ymf1, ev, cv, high0, mf1_o, av, mapped = hold(ymf1, ev, cv, high0, mf1_o, av, mapped)
        ynv = across(av)
        fv = near(cv)
        ymf1_o = swap_genes(ymf1)
        high0_away = swap_cells(high0)
        av_o = swap_genes(av)
        (partial1,), (panel1,) = run([expr_2, a01_2, (mf1, mf1_o), beside_2, yn_2, (ymf1, ymf1_o)], [whole(1, 1)], 2)
        ynv, fv, partial1, high0_away, av_o, sf, mapped = hold(ynv, fv, partial1, high0_away, av_o, sf, mapped)
        m2, m34 = pick(bv, ev, cv, fv, 1, 2, pad=16)
        ym2 = across(m2)
        af, bf = near(sf), middle(sf)
        away1 = swap_cells(partial1)
        ynv_o = swap_genes(ynv)
        more = run(
            [(av, av_o), (ynv, ynv_o)], [((1, 0, 0, q), (5, 1, 0, q)) for q in range(3)], 1, (begun[0:3], begun[4:7])
        )
        ym2, m2, m34, mapped, *more = hold(ym2, m2, m34, mapped, *more[0], *more[1])
        ym34 = across(m34)
        ym2_o, m2_o = swap_genes(ym2), swap_genes(m2)
        af, bf = hold(af, bf)
        cf = middle(af)

        def rest(column):
            return ((2, 0, 0, column), (3, 0, 1, column), (6, 1, 0, column), (7, 1, 1, column))

        (high2, low), (panel2,) = run(
            [(m2, m2_o), (ym2, ym2_o)], [rest(0)], 1, (more[0:1], more[3:4]), near=True, column=0, columns=4
        )
        stats0 = self.stats([high0, high0_away], target_0, 0, 2 * unit)
        cf, high2, away1, m34, bf, af, target_2, *stats0 = hold(
            cf, high2, away1, m34, bf, af, self.target_sent[2], *stats0
        )
        target_2 = swap_genes(target_2)
        ef, ff = near(bf), near(cf)
        m34_o = swap_genes(m34)
        high2_away = swap_cells(high2)
        stats1 = self.stats([partial1, away1], target_1, 2 * unit, 2 * unit)
        ym34, ef, m34, mapped, high2_away, af, low0, target_2, target_3, *stats1 = hold(
            ym34, ef, m34, mapped, high2_away, af, low0, target_2, self.target_sent[3], *stats1
        )
        ym34_o, af_o = swap_genes(ym34), swap_genes(af)
        low0_away = swap_cells(low0)
        target_3 = swap_genes(target_3)
        self.target_other = (target_0, target_1, target_2, target_3)
        (high34, low), (panel3, panel4) = run(
            [(m34, m34_o), (ym34, ym34_o)],
            [rest(0), rest(1)],
            1,
            (more[1:3], more[4:6]),
            column=1,
            columns=4,
            left=low,
        )
        ff, high34, low0_away, target_3, af_o, mapped = hold(ff, high34, low0_away, target_3, af_o, mapped)
        high34_away = swap_cells(high34)
        (mff,) = pick(bf, ef, cf, ff, 1)
        mff_o = swap_genes(mff)
        late = ((1, 0, 0, 0), (2, 1, 0, 0), (3, 1, 2, 0), (5, 0, 1, 0), (6, 1, 1, 0), (7, 1, 3, 0))
        (highf, low), (panelf,) = run(
            [(af, af_o), (mff, mff_o)], [late], 1, (begun[3:4], begun[7:8]), column=3, columns=4, left=low, near=True
        )
        highf, high2, high2_away = hold(highf, high2, high2_away)
        highf_away = swap_cells(highf)
        high34, high34_away, highf = hold(high34, high34_away, highf)
        late = [
            self.stats([high2, high2_away], target_2, 4 * unit, unit),
            self.stats([high34, high34_away], target_2, 5 * unit, unit),
            self.stats([high34, high34_away], target_3, 6 * unit, unit, 1),
            self.stats([highf, highf_away], target_3, 7 * unit, unit),
        ]
        widths = (2 * unit,) * 2 + (unit,) * 4
        panels = (panel0, panel1, panel2, panel3, panel4, panelf)
        return order, widths, panels, [stats0, stats1, *late], (low0, low0_away), low


def body(logits, filter_logits, expression, spot_expression, cell_mask, spot_counts):
    cells_total = logits.shape[0] * lax.axis_size("cells")
    spots = logits.shape[1]
    spots_total = spots * lax.axis_size("spots") * lax.axis_size("genes")
    genes_total = expression.shape[1] * lax.axis_size("genes")
    step = Step(logits, filter_logits, expression, spot_expression, cell_mask, spot_counts)
    gathered = step.gathered_line() if lax.axis_size("spots") == 8 else step.gathered_whole()
    order, widths, panels, stats, left, late_left = gathered
    gene_stats, preds, spot_stats = zip(*stats)
    split = 2
    gene, (kept, sent) = sum_spots_genes(
        jnp.concatenate([*gene_stats, step.kl_parts], axis=1),
        preds[:split],
        lambda *first: share(step.core_flag, first, left, [0, None] if left else [None] * split),
    )
    spot = functools.reduce(jnp.add, spot_stats)
    cols = jnp.concatenate([step.shift, step.density, step.counts], axis=0)
    turned, col, sums = grad_pred(
        step.core_flag, widths, genes_total, spots_total, spot, gene, cols, step.target, step.target_other, preds
    )
    left, places = [], [None] * (len(widths) - split)
    if late_left is not None:
        turned, late_left = hold(turned, late_left)
        left, places = [late_left, swap_cells(late_left)], [2 * sum(widths[split:q]) for q in range(split, len(widths))]
    turned, sent = hold(turned, sent)
    theirs = swap_genes(sent)
    grad_logits, row = backward(order, step.logits, step.enable, step.retain, col, turned, panels)

    row, core, theirs, *left = hold(row, step.core_flag, theirs, *left)
    half = expression.shape[1]

    def lay_both(late_kept, late_sent):
        predicted = lay(core, kept, theirs, half, 0)
        return (lay(core, late_kept, swap_genes(late_sent), half, 1, predicted),)

    row_sums, (predicted,) = sum_spots_genes(jnp.concatenate([row, sums], axis=0), share(core, preds[split:], left, places), lay_both)
    copies = lax.axis_size("spots") * lax.axis_size("genes")
    filter_grad, total_loss = final(
        genes_total, spots_total, cells_total, copies, row_sums, gene, step.cell_count, step.enable, step.retain
    )
    return (predicted, total_loss.reshape(()), grad_logits, filter_grad.reshape(-1))


def solution(mesh):
    placed = (
        P("cells", ("spots", "genes")),
        P("cells"),
        P(("cells", "spots"), "genes"),
        P("spots", "genes"),
        P("cells"),
        P(("spots", "genes")),
    )
    return jax.shard_map(
        body,
        mesh=mesh,
        in_specs=placed,
        out_specs=(P("spots", "genes"), P(), P("cells", ("spots", "genes")), P("cells")),
        check_vma=False,
    )
```

```python
import functools

import jax
import jax.numpy as jnp
from jax import lax
from jax.experimental import pallas as pl
from jax.experimental.pallas import tpu as pltpu
from jax.sharding import PartitionSpec as P

epsilon = 1e-06
bf16 = jnp.bfloat16
f32 = jnp.float32
PIECES = 8
MIB = 1024 * 1024
VMEM = pl.BlockSpec(memory_space=pltpu.VMEM)


def params(limit):
    return pltpu.CompilerParams(vmem_limit_bytes=limit * MIB)


def cost(flops=0, bytes_accessed=0, transcendentals=0):
    return pl.CostEstimate(flops=1, bytes_accessed=1, transcendentals=0)


def in_hbm(x):
    return pltpu.with_memory_space_constraint(x, pltpu.HBM)


def hold(*values):
    return lax.optimization_barrier(values)


def col_stats_kernel(logits_ref, enable_ref, retain_ref, out_ref, top, total, dens):
    step = pl.program_id(0)

    @pl.when(step == 0)
    def _():
        top[...] = jnp.full_like(top, -1e29)
        total[...] = jnp.zeros_like(total)
        dens[...] = jnp.zeros_like(dens)

    rows, spots = logits_ref.shape
    enable = enable_ref[...].T
    retain = retain_ref[...].T
    blocks = []
    new = top[...]
    for k in range(rows // 128):
        block = jnp.where(enable[:, k : k + 1] > 0, logits_ref[128 * k : 128 * (k + 1), :], -1e30)
        blocks.append(block.reshape(16, 8, spots))
        new = jnp.maximum(new, jnp.max(blocks[-1], axis=0))
    shrink = jnp.exp(top[...] - new)
    top[...] = new
    sums = total[...] * shrink
    kept = dens[...] * shrink
    for k in range(rows // 128):
        part = jnp.exp(blocks[k] - new[None])
        share = jnp.broadcast_to(retain[:, k : k + 1], (128, spots)).reshape(16, 8, spots)
        sums = sums + jnp.sum(part, axis=0)
        kept = kept + jnp.sum(part * share, axis=0)
    total[...] = sums
    dens[...] = kept

    @pl.when(step == pl.num_programs(0) - 1)
    def _():
        best = jnp.max(new, axis=0, keepdims=True)
        scale = jnp.exp(new - best)
        out_ref[0:1, :] = best
        out_ref[1:2, :] = jnp.sum(sums * scale, axis=0, keepdims=True)
        out_ref[2:3, :] = jnp.sum(kept * scale, axis=0, keepdims=True)


def col_stats(logits, enable, retain, block=1024):
    cells, spots = logits.shape
    cell = pl.BlockSpec((block // 128, 128), lambda i: (i, 0))
    return pl.pallas_call(
        col_stats_kernel,
        grid=(cells // block,),
        in_specs=[pl.BlockSpec((block, spots), lambda i: (i, 0)), cell, cell],
        out_specs=pl.BlockSpec((3, spots), lambda i: (0, 0)),
        out_shape=jax.ShapeDtypeStruct((3, spots), f32),
        scratch_shapes=[pltpu.VMEM((8, spots), f32)] * 3,
        compiler_params=params(20),
        cost_estimate=cost(cells * spots * 8, cells * spots * 4, cells * spots),
        name="col_stats",
    )(logits, enable, retain)


def mapped_kernel(order_ref, logits_ref, enable_ref, retain_ref, shift_ref, out_ref):
    rows, spots = logits_ref.shape
    enable = enable_ref[...].T
    retain = retain_ref[...].T
    shift = shift_ref[...]
    for k in range(rows // 128):
        block = jnp.where(enable[:, k : k + 1] > 0, logits_ref[128 * k : 128 * (k + 1), :], -1e30)
        mapped = retain[:, k : k + 1] * jnp.exp(block - shift)
        out_ref[:, 128 * k : 128 * (k + 1)] = mapped.astype(bf16).T


def mapped_turned(order, logits, enable, retain, shift):
    cells, spots = logits.shape
    block = cells // PIECES
    cell = pl.BlockSpec((block // 128, 128), lambda i, order: (order[i], 0))
    return pl.pallas_call(
        mapped_kernel,
        grid_spec=pltpu.PrefetchScalarGridSpec(
            num_scalar_prefetch=1,
            grid=(PIECES,),
            in_specs=[
                pl.BlockSpec((block, spots), lambda i, order: (order[i], 0)),
                cell,
                cell,
                pl.BlockSpec((1, spots), lambda i, order: (0, 0)),
            ],
            out_specs=pl.BlockSpec((spots, block), lambda i, order: (0, i)),
        ),
        out_shape=pltpu.HBM((spots, cells), bf16),
        compiler_params=params(20),
        cost_estimate=cost(cells * spots * 6, cells * spots * 6, cells * spots),
        name="mapped_turned",
    )(order, logits, enable, retain, shift)


def forward_kernel(chunks, count, rows, wide, more, column, core_ref, mapped_ref, *refs):
    n = len(chunks)
    sources = (refs[:count], refs[count : 2 * count])
    refs = refs[2 * count :]
    totals = [None] * n
    if "begun" in more:
        totals = [ref[...] for ref in refs[:n]]
        refs = refs[2 * n :]
    if "left" in more:
        refs = refs[1:]
    outs = n if column is None else 2
    pred_refs, refs = refs[:outs], refs[outs:]
    panel_refs, held = refs[:n], refs[n : 2 * n]
    turned, own_sems, other_sems, mapped_sems, panel_sems = refs[2 * n : 2 * n + 5]
    used = sorted({piece[0] for pieces in chunks for piece in pieces})

    def fetch(q, k, which, place):
        r, source, block, col = chunks[q][k]
        part = sources[which][source].at[pl.ds(block * rows, rows), pl.ds(col * wide, wide)]
        target = held[q].at[pl.ds(k * rows, rows), pl.ds(place, wide)]
        return pltpu.make_async_copy(part, target, (own_sems, other_sems)[which].at[q, k])

    def load(r):
        at = used.index(r) * rows
        return pltpu.make_async_copy(
            mapped_ref.at[:, pl.ds(r * rows, rows)], turned.at[:, pl.ds(at, rows)], mapped_sems.at[r]
        )

    def save(q, k):
        target = panel_refs[q].at[pl.ds(chunks[q][k][0] * rows, rows), :]
        return pltpu.make_async_copy(held[q].at[pl.ds(k * rows, rows), :], target, panel_sems.at[q, k])

    steps = [[(q, k) for q in range(n) for k in range(len(chunks[q])) if chunks[q][k][0] == r] for r in used]
    for r, step in zip(used, steps):
        for q, k in step:
            for core in range(2):

                @pl.when(core_ref[0] == core)
                def _(core=core, q=q, k=k):
                    fetch(q, k, 0, core * wide).start()
                    fetch(q, k, 1, (1 - core) * wide).start()

        load(r).start()
    for at, (r, step) in enumerate(zip(used, steps)):
        load(r).wait()
        for q, k in step:
            fetch(q, k, 0, 0).wait()
            fetch(q, k, 1, 0).wait()
            save(q, k).start()
            part = jnp.dot(
                turned[:, at * rows : (at + 1) * rows],
                held[q][k * rows : (k + 1) * rows, :],
                preferred_element_type=f32,
            )
            totals[q] = part if totals[q] is None else totals[q] + part
    if column is None:
        for q in range(n):
            pred_refs[q][...] = totals[q]
    else:
        left, left_sem = refs[-2:]
        for q in range(n):
            high = totals[q].astype(bf16)
            cols = slice(2 * q * wide, 2 * (q + 1) * wide)
            pred_refs[0][:, cols] = high
            left[:, cols] = (totals[q] - high.astype(f32)).astype(bf16)
        copy = pltpu.make_async_copy(left, pred_refs[1].at[:, pl.ds(column, 2 * n * wide)], left_sem.at[0])
        copy.start()
        copy.wait()
    for step in steps:
        for q, k in step:
            save(q, k).wait()


def forward(core, mapped, sources, chunks, wide, begun=None, near=False, column=None, columns=0, left=None):
    spots, cells = mapped.shape
    rows = cells // PIECES
    own, other = zip(*sources)
    n = len(chunks)
    hbm = pl.BlockSpec(memory_space=pltpu.HBM)
    used = {piece[0] for pieces in chunks for piece in pieces}
    longest = max(len(pieces) for pieces in chunks)
    outs = n if column is None else 2
    arrays = [x if near else in_hbm(x) for x in own + other]
    specs = [VMEM if near else hbm] * len(arrays)
    aliases = {}
    if begun is not None:
        aliases = {2 + len(arrays) + n + q: outs + q for q in range(n)}
        arrays += [*begun[0], *begun[1]]
        specs += [VMEM] * n + [hbm] * n
    if left is not None:
        aliases[2 + len(arrays)] = 1
        arrays.append(left)
        specs.append(hbm)
    more = ("begun",) * (begun is not None) + ("left",) * (left is not None)
    results = pl.pallas_call(
        functools.partial(forward_kernel, chunks, len(own), rows, wide, more, column),
        in_specs=[pl.BlockSpec(memory_space=pltpu.SMEM), hbm] + specs,
        out_specs=([VMEM] * n if column is None else [VMEM, hbm]) + [hbm] * n,
        out_shape=(
            [jax.ShapeDtypeStruct((spots, 2 * wide), f32)] * n
            if column is None
            else [jax.ShapeDtypeStruct((spots, 2 * n * wide), bf16), pltpu.HBM((spots, columns), bf16)]
        )
        + [pltpu.HBM((cells, 2 * wide), bf16)] * n,
        scratch_shapes=[pltpu.VMEM((len(pieces) * rows, 2 * wide), bf16) for pieces in chunks]
        + [pltpu.VMEM((spots, len(used) * rows), bf16)]
        + [pltpu.SemaphoreType.DMA((n, longest))] * 2
        + [pltpu.SemaphoreType.DMA((PIECES,)), pltpu.SemaphoreType.DMA((n, longest))]
        + ([] if column is None else [pltpu.VMEM((spots, 2 * n * wide), bf16), pltpu.SemaphoreType.DMA((1,))]),
        input_output_aliases=aliases,
        compiler_params=params(22),
        cost_estimate=cost(),
        name="forward",
    )(core, in_hbm(mapped), *arrays)
    return results[:outs], results[outs:]


def in_order(core, own, other):
    first = core == 0
    return jnp.concatenate([jnp.where(first, own, other), jnp.where(first, other, own)], axis=1)


def total_of(refs):
    return functools.reduce(jnp.add, [ref[...].astype(f32) for ref in refs])


def stats_kernel(parts, core_ref, *refs):
    own_ref, other_ref, gene_ref, pred_ref, spot_ref = refs[parts:]
    pred = total_of(refs[:parts])
    pred_ref[...] = pred
    target = in_order(core_ref[0], own_ref[...], other_ref[...])
    lane = lax.broadcasted_iota(jnp.int32, spot_ref.shape, 1)
    spot = jnp.zeros(spot_ref.shape, f32)
    for k, term in enumerate((pred * target, pred * pred, target * target)):
        gene_ref[k : k + 1, :] = jnp.sum(term, axis=0, keepdims=True)
        spot = jnp.where(lane == k, jnp.sum(term, axis=1, keepdims=True), spot)
    spot_ref[...] = spot


def pred_stats(core, parts, target, other, column, other_column, wide, part=0):
    spots = parts[0].shape[0]
    whole = pl.BlockSpec((spots, 2 * wide), lambda i, core: (0, 0))
    return pl.pallas_call(
        functools.partial(stats_kernel, len(parts)),
        grid_spec=pltpu.PrefetchScalarGridSpec(
            num_scalar_prefetch=1,
            grid=(1,),
            in_specs=[pl.BlockSpec((spots, 2 * wide), lambda i, core: (0, part))] * len(parts)
            + [
                pl.BlockSpec((spots, wide), lambda i, core: (core[0], column)),
                pl.BlockSpec((spots, wide), lambda i, core: (0, other_column)),
            ],
            out_specs=[
                pl.BlockSpec((3, 2 * wide), lambda i, core: (0, 0)),
                whole,
                pl.BlockSpec((spots, 4), lambda i, core: (0, 0)),
            ],
        ),
        out_shape=[
            jax.ShapeDtypeStruct((3, 2 * wide), f32),
            jax.ShapeDtypeStruct((spots, 2 * wide), f32),
            jax.ShapeDtypeStruct((spots, 4), f32),
        ],
        compiler_params=params(16),
        cost_estimate=cost(),
        name="pred_stats",
    )(core, *parts, target, other)


def grad_pred_kernel(widths, genes_total, spots_total, core_ref, spot_ref, gene_ref, cols_ref, own_ref, *refs):
    n = len(widths)
    other_refs, pred_refs = refs[:4], refs[4 : 4 + n]
    refs = refs[4:]
    quarter = other_refs[0].shape[1]
    turned_ref, col_ref, sums_ref = refs[n:]
    spot = spot_ref[...]
    spot_pg, spot_pp, spot_gg = spot[:, 0:1], spot[:, 1:2], spot[:, 2:3]
    spot_scale = lax.rsqrt(spot_pp + epsilon) * lax.rsqrt(spot_gg + epsilon)
    spot_cos = spot_pg * spot_scale
    spot_back = spot_cos / (spot_pp + epsilon)
    gene = gene_ref[:, : 2 * sum(widths)]
    gene_scale = lax.rsqrt(gene[1:2, :] + epsilon) * lax.rsqrt(gene[2:3, :] + epsilon)
    gene_cos = gene[0:1, :] * gene_scale
    gene_back = gene_cos / (gene[1:2, :] + epsilon)
    gene_pred, gene_target = gene_back / genes_total, gene_scale / genes_total
    spot_pred, spot_target = spot_back / spots_total, spot_scale / spots_total
    folded = jnp.zeros((spot.shape[0], 128), f32)
    at = 0
    low = 0
    for q in range(n):
        wide = widths[q]
        pred = pred_refs[q][...]
        other = other_refs[low // quarter]
        other_low = low % quarter
        target = in_order(core_ref[0], own_ref[:, low : low + wide], other[:, other_low : other_low + wide])
        cols = slice(at, at + 2 * wide)
        grad = pred * (gene_pred[:, cols] + spot_pred) - target * (gene_target[:, cols] + spot_target)
        grad_low = grad.astype(bf16)
        turned_ref[at : at + 2 * wide, :] = grad_low.T
        prod = grad_low.astype(f32) * pred
        for k in range(0, 2 * wide, 128):
            folded = folded + prod[:, k : k + 128]
        at += 2 * wide
        low += wide
    shift, density, counts = cols_ref[0:1, :], cols_ref[1:2, :], cols_ref[2:3, :]
    dens_total = gene_ref[0:1, at : at + 1]
    count_total = gene_ref[2:3, at : at + 1]
    dens_grad = -counts / (count_total * density) + 1.0 / dens_total
    col_ref[0:1, :] = shift
    col_ref[1:2, :] = dens_grad
    col_ref[2:3, :] = jnp.sum(folded.T, axis=0, keepdims=True) + density * dens_grad
    lane = lax.broadcasted_iota(jnp.int32, (1, 128), 1)
    gene_sum = jnp.sum(gene_cos, axis=1, keepdims=True)
    spot_sum = jnp.sum(spot_cos, axis=0, keepdims=True)
    sums_ref[...] = jnp.where(lane == 0, gene_sum, jnp.where(lane == 1, spot_sum, 0.0))


def grad_pred(core, widths, genes_total, spots_total, spot, gene, cols, target, others, preds):
    half = target.shape[1]
    spots = spot.shape[0]
    genes = 2 * half
    return pl.pallas_call(
        functools.partial(grad_pred_kernel, widths, genes_total, spots_total),
        grid_spec=pltpu.PrefetchScalarGridSpec(
            num_scalar_prefetch=1,
            grid=(1,),
            in_specs=[VMEM] * 3
            + [pl.BlockSpec((spots, half), lambda i, core: (core[0], 0))]
            + [VMEM] * (4 + len(preds)),
            out_specs=[VMEM] * 3,
        ),
        out_shape=[
            pltpu.VMEM((genes, spots), bf16),
            jax.ShapeDtypeStruct((3, spots), f32),
            jax.ShapeDtypeStruct((1, 128), f32),
        ],
        compiler_params=params(20),
        cost_estimate=cost(spots * genes * 14, spots * genes * 10),
        name="grad_pred",
    )(core, spot, gene, cols, target, *others, *preds)


def backward_kernel(widths, order_ref, logits_ref, enable_ref, retain_ref, col_ref, turned_ref, *refs):
    n = len(widths)
    panel_refs = refs[:n]
    grad_ref, row_ref = refs[n:]
    rows, spots = logits_ref.shape
    first = pl.multiple_of(pl.program_id(0) * rows, rows)
    enable = enable_ref[...].T
    retain = retain_ref[...].T
    shift, dens, inner = col_ref[0:1, :], col_ref[1:2, :], col_ref[2:3, :]
    part = rows // 2
    for h in range(2):
        here = pl.ds(first + h * part, part)
        near = slice(h * part, (h + 1) * part)
        panel = jnp.concatenate([ref[near if ref.shape[0] == rows else here, :] for ref in panel_refs], axis=1)
        grad_mapped = jnp.dot(panel, turned_ref[...], preferred_element_type=f32) + dens
        for k in range(part // 128):
            at = h * (part // 128) + k
            lines = slice(128 * at, 128 * (at + 1))
            block = jnp.where(enable[:, at : at + 1] > 0, logits_ref[lines, :], -1e30)
            mapping = jnp.exp(block - shift)
            grad = grad_mapped[128 * k : 128 * (k + 1), :]
            grad_ref[lines, :] = mapping * (retain[:, at : at + 1] * grad - inner)
            prod = grad * mapping
            folded = prod[:, 0:128]
            for c in range(128, spots, 128):
                folded = folded + prod[:, c : c + 128]
            row_ref[at : at + 1, :] = jnp.sum(folded.T, axis=0, keepdims=True)


def backward(order, logits, enable, retain, col, turned, panels):
    cells, spots = logits.shape
    genes = turned.shape[0]
    block = cells // PIECES
    widths = tuple(p.shape[1] for p in panels)
    streamed = (0,) + tuple(range(len(panels) - 2, len(panels)))
    cell = pl.BlockSpec((block // 128, 128), lambda i, order: (order[i], 0))
    return pl.pallas_call(
        functools.partial(backward_kernel, widths),
        grid_spec=pltpu.PrefetchScalarGridSpec(
            num_scalar_prefetch=1,
            grid=(PIECES,),
            in_specs=[
                pl.BlockSpec((block, spots), lambda i, order: (order[i], 0)),
                cell,
                cell,
                pl.BlockSpec((3, spots), lambda i, order: (0, 0)),
            ]
            + [VMEM]
            + [pl.BlockSpec((block, w), lambda i, order: (i, 0)) if q in streamed else VMEM for q, w in enumerate(widths)],
            out_specs=[pl.BlockSpec((block, spots), lambda i, order: (order[i], 0)), cell],
        ),
        out_shape=[
            jax.ShapeDtypeStruct((cells, spots), f32),
            jax.ShapeDtypeStruct((cells // 128, 128), f32),
        ],
        compiler_params=params(26),
        cost_estimate=cost(2 * cells * spots * genes, cells * 8 * spots, cells * spots),
        name="backward",
    )(order, logits, enable, retain, col, turned, *[in_hbm(p) if q in streamed else p for q, p in enumerate(panels)])


def final_kernel(genes_total, spots_total, cells_total, copies, sums_ref, gene_ref, count_ref, enable_ref, retain_ref, *refs):
    grad_ref, loss_ref = refs
    n = enable_ref.shape[0]
    last = gene_ref.shape[1] - 1
    offset = (count_ref[...] - 0.5 * cells_total) / cells_total
    penalty = jnp.sqrt(offset * offset + 0.01)
    retain = retain_ref[...]
    retain_grad = sums_ref[0:n, :] + enable_ref[...] * offset / (penalty * cells_total)
    grad_ref[...] = retain_grad * retain * (1.0 - retain)
    dens_total, kl_part, count_total = [gene_ref[k : k + 1, last : last + 1] for k in range(3)]
    kl_term = kl_part / count_total - jnp.log(count_total) + jnp.log(dens_total)
    gene_sum = sums_ref[n : n + 1, 0:1] / copies
    spot_sum = sums_ref[n : n + 1, 1:2]
    loss_ref[...] = -gene_sum / genes_total - spot_sum / spots_total + kl_term + penalty[:, 0:1]


def final(genes_total, spots_total, cells_total, copies, sums, gene, count, enable, retain):
    return pl.pallas_call(
        functools.partial(final_kernel, genes_total, spots_total, cells_total, copies),
        in_specs=[VMEM] * 5,
        out_specs=[VMEM] * 2,
        out_shape=[jax.ShapeDtypeStruct(enable.shape, f32), jax.ShapeDtypeStruct((1, 1), f32)],
        compiler_params=params(12),
        cost_estimate=cost(),
        name="final",
    )(sums, gene, count, enable, retain)


def join_kernel(*refs):
    at = 0
    for ref in refs[:-1]:
        refs[-1][at : at + ref.shape[0], :] = ref[...]
        at += ref.shape[0]


def join(*parts):
    rows = sum(p.shape[0] for p in parts)
    return pl.pallas_call(
        join_kernel,
        in_specs=[VMEM] * len(parts),
        out_specs=VMEM,
        out_shape=jax.ShapeDtypeStruct((rows, parts[0].shape[1]), bf16),
        compiler_params=params(12),
        cost_estimate=cost(0, 4 * rows * parts[0].shape[1]),
        name="join",
    )(*parts)


def select_kernel(inside_ref, b_ref, e_ref, c_ref, f_ref, *out_refs):
    rows = b_ref.shape[0]
    at = 0
    for out in out_refs:
        cols = slice(at, at + out.shape[1])
        at += out.shape[1]
        for flag, refs in ((1, (b_ref, c_ref)), (0, (e_ref, f_ref))):

            @pl.when(inside_ref[0] == flag)
            def _(out=out, refs=refs, cols=cols):
                out[0:rows, :] = refs[0][:, cols]
                out[rows : 2 * rows, :] = refs[1][:, cols]
                if out.shape[0] > 2 * rows:
                    out[2 * rows :, :] = jnp.zeros_like(out[2 * rows :, :])


def select(inside, b, e, c, f, widths, pad):
    rows = b.shape[0]
    return pl.pallas_call(
        select_kernel,
        in_specs=[pl.BlockSpec(memory_space=pltpu.SMEM)] + [VMEM] * 4,
        out_specs=[VMEM] * len(widths),
        out_shape=[jax.ShapeDtypeStruct((2 * rows + pad * k, wide), bf16) for k, wide in enumerate(widths)],
        compiler_params=params(12),
        cost_estimate=cost(),
        name="select",
    )(inside, b, e, c, f)


def share_kernel(places, core_ref, *refs):
    kept_ref, sent_ref = refs[-2:]
    first = core_ref[0] == 0
    n = len(places)
    at = 0
    for ref, place in zip(refs, places):
        pred = ref[...]
        wide = pred.shape[1] // 2
        if place is not None:
            theirs = jnp.concatenate([x[...] for x in refs[n + 1 : -2]], axis=1)
            left = [x[:, place : place + 2 * wide].astype(f32) for x in (refs[n], theirs)]
            pred = pred + (left[0] + left[1])
        kept_ref[:, at : at + wide] = jnp.where(first, pred[:, :wide], pred[:, wide:])
        sent_ref[:, at : at + wide] = jnp.where(first, pred[:, wide:], pred[:, :wide])
        at += wide


def share(core, preds, left, places):
    spots = preds[0].shape[0]
    wide = sum(p.shape[1] // 2 for p in preds)
    arrays = [*preds, *left]
    return pl.pallas_call(
        functools.partial(share_kernel, places),
        in_specs=[pl.BlockSpec(memory_space=pltpu.SMEM)] + [pl.BlockSpec()] * len(arrays),
        out_specs=[VMEM] * 2,
        out_shape=[jax.ShapeDtypeStruct((spots, wide), f32)] * 2,
        compiler_params=params(24),
        cost_estimate=cost(),
        name="share",
    )(core, *[in_hbm(x) for x in arrays])


def lay_kernel(core_ref, kept_ref, theirs_ref, *refs):
    mine = pl.program_id(0) == core_ref[0]

    @pl.when(mine)
    def _():
        refs[-1][...] = kept_ref[...]

    @pl.when(jnp.logical_not(mine))
    def _():
        refs[-1][...] = theirs_ref[...]


def lay(core, kept, theirs, half, column, begun=None):
    spots, wide = kept.shape
    part = pl.BlockSpec((spots, wide), lambda i, core: (0, 0))
    return pl.pallas_call(
        lay_kernel,
        grid_spec=pltpu.PrefetchScalarGridSpec(
            num_scalar_prefetch=1,
            grid=(2,),
            in_specs=[part, part] + ([] if begun is None else [pl.BlockSpec(memory_space=pl.ANY)]),
            out_specs=pl.BlockSpec((spots, wide), lambda i, core: (i, column)),
        ),
        out_shape=jax.ShapeDtypeStruct((2 * spots, half), f32),
        input_output_aliases={} if begun is None else {3: 0},
        compiler_params=params(16),
        cost_estimate=cost(),
        name="lay",
    )(core, kept, theirs, *(() if begun is None else (begun,)))


def swap_cells(x):
    return lax.ppermute(x, "cells", [(0, 1), (1, 0)])


def swap_genes(x):
    return lax.ppermute(x, "genes", [(0, 1), (1, 0)])


def sum_spots_genes(x, first=(), second=lambda *_: ()):
    if lax.axis_size("spots") != 8:
        return lax.psum(x, ("spots", "genes")), second(*first)
    moved = [lax.ppermute(x, "spots", [(i, i ^ d) for i in range(8)]) for d in (2, 4, 6)]
    moved[0], moved[1], moved[2], *first = hold(*moved, *first)
    x = (x + moved[0]) + (moved[1] + moved[2])
    pairs = [lax.ppermute(x, ("spots", "genes"), [(i, i ^ d) for i in range(16)]) for d in (1, 2, 3)]
    pairs[0], pairs[1], pairs[2], *more = hold(*pairs, *second(*first))
    return (x + pairs[0]) + (pairs[1] + pairs[2]), more


class Step:
    def __init__(self, logits, filter_logits, expression, spot_expression, cell_mask, spot_counts):
        self.logits = pltpu.with_memory_space_constraint(logits, pltpu.HBM)
        self.expression = expression
        self.core = lax.axis_index("genes")
        self.enable = cell_mask.astype(f32).reshape(-1, 128)
        self.retain = jax.nn.sigmoid(filter_logits).reshape(-1, 128)
        self.spots = logits.shape[1]
        self.counts = spot_counts.astype(f32)[None, :]
        self.core_flag = self.core.astype(jnp.int32).reshape(1)
        self.half = expression.shape[1]
        self.target = spot_expression
        sent = lax.dynamic_slice_in_dim(spot_expression, (1 - self.core) * self.spots, self.spots, 0)
        quarter = self.half // 4
        self.target_sent = [sent[:, k * quarter : (k + 1) * quarter] for k in range(4)]

    def local_stats(self):
        part = col_stats(self.logits, self.enable, self.retain)
        count = jnp.broadcast_to(jnp.sum(self.enable * self.retain), (1, self.spots))
        return jnp.concatenate([part, count], axis=0)

    def merge_stats(self, part, away):
        top = jnp.maximum(part[0], away[0])
        here, there = jnp.exp(part[0] - top), jnp.exp(away[0] - top)
        total = part[1] * here + away[1] * there
        density = (part[2] * here + away[2] * there) / total
        self.density = density[None, :]
        self.cell_count = part[3:4, :128] + away[3:4, :128]
        self.shift = (top + jnp.log(total))[None, :]
        counts = self.counts[0]
        kl_parts = (jnp.sum(density), jnp.sum(counts * (jnp.log(counts) - jnp.log(density))), jnp.sum(counts))
        self.kl_parts = jnp.broadcast_to(jnp.stack(kl_parts)[:, None], (3, 128))

    def turned(self, order, shift, logits):
        return mapped_turned(order, logits, self.enable, self.retain, shift)

    def stats(self, parts, other, at, wide, part=0):
        column = at % (self.half // 4) // wide
        return pred_stats(self.core_flag, parts, self.target, other, at // wide, column, wide, part)

    def gathered_whole(self):
        own = lax.all_gather(self.expression, "spots", axis=0, tiled=True)
        other = swap_genes(own)
        part = self.local_stats()
        self.target_other = [swap_genes(x) for x in self.target_sent]
        self.merge_stats(part, swap_cells(part))
        order = jnp.arange(PIECES, dtype=jnp.int32)
        mapped = self.turned(order, self.shift, self.logits)
        wide = self.half // 4
        widths, panels, stats = (wide,) * 4, [], []
        for q in range(4):
            pieces = tuple((r, 0, r, q) for r in range(PIECES))
            (partial,), (panel,) = forward(self.core_flag, mapped, [(own, other)], [pieces], wide)
            panels.append(panel)
            stats.append(self.stats([lax.psum(partial, "cells")], self.target_other[q], q * wide, wide))
        return order, widths, panels, stats, (), None

    def gathered_line(self):
        near_pairs = [(2 * z + y, 2 * (z ^ 1) + y) for z in range(4) for y in range(2)]
        middle_pairs = [(2 * z + y, 2 * (3 - z) + y) for z in (1, 2) for y in range(2)]
        across_pairs = [(i, i ^ 1) for i in range(8)]

        def near(x):
            return lax.ppermute(x, "spots", near_pairs)

        def middle(x):
            return lax.ppermute(x, "spots", middle_pairs)

        def across(x):
            return lax.ppermute(x, "spots", across_pairs)

        spot = lax.axis_index("spots")
        z, y = spot // 2, spot % 2
        inside = (z == 1) | (z == 2)
        inside_flag = inside.astype(jnp.int32).reshape(1)
        column = jnp.stack([z, z ^ 1, jnp.where(z < 2, 2, 1), jnp.where(z < 2, 3, 0)])
        order = jnp.concatenate([2 * column + y, 2 * column + (1 - y)]).astype(jnp.int32)
        unit = self.half // 8
        expr = self.expression

        def cut(x, at, wide):
            return x[:, at * unit : (at + wide) * unit]

        def pick(b, e, c, f, *widths, pad=0):
            return select(inside_flag, b, e, c, f, [wide * unit for wide in widths], pad)

        core = self.core_flag

        def run(sources, chunks, wide, begun=None, near=False, column=None, columns=0, left=None):
            columns = (None if column is None else 2 * column * unit), 2 * columns * unit
            return forward(core, mapped, sources, chunks, wide * unit, begun, near, *columns, left)

        def whole(c, d):
            return ((0, 0, 0, c), (1, 1, 0, d), (2, 2, 0, 0), (3, 2, 1, 0), (4, 3, 0, c), (5, 4, 0, d), (6, 5, 0, 0), (7, 5, 1, 0))

        s01 = cut(expr, 0, 4)
        beside = across(expr)
        a01 = near(s01)
        b01 = middle(s01)
        expr_o = swap_genes(expr)
        target_0 = swap_genes(self.target_sent[0])
        part = self.local_stats()
        a01, b01, part, target_0, sv, target_1 = hold(
            a01, b01, part, target_0, cut(expr, 4, 3), self.target_sent[1]
        )
        c01 = middle(a01)
        e01 = near(b01)
        away = swap_cells(part)
        target_1 = swap_genes(target_1)
        self.merge_stats(part, away)
        mapped = self.turned(order, self.shift, self.logits)
        beside, e01, c01, expr_o, mapped, a01, sv, target_1 = hold(
            beside, e01, c01, expr_o, mapped, a01, sv, target_1
        )
        yn = across(a01)
        f01 = near(c01)
        beside_o = swap_genes(beside)
        a01_o = swap_genes(a01)
        bv = middle(sv)
        mf0, mf1 = pick(b01, e01, c01, f01, 2, 2)
        yn, mf0, mf1, a01_o, sv, bv, beside, self.kl_parts = hold(
            yn, mf0, mf1, a01_o, sv, bv, beside, self.kl_parts
        )
        ymf0 = across(mf0)
        av = near(sv)
        mf0_o, yn_o = swap_genes(mf0), swap_genes(yn)
        sf = join(cut(expr, 7, 1), cut(beside, 7, 1))
        expr_2, a01_2, beside_2, yn_2 = (expr, expr_o), (a01, a01_o), (beside, beside_o), (yn, yn_o)
        begun = run([expr_2, beside_2], [((0, 0, 0, q), (4, 1, 0, q)) for q in range(4, 8)], 1)
        ymf0, av, mf0_o, yn_o, mf1, bv, mapped, *begun = hold(
            ymf0, av, mf0_o, yn_o, mf1, bv, mapped, *begun[0], *begun[1]
        )
        ymf1 = across(mf1)
        ev = near(bv)
        cv = middle(av)
        ymf0_o, mf1_o = swap_genes(ymf0), swap_genes(mf1)
        (high0, low0), (panel0,) = run(
            [expr_2, a01_2, (mf0, mf0_o), beside_2, yn_2, (ymf0, ymf0_o)], [whole(0, 0)], 2, column=0, columns=2
        )
        ymf1, ev, cv, high0, mf1_o, av, mapped = hold(ymf1, ev, cv, high0, mf1_o, av, mapped)
        ynv = across(av)
        fv = near(cv)
        ymf1_o = swap_genes(ymf1)
        high0_away = swap_cells(high0)
        av_o = swap_genes(av)
        (partial1,), (panel1,) = run([expr_2, a01_2, (mf1, mf1_o), beside_2, yn_2, (ymf1, ymf1_o)], [whole(1, 1)], 2)
        ynv, fv, partial1, high0_away, av_o, sf, mapped = hold(ynv, fv, partial1, high0_away, av_o, sf, mapped)
        m2, m34 = pick(bv, ev, cv, fv, 1, 2, pad=16)
        ym2 = across(m2)
        af, bf = near(sf), middle(sf)
        away1 = swap_cells(partial1)
        ynv_o = swap_genes(ynv)
        more = run(
            [(av, av_o), (ynv, ynv_o)], [((1, 0, 0, q), (5, 1, 0, q)) for q in range(3)], 1, (begun[0:3], begun[4:7])
        )
        ym2, m2, m34, mapped, *more = hold(ym2, m2, m34, mapped, *more[0], *more[1])
        ym34 = across(m34)
        ym2_o, m2_o = swap_genes(ym2), swap_genes(m2)
        af, bf = hold(af, bf)
        cf = middle(af)

        def rest(column):
            return ((2, 0, 0, column), (3, 0, 1, column), (6, 1, 0, column), (7, 1, 1, column))

        (high2, low), (panel2,) = run(
            [(m2, m2_o), (ym2, ym2_o)], [rest(0)], 1, (more[0:1], more[3:4]), near=True, column=0, columns=4
        )
        stats0 = self.stats([high0, high0_away], target_0, 0, 2 * unit)
        cf, high2, away1, m34, bf, af, target_2, *stats0 = hold(
            cf, high2, away1, m34, bf, af, self.target_sent[2], *stats0
        )
        target_2 = swap_genes(target_2)
        ef, ff = near(bf), near(cf)
        m34_o = swap_genes(m34)
        high2_away = swap_cells(high2)
        stats1 = self.stats([partial1, away1], target_1, 2 * unit, 2 * unit)
        ym34, ef, m34, mapped, high2_away, af, low0, target_2, target_3, *stats1 = hold(
            ym34, ef, m34, mapped, high2_away, af, low0, target_2, self.target_sent[3], *stats1
        )
        ym34_o, af_o = swap_genes(ym34), swap_genes(af)
        low0_first_away = swap_cells(cut(low0, 0, 2))
        target_3 = swap_genes(target_3)
        self.target_other = (target_0, target_1, target_2, target_3)
        sources = [(m34, m34_o), (ym34, ym34_o)]
        (high3, low), (panel3,) = run(sources, [rest(0)], 1, (more[1:2], more[4:5]), column=1, columns=4, left=low, near=True)
        high3_away = swap_cells(high3)
        (high4, low), (panel4,) = run(sources, [rest(1)], 1, (more[2:3], more[5:6]), column=2, columns=4, left=low, near=True)
        ff, high3_away, high4, low0_first_away, target_3, af_o, mapped = hold(
            ff, high3_away, high4, low0_first_away, target_3, af_o, mapped
        )
        high4_away = swap_cells(high4)
        (mff,) = pick(bf, ef, cf, ff, 1)
        mff_o = swap_genes(mff)
        late = ((1, 0, 0, 0), (2, 1, 0, 0), (3, 1, 2, 0), (5, 0, 1, 0), (6, 1, 1, 0), (7, 1, 3, 0))
        (highf, low), (panelf,) = run(
            [(af, af_o), (mff, mff_o)], [late], 1, (begun[3:4], begun[7:8]), column=3, columns=4, left=low, near=True
        )
        highf, high2, high2_away = hold(highf, high2, high2_away)
        highf_away = swap_cells(highf)
        low0_last = cut(low0, 2, 2)
        high4, high4_away, highf, low0_last = hold(high4, high4_away, highf, low0_last)
        low0_last_away = swap_cells(low0_last)
        late = [
            self.stats([high2, high2_away], target_2, 4 * unit, unit),
            self.stats([high3, high3_away], target_2, 5 * unit, unit),
            self.stats([high4, high4_away], target_3, 6 * unit, unit),
            self.stats([highf, highf_away], target_3, 7 * unit, unit),
        ]
        widths = (2 * unit,) * 2 + (unit,) * 4
        panels = (panel0, panel1, panel2, panel3, panel4, panelf)
        return order, widths, panels, [stats0, stats1, *late], (low0, low0_first_away, low0_last_away), low


def body(logits, filter_logits, expression, spot_expression, cell_mask, spot_counts):
    cells_total = logits.shape[0] * lax.axis_size("cells")
    spots = logits.shape[1]
    spots_total = spots * lax.axis_size("spots") * lax.axis_size("genes")
    genes_total = expression.shape[1] * lax.axis_size("genes")
    step = Step(logits, filter_logits, expression, spot_expression, cell_mask, spot_counts)
    gathered = step.gathered_line() if lax.axis_size("spots") == 8 else step.gathered_whole()
    order, widths, panels, stats, left, late_left = gathered
    gene_stats, preds, spot_stats = zip(*stats)
    split = 2
    gene, (kept, sent) = sum_spots_genes(
        jnp.concatenate([*gene_stats, step.kl_parts], axis=1),
        preds[:split],
        lambda *first: share(step.core_flag, first, left, [0, None] if left else [None] * split),
    )
    spot = functools.reduce(jnp.add, spot_stats)
    cols = jnp.concatenate([step.shift, step.density, step.counts], axis=0)
    turned, col, sums = grad_pred(
        step.core_flag, widths, genes_total, spots_total, spot, gene, cols, step.target, step.target_other, preds
    )
    left, places = [], [None] * (len(widths) - split)
    if late_left is not None:
        turned, late_left = hold(turned, late_left)
        left, places = [late_left, swap_cells(late_left)], [2 * sum(widths[split:q]) for q in range(split, len(widths))]
    turned, sent = hold(turned, sent)
    theirs = swap_genes(sent)
    grad_logits, row = backward(order, step.logits, step.enable, step.retain, col, turned, panels)

    row, core, theirs, *left = hold(row, step.core_flag, theirs, *left)
    half = expression.shape[1]

    def lay_both(late_kept, late_sent):
        predicted = lay(core, kept, theirs, half, 0)
        return (lay(core, late_kept, swap_genes(late_sent), half, 1, predicted),)

    row_sums, (predicted,) = sum_spots_genes(jnp.concatenate([row, sums], axis=0), share(core, preds[split:], left, places), lay_both)
    copies = lax.axis_size("spots") * lax.axis_size("genes")
    filter_grad, total_loss = final(
        genes_total, spots_total, cells_total, copies, row_sums, gene, step.cell_count, step.enable, step.retain
    )
    return (predicted, total_loss.reshape(()), grad_logits, filter_grad.reshape(-1))


def solution(mesh):
    placed = (
        P("cells", ("spots", "genes")),
        P("cells"),
        P(("cells", "spots"), "genes"),
        P("spots", "genes"),
        P("cells"),
        P(("spots", "genes")),
    )
    return jax.shard_map(
        body,
        mesh=mesh,
        in_specs=placed,
        out_specs=(P("spots", "genes"), P(), P("cells", ("spots", "genes")), P("cells")),
        check_vma=False,
    )
```

```python
import functools

import jax
import jax.numpy as jnp
from jax import lax
from jax.experimental import pallas as pl
from jax.experimental.pallas import tpu as pltpu
from jax.sharding import PartitionSpec as P

epsilon = 1e-06
bf16 = jnp.bfloat16
f32 = jnp.float32
PIECES = 8
MIB = 1024 * 1024
VMEM = pl.BlockSpec(memory_space=pltpu.VMEM)


def params(limit):
    return pltpu.CompilerParams(vmem_limit_bytes=limit * MIB)


def cost(flops=0, bytes_accessed=0, transcendentals=0):
    return pl.CostEstimate(flops=1, bytes_accessed=1, transcendentals=0)


def in_hbm(x):
    return pltpu.with_memory_space_constraint(x, pltpu.HBM)


def hold(*values):
    return lax.optimization_barrier(values)


def col_stats_kernel(logits_ref, enable_ref, retain_ref, out_ref, top, total, dens):
    step = pl.program_id(0)

    @pl.when(step == 0)
    def _():
        top[...] = jnp.full_like(top, -1e29)
        total[...] = jnp.zeros_like(total)
        dens[...] = jnp.zeros_like(dens)

    rows, spots = logits_ref.shape
    enable = enable_ref[...].T
    retain = retain_ref[...].T
    blocks = []
    new = top[...]
    for k in range(rows // 128):
        block = jnp.where(enable[:, k : k + 1] > 0, logits_ref[128 * k : 128 * (k + 1), :], -1e30)
        blocks.append(block.reshape(16, 8, spots))
        new = jnp.maximum(new, jnp.max(blocks[-1], axis=0))
    shrink = jnp.exp(top[...] - new)
    top[...] = new
    sums = total[...] * shrink
    kept = dens[...] * shrink
    for k in range(rows // 128):
        part = jnp.exp(blocks[k] - new[None])
        share = jnp.broadcast_to(retain[:, k : k + 1], (128, spots)).reshape(16, 8, spots)
        sums = sums + jnp.sum(part, axis=0)
        kept = kept + jnp.sum(part * share, axis=0)
    total[...] = sums
    dens[...] = kept

    @pl.when(step == pl.num_programs(0) - 1)
    def _():
        best = jnp.max(new, axis=0, keepdims=True)
        scale = jnp.exp(new - best)
        out_ref[0:1, :] = best
        out_ref[1:2, :] = jnp.sum(sums * scale, axis=0, keepdims=True)
        out_ref[2:3, :] = jnp.sum(kept * scale, axis=0, keepdims=True)


def col_stats(logits, enable, retain, block=1024):
    cells, spots = logits.shape
    cell = pl.BlockSpec((block // 128, 128), lambda i: (i, 0))
    return pl.pallas_call(
        col_stats_kernel,
        grid=(cells // block,),
        in_specs=[pl.BlockSpec((block, spots), lambda i: (i, 0)), cell, cell],
        out_specs=pl.BlockSpec((3, spots), lambda i: (0, 0)),
        out_shape=jax.ShapeDtypeStruct((3, spots), f32),
        scratch_shapes=[pltpu.VMEM((8, spots), f32)] * 3,
        compiler_params=params(20),
        cost_estimate=cost(cells * spots * 8, cells * spots * 4, cells * spots),
        name="col_stats",
    )(logits, enable, retain)


def mapped_kernel(order_ref, logits_ref, enable_ref, retain_ref, shift_ref, out_ref):
    rows, spots = logits_ref.shape
    enable = enable_ref[...].T
    retain = retain_ref[...].T
    shift = shift_ref[...]
    for k in range(rows // 128):
        block = jnp.where(enable[:, k : k + 1] > 0, logits_ref[128 * k : 128 * (k + 1), :], -1e30)
        mapped = retain[:, k : k + 1] * jnp.exp(block - shift)
        out_ref[:, 128 * k : 128 * (k + 1)] = mapped.astype(bf16).T


def mapped_turned(order, logits, enable, retain, shift):
    cells, spots = logits.shape
    block = cells // PIECES
    cell = pl.BlockSpec((block // 128, 128), lambda i, order: (order[i], 0))
    return pl.pallas_call(
        mapped_kernel,
        grid_spec=pltpu.PrefetchScalarGridSpec(
            num_scalar_prefetch=1,
            grid=(PIECES,),
            in_specs=[
                pl.BlockSpec((block, spots), lambda i, order: (order[i], 0)),
                cell,
                cell,
                pl.BlockSpec((1, spots), lambda i, order: (0, 0)),
            ],
            out_specs=pl.BlockSpec((spots, block), lambda i, order: (0, i)),
        ),
        out_shape=pltpu.HBM((spots, cells), bf16),
        compiler_params=params(20),
        cost_estimate=cost(cells * spots * 6, cells * spots * 6, cells * spots),
        name="mapped_turned",
    )(order, logits, enable, retain, shift)


def forward_kernel(chunks, count, rows, wide, more, column, core_ref, mapped_ref, *refs):
    n = len(chunks)
    sources = (refs[:count], refs[count : 2 * count])
    refs = refs[2 * count :]
    totals = [None] * n
    if "begun" in more:
        totals = [ref[...] for ref in refs[:n]]
        refs = refs[2 * n :]
    if "left" in more:
        refs = refs[1:]
    outs = n if column is None else 2
    pred_refs, refs = refs[:outs], refs[outs:]
    panel_refs, held = refs[:n], refs[n : 2 * n]
    turned, own_sems, other_sems, mapped_sems, panel_sems = refs[2 * n : 2 * n + 5]
    used = sorted({piece[0] for pieces in chunks for piece in pieces})

    def fetch(q, k, which, place):
        r, source, block, col = chunks[q][k]
        part = sources[which][source].at[pl.ds(block * rows, rows), pl.ds(col * wide, wide)]
        target = held[q].at[pl.ds(k * rows, rows), pl.ds(place, wide)]
        return pltpu.make_async_copy(part, target, (own_sems, other_sems)[which].at[q, k])

    def load(r):
        at = used.index(r) * rows
        return pltpu.make_async_copy(
            mapped_ref.at[:, pl.ds(r * rows, rows)], turned.at[:, pl.ds(at, rows)], mapped_sems.at[r]
        )

    def save(q, k):
        target = panel_refs[q].at[pl.ds(chunks[q][k][0] * rows, rows), :]
        return pltpu.make_async_copy(held[q].at[pl.ds(k * rows, rows), :], target, panel_sems.at[q, k])

    steps = [[(q, k) for q in range(n) for k in range(len(chunks[q])) if chunks[q][k][0] == r] for r in used]
    for r, step in zip(used, steps):
        for q, k in step:
            for core in range(2):

                @pl.when(core_ref[0] == core)
                def _(core=core, q=q, k=k):
                    fetch(q, k, 0, core * wide).start()
                    fetch(q, k, 1, (1 - core) * wide).start()

        load(r).start()
    for at, (r, step) in enumerate(zip(used, steps)):
        load(r).wait()
        for q, k in step:
            fetch(q, k, 0, 0).wait()
            fetch(q, k, 1, 0).wait()
            save(q, k).start()
            part = jnp.dot(
                turned[:, at * rows : (at + 1) * rows],
                held[q][k * rows : (k + 1) * rows, :],
                preferred_element_type=f32,
            )
            totals[q] = part if totals[q] is None else totals[q] + part
    if column is None:
        for q in range(n):
            pred_refs[q][...] = totals[q]
    else:
        left, left_sem = refs[-2:]
        for q in range(n):
            high = totals[q].astype(bf16)
            cols = slice(2 * q * wide, 2 * (q + 1) * wide)
            pred_refs[0][:, cols] = high
            left[:, cols] = (totals[q] - high.astype(f32)).astype(bf16)
        copy = pltpu.make_async_copy(left, pred_refs[1].at[:, pl.ds(column, 2 * n * wide)], left_sem.at[0])
        copy.start()
        copy.wait()
    for step in steps:
        for q, k in step:
            save(q, k).wait()


def forward(core, mapped, sources, chunks, wide, begun=None, near=False, column=None, columns=0, left=None):
    spots, cells = mapped.shape
    rows = cells // PIECES
    own, other = zip(*sources)
    n = len(chunks)
    hbm = pl.BlockSpec(memory_space=pltpu.HBM)
    used = {piece[0] for pieces in chunks for piece in pieces}
    longest = max(len(pieces) for pieces in chunks)
    outs = n if column is None else 2
    arrays = [x if near else in_hbm(x) for x in own + other]
    specs = [VMEM if near else hbm] * len(arrays)
    aliases = {}
    if begun is not None:
        aliases = {2 + len(arrays) + n + q: outs + q for q in range(n)}
        arrays += [*begun[0], *begun[1]]
        specs += [VMEM] * n + [hbm] * n
    if left is not None:
        aliases[2 + len(arrays)] = 1
        arrays.append(left)
        specs.append(hbm)
    more = ("begun",) * (begun is not None) + ("left",) * (left is not None)
    results = pl.pallas_call(
        functools.partial(forward_kernel, chunks, len(own), rows, wide, more, column),
        in_specs=[pl.BlockSpec(memory_space=pltpu.SMEM), hbm] + specs,
        out_specs=([VMEM] * n if column is None else [VMEM, hbm]) + [hbm] * n,
        out_shape=(
            [jax.ShapeDtypeStruct((spots, 2 * wide), f32)] * n
            if column is None
            else [jax.ShapeDtypeStruct((spots, 2 * n * wide), bf16), pltpu.HBM((spots, columns), bf16)]
        )
        + [pltpu.HBM((cells, 2 * wide), bf16)] * n,
        scratch_shapes=[pltpu.VMEM((len(pieces) * rows, 2 * wide), bf16) for pieces in chunks]
        + [pltpu.VMEM((spots, len(used) * rows), bf16)]
        + [pltpu.SemaphoreType.DMA((n, longest))] * 2
        + [pltpu.SemaphoreType.DMA((PIECES,)), pltpu.SemaphoreType.DMA((n, longest))]
        + ([] if column is None else [pltpu.VMEM((spots, 2 * n * wide), bf16), pltpu.SemaphoreType.DMA((1,))]),
        input_output_aliases=aliases,
        compiler_params=params(22),
        cost_estimate=cost(),
        name="forward",
    )(core, in_hbm(mapped), *arrays)
    return results[:outs], results[outs:]


def in_order(core, own, other):
    first = core == 0
    return jnp.concatenate([jnp.where(first, own, other), jnp.where(first, other, own)], axis=1)


def total_of(refs):
    return functools.reduce(jnp.add, [ref[...].astype(f32) for ref in refs])


def stats_kernel(parts, core_ref, *refs):
    own_ref, other_ref, gene_ref, pred_ref, spot_ref = refs[parts:]
    pred = total_of(refs[:parts])
    pred_ref[...] = pred
    target = in_order(core_ref[0], own_ref[...], other_ref[...])
    lane = lax.broadcasted_iota(jnp.int32, spot_ref.shape, 1)
    spot = jnp.zeros(spot_ref.shape, f32)
    for k, term in enumerate((pred * target, pred * pred, target * target)):
        gene_ref[k : k + 1, :] = jnp.sum(term, axis=0, keepdims=True)
        spot = jnp.where(lane == k, jnp.sum(term, axis=1, keepdims=True), spot)
    spot_ref[...] = spot


def pred_stats(core, parts, target, other, column, other_column, wide, part=0):
    spots = parts[0].shape[0]
    whole = pl.BlockSpec((spots, 2 * wide), lambda i, core: (0, 0))
    return pl.pallas_call(
        functools.partial(stats_kernel, len(parts)),
        grid_spec=pltpu.PrefetchScalarGridSpec(
            num_scalar_prefetch=1,
            grid=(1,),
            in_specs=[pl.BlockSpec((spots, 2 * wide), lambda i, core: (0, part))] * len(parts)
            + [
                pl.BlockSpec((spots, wide), lambda i, core: (core[0], column)),
                pl.BlockSpec((spots, wide), lambda i, core: (0, other_column)),
            ],
            out_specs=[
                pl.BlockSpec((3, 2 * wide), lambda i, core: (0, 0)),
                whole,
                pl.BlockSpec((spots, 4), lambda i, core: (0, 0)),
            ],
        ),
        out_shape=[
            jax.ShapeDtypeStruct((3, 2 * wide), f32),
            jax.ShapeDtypeStruct((spots, 2 * wide), f32),
            jax.ShapeDtypeStruct((spots, 4), f32),
        ],
        compiler_params=params(16),
        cost_estimate=cost(),
        name="pred_stats",
    )(core, *parts, target, other)


def grad_pred_kernel(widths, genes_total, spots_total, core_ref, spot_ref, gene_ref, cols_ref, own_ref, *refs):
    n = len(widths)
    other_refs, pred_refs = refs[:4], refs[4 : 4 + n]
    refs = refs[4:]
    quarter = other_refs[0].shape[1]
    turned_ref, col_ref, sums_ref = refs[n:]
    spot = spot_ref[...]
    spot_pg, spot_pp, spot_gg = spot[:, 0:1], spot[:, 1:2], spot[:, 2:3]
    spot_scale = lax.rsqrt(spot_pp + epsilon) * lax.rsqrt(spot_gg + epsilon)
    spot_cos = spot_pg * spot_scale
    spot_back = spot_cos / (spot_pp + epsilon)
    gene = gene_ref[:, : 2 * sum(widths)]
    gene_scale = lax.rsqrt(gene[1:2, :] + epsilon) * lax.rsqrt(gene[2:3, :] + epsilon)
    gene_cos = gene[0:1, :] * gene_scale
    gene_back = gene_cos / (gene[1:2, :] + epsilon)
    gene_pred, gene_target = gene_back / genes_total, gene_scale / genes_total
    spot_pred, spot_target = spot_back / spots_total, spot_scale / spots_total
    folded = jnp.zeros((spot.shape[0], 128), f32)
    at = 0
    low = 0
    for q in range(n):
        wide = widths[q]
        pred = pred_refs[q][...]
        other = other_refs[low // quarter]
        other_low = low % quarter
        target = in_order(core_ref[0], own_ref[:, low : low + wide], other[:, other_low : other_low + wide])
        cols = slice(at, at + 2 * wide)
        grad = pred * (gene_pred[:, cols] + spot_pred) - target * (gene_target[:, cols] + spot_target)
        grad_low = grad.astype(bf16)
        turned_ref[at : at + 2 * wide, :] = grad_low.T
        prod = grad_low.astype(f32) * pred
        for k in range(0, 2 * wide, 128):
            folded = folded + prod[:, k : k + 128]
        at += 2 * wide
        low += wide
    shift, density, counts = cols_ref[0:1, :], cols_ref[1:2, :], cols_ref[2:3, :]
    dens_total = gene_ref[0:1, at : at + 1]
    count_total = gene_ref[2:3, at : at + 1]
    dens_grad = -counts / (count_total * density) + 1.0 / dens_total
    col_ref[0:1, :] = shift
    col_ref[1:2, :] = dens_grad
    col_ref[2:3, :] = jnp.sum(folded.T, axis=0, keepdims=True) + density * dens_grad
    lane = lax.broadcasted_iota(jnp.int32, (1, 128), 1)
    gene_sum = jnp.sum(gene_cos, axis=1, keepdims=True)
    spot_sum = jnp.sum(spot_cos, axis=0, keepdims=True)
    sums_ref[...] = jnp.where(lane == 0, gene_sum, jnp.where(lane == 1, spot_sum, 0.0))


def grad_pred(core, widths, genes_total, spots_total, spot, gene, cols, target, others, preds):
    half = target.shape[1]
    spots = spot.shape[0]
    genes = 2 * half
    return pl.pallas_call(
        functools.partial(grad_pred_kernel, widths, genes_total, spots_total),
        grid_spec=pltpu.PrefetchScalarGridSpec(
            num_scalar_prefetch=1,
            grid=(1,),
            in_specs=[VMEM] * 3
            + [pl.BlockSpec((spots, half), lambda i, core: (core[0], 0))]
            + [VMEM] * (4 + len(preds)),
            out_specs=[VMEM] * 3,
        ),
        out_shape=[
            pltpu.VMEM((genes, spots), bf16),
            jax.ShapeDtypeStruct((3, spots), f32),
            jax.ShapeDtypeStruct((1, 128), f32),
        ],
        compiler_params=params(20),
        cost_estimate=cost(spots * genes * 14, spots * genes * 10),
        name="grad_pred",
    )(core, spot, gene, cols, target, *others, *preds)


def backward_kernel(widths, order_ref, logits_ref, enable_ref, retain_ref, col_ref, turned_ref, *refs):
    n = len(widths)
    panel_refs = refs[:n]
    grad_ref, row_ref = refs[n:]
    rows, spots = logits_ref.shape
    first = pl.multiple_of(pl.program_id(0) * rows, rows)
    enable = enable_ref[...].T
    retain = retain_ref[...].T
    shift, dens, inner = col_ref[0:1, :], col_ref[1:2, :], col_ref[2:3, :]
    part = rows // 2
    for h in range(2):
        here = pl.ds(first + h * part, part)
        near = slice(h * part, (h + 1) * part)
        panel = jnp.concatenate([ref[near if ref.shape[0] == rows else here, :] for ref in panel_refs], axis=1)
        grad_mapped = jnp.dot(panel, turned_ref[...], preferred_element_type=f32) + dens
        for k in range(part // 128):
            at = h * (part // 128) + k
            lines = slice(128 * at, 128 * (at + 1))
            block = jnp.where(enable[:, at : at + 1] > 0, logits_ref[lines, :], -1e30)
            mapping = jnp.exp(block - shift)
            grad = grad_mapped[128 * k : 128 * (k + 1), :]
            grad_ref[lines, :] = mapping * (retain[:, at : at + 1] * grad - inner)
            prod = grad * mapping
            folded = prod[:, 0:128]
            for c in range(128, spots, 128):
                folded = folded + prod[:, c : c + 128]
            row_ref[at : at + 1, :] = jnp.sum(folded.T, axis=0, keepdims=True)


def backward(order, logits, enable, retain, col, turned, panels):
    cells, spots = logits.shape
    genes = turned.shape[0]
    block = cells // PIECES
    widths = tuple(p.shape[1] for p in panels)
    streamed = (0,) + tuple(range(len(panels) - 2, len(panels)))
    cell = pl.BlockSpec((block // 128, 128), lambda i, order: (order[i], 0))
    return pl.pallas_call(
        functools.partial(backward_kernel, widths),
        grid_spec=pltpu.PrefetchScalarGridSpec(
            num_scalar_prefetch=1,
            grid=(PIECES,),
            in_specs=[
                pl.BlockSpec((block, spots), lambda i, order: (order[i], 0)),
                cell,
                cell,
                pl.BlockSpec((3, spots), lambda i, order: (0, 0)),
            ]
            + [VMEM]
            + [pl.BlockSpec((block, w), lambda i, order: (i, 0)) if q in streamed else VMEM for q, w in enumerate(widths)],
            out_specs=[pl.BlockSpec((block, spots), lambda i, order: (order[i], 0)), cell],
        ),
        out_shape=[
            jax.ShapeDtypeStruct((cells, spots), f32),
            jax.ShapeDtypeStruct((cells // 128, 128), f32),
        ],
        compiler_params=params(26),
        cost_estimate=cost(2 * cells * spots * genes, cells * 8 * spots, cells * spots),
        name="backward",
    )(order, logits, enable, retain, col, turned, *[in_hbm(p) if q in streamed else p for q, p in enumerate(panels)])


def final_kernel(genes_total, spots_total, cells_total, copies, sums_ref, gene_ref, count_ref, enable_ref, retain_ref, *refs):
    grad_ref, loss_ref = refs
    n = enable_ref.shape[0]
    last = gene_ref.shape[1] - 1
    offset = (count_ref[...] - 0.5 * cells_total) / cells_total
    penalty = jnp.sqrt(offset * offset + 0.01)
    retain = retain_ref[...]
    retain_grad = sums_ref[0:n, :] + enable_ref[...] * offset / (penalty * cells_total)
    grad_ref[...] = retain_grad * retain * (1.0 - retain)
    dens_total, kl_part, count_total = [gene_ref[k : k + 1, last : last + 1] for k in range(3)]
    kl_term = kl_part / count_total - jnp.log(count_total) + jnp.log(dens_total)
    gene_sum = sums_ref[n : n + 1, 0:1] / copies
    spot_sum = sums_ref[n : n + 1, 1:2]
    loss_ref[...] = -gene_sum / genes_total - spot_sum / spots_total + kl_term + penalty[:, 0:1]


def final(genes_total, spots_total, cells_total, copies, sums, gene, count, enable, retain):
    return pl.pallas_call(
        functools.partial(final_kernel, genes_total, spots_total, cells_total, copies),
        in_specs=[VMEM] * 5,
        out_specs=[VMEM] * 2,
        out_shape=[jax.ShapeDtypeStruct(enable.shape, f32), jax.ShapeDtypeStruct((1, 1), f32)],
        compiler_params=params(12),
        cost_estimate=cost(),
        name="final",
    )(sums, gene, count, enable, retain)


def join_kernel(*refs):
    at = 0
    for ref in refs[:-1]:
        refs[-1][at : at + ref.shape[0], :] = ref[...]
        at += ref.shape[0]


def join(*parts):
    rows = sum(p.shape[0] for p in parts)
    return pl.pallas_call(
        join_kernel,
        in_specs=[VMEM] * len(parts),
        out_specs=VMEM,
        out_shape=jax.ShapeDtypeStruct((rows, parts[0].shape[1]), bf16),
        compiler_params=params(12),
        cost_estimate=cost(0, 4 * rows * parts[0].shape[1]),
        name="join",
    )(*parts)


def select_kernel(inside_ref, b_ref, e_ref, c_ref, f_ref, *out_refs):
    rows = b_ref.shape[0]
    at = 0
    for out in out_refs:
        cols = slice(at, at + out.shape[1])
        at += out.shape[1]
        for flag, refs in ((1, (b_ref, c_ref)), (0, (e_ref, f_ref))):

            @pl.when(inside_ref[0] == flag)
            def _(out=out, refs=refs, cols=cols):
                out[0:rows, :] = refs[0][:, cols]
                out[rows : 2 * rows, :] = refs[1][:, cols]
                if out.shape[0] > 2 * rows:
                    out[2 * rows :, :] = jnp.zeros_like(out[2 * rows :, :])


def select(inside, b, e, c, f, widths, pad):
    rows = b.shape[0]
    return pl.pallas_call(
        select_kernel,
        in_specs=[pl.BlockSpec(memory_space=pltpu.SMEM)] + [VMEM] * 4,
        out_specs=[VMEM] * len(widths),
        out_shape=[jax.ShapeDtypeStruct((2 * rows + pad * k, wide), bf16) for k, wide in enumerate(widths)],
        compiler_params=params(12),
        cost_estimate=cost(),
        name="select",
    )(inside, b, e, c, f)


def share_kernel(places, core_ref, *refs):
    kept_ref, sent_ref = refs[-2:]
    first = core_ref[0] == 0
    n = len(places)
    at = 0
    for ref, place in zip(refs, places):
        pred = ref[...]
        wide = pred.shape[1] // 2
        if place is not None:
            theirs = jnp.concatenate([x[...] for x in refs[n + 1 : -2]], axis=1)
            left = [x[:, place : place + 2 * wide].astype(f32) for x in (refs[n], theirs)]
            pred = pred + (left[0] + left[1])
        kept_ref[:, at : at + wide] = jnp.where(first, pred[:, :wide], pred[:, wide:])
        sent_ref[:, at : at + wide] = jnp.where(first, pred[:, wide:], pred[:, :wide])
        at += wide


def share(core, preds, left, places):
    spots = preds[0].shape[0]
    wide = sum(p.shape[1] // 2 for p in preds)
    arrays = [*preds, *left]
    return pl.pallas_call(
        functools.partial(share_kernel, places),
        in_specs=[pl.BlockSpec(memory_space=pltpu.SMEM)] + [pl.BlockSpec()] * len(arrays),
        out_specs=[VMEM] * 2,
        out_shape=[jax.ShapeDtypeStruct((spots, wide), f32)] * 2,
        compiler_params=params(24),
        cost_estimate=cost(),
        name="share",
    )(core, *[in_hbm(x) for x in arrays])


def lay_kernel(core_ref, kept_ref, theirs_ref, *refs):
    mine = pl.program_id(0) == core_ref[0]

    @pl.when(mine)
    def _():
        refs[-1][...] = kept_ref[...]

    @pl.when(jnp.logical_not(mine))
    def _():
        refs[-1][...] = theirs_ref[...]


def lay(core, kept, theirs, half, column, begun=None):
    spots, wide = kept.shape
    part = pl.BlockSpec((spots, wide), lambda i, core: (0, 0))
    return pl.pallas_call(
        lay_kernel,
        grid_spec=pltpu.PrefetchScalarGridSpec(
            num_scalar_prefetch=1,
            grid=(2,),
            in_specs=[part, part] + ([] if begun is None else [pl.BlockSpec(memory_space=pl.ANY)]),
            out_specs=pl.BlockSpec((spots, wide), lambda i, core: (i, column)),
        ),
        out_shape=jax.ShapeDtypeStruct((2 * spots, half), f32),
        input_output_aliases={} if begun is None else {3: 0},
        compiler_params=params(16),
        cost_estimate=cost(),
        name="lay",
    )(core, kept, theirs, *(() if begun is None else (begun,)))


def swap_cells(x):
    return lax.ppermute(x, "cells", [(0, 1), (1, 0)])


def swap_genes(x):
    return lax.ppermute(x, "genes", [(0, 1), (1, 0)])


def sum_spots_genes(x, first=(), second=lambda *_: ()):
    if lax.axis_size("spots") != 8:
        return lax.psum(x, ("spots", "genes")), second(*first)
    moved = [lax.ppermute(x, "spots", [(i, i ^ d) for i in range(8)]) for d in (2, 4, 6)]
    moved[0], moved[1], moved[2], *first = hold(*moved, *first)
    x = (x + moved[0]) + (moved[1] + moved[2])
    pairs = [lax.ppermute(x, ("spots", "genes"), [(i, i ^ d) for i in range(16)]) for d in (1, 2, 3)]
    pairs[0], pairs[1], pairs[2], *more = hold(*pairs, *second(*first))
    return (x + pairs[0]) + (pairs[1] + pairs[2]), more


class Step:
    def __init__(self, logits, filter_logits, expression, spot_expression, cell_mask, spot_counts):
        self.logits = pltpu.with_memory_space_constraint(logits, pltpu.HBM)
        self.expression = expression
        self.core = lax.axis_index("genes")
        self.enable = cell_mask.astype(f32).reshape(-1, 128)
        self.retain = jax.nn.sigmoid(filter_logits).reshape(-1, 128)
        self.spots = logits.shape[1]
        self.counts = spot_counts.astype(f32)[None, :]
        self.core_flag = self.core.astype(jnp.int32).reshape(1)
        self.half = expression.shape[1]
        self.target = spot_expression
        sent = lax.dynamic_slice_in_dim(spot_expression, (1 - self.core) * self.spots, self.spots, 0)
        quarter = self.half // 4
        self.target_sent = [sent[:, k * quarter : (k + 1) * quarter] for k in range(4)]

    def local_stats(self):
        part = col_stats(self.logits, self.enable, self.retain)
        count = jnp.broadcast_to(jnp.sum(self.enable * self.retain), (1, self.spots))
        return jnp.concatenate([part, count], axis=0)

    def merge_stats(self, part, away):
        top = jnp.maximum(part[0], away[0])
        here, there = jnp.exp(part[0] - top), jnp.exp(away[0] - top)
        total = part[1] * here + away[1] * there
        density = (part[2] * here + away[2] * there) / total
        self.density = density[None, :]
        self.cell_count = part[3:4, :128] + away[3:4, :128]
        self.shift = (top + jnp.log(total))[None, :]
        counts = self.counts[0]
        kl_parts = (jnp.sum(density), jnp.sum(counts * (jnp.log(counts) - jnp.log(density))), jnp.sum(counts))
        self.kl_parts = jnp.broadcast_to(jnp.stack(kl_parts)[:, None], (3, 128))

    def turned(self, order, shift, logits):
        return mapped_turned(order, logits, self.enable, self.retain, shift)

    def stats(self, parts, other, at, wide, part=0):
        column = at % (self.half // 4) // wide
        return pred_stats(self.core_flag, parts, self.target, other, at // wide, column, wide, part)

    def gathered_whole(self):
        own = lax.all_gather(self.expression, "spots", axis=0, tiled=True)
        other = swap_genes(own)
        part = self.local_stats()
        self.target_other = [swap_genes(x) for x in self.target_sent]
        self.merge_stats(part, swap_cells(part))
        order = jnp.arange(PIECES, dtype=jnp.int32)
        mapped = self.turned(order, self.shift, self.logits)
        wide = self.half // 4
        widths, panels, stats = (wide,) * 4, [], []
        for q in range(4):
            pieces = tuple((r, 0, r, q) for r in range(PIECES))
            (partial,), (panel,) = forward(self.core_flag, mapped, [(own, other)], [pieces], wide)
            panels.append(panel)
            stats.append(self.stats([lax.psum(partial, "cells")], self.target_other[q], q * wide, wide))
        return order, widths, panels, stats, (), None

    def gathered_line(self):
        near_pairs = [(2 * z + y, 2 * (z ^ 1) + y) for z in range(4) for y in range(2)]
        middle_pairs = [(2 * z + y, 2 * (3 - z) + y) for z in (1, 2) for y in range(2)]
        across_pairs = [(i, i ^ 1) for i in range(8)]

        def near(x):
            return lax.ppermute(x, "spots", near_pairs)

        def middle(x):
            return lax.ppermute(x, "spots", middle_pairs)

        def across(x):
            return lax.ppermute(x, "spots", across_pairs)

        spot = lax.axis_index("spots")
        z, y = spot // 2, spot % 2
        inside = (z == 1) | (z == 2)
        inside_flag = inside.astype(jnp.int32).reshape(1)
        column = jnp.stack([z, z ^ 1, jnp.where(z < 2, 2, 1), jnp.where(z < 2, 3, 0)])
        order = jnp.concatenate([2 * column + y, 2 * column + (1 - y)]).astype(jnp.int32)
        unit = self.half // 8
        expr = self.expression

        def cut(x, at, wide):
            return x[:, at * unit : (at + wide) * unit]

        def pick(b, e, c, f, *widths, pad=0):
            return select(inside_flag, b, e, c, f, [wide * unit for wide in widths], pad)

        core = self.core_flag

        def run(sources, chunks, wide, begun=None, near=False, column=None, columns=0, left=None):
            columns = (None if column is None else 2 * column * unit), 2 * columns * unit
            return forward(core, mapped, sources, chunks, wide * unit, begun, near, *columns, left)

        def whole(c, d):
            return ((0, 0, 0, c), (1, 1, 0, d), (2, 2, 0, 0), (3, 2, 1, 0), (4, 3, 0, c), (5, 4, 0, d), (6, 5, 0, 0), (7, 5, 1, 0))

        s01 = cut(expr, 0, 4)
        beside = across(expr)
        a01 = near(s01)
        b01 = middle(s01)
        expr_o = swap_genes(expr)
        target_0 = swap_genes(self.target_sent[0])
        part = self.local_stats()
        a01, b01, part, target_0, sv, target_1 = hold(
            a01, b01, part, target_0, cut(expr, 4, 3), self.target_sent[1]
        )
        c01 = middle(a01)
        e01 = near(b01)
        away = swap_cells(part)
        target_1 = swap_genes(target_1)
        self.merge_stats(part, away)
        mapped = self.turned(order, self.shift, self.logits)
        beside, e01, c01, expr_o, mapped, a01, sv, target_1 = hold(
            beside, e01, c01, expr_o, mapped, a01, sv, target_1
        )
        yn = across(a01)
        f01 = near(c01)
        beside_o = swap_genes(beside)
        a01_o = swap_genes(a01)
        bv = middle(sv)
        mf0, mf1 = pick(b01, e01, c01, f01, 2, 2)
        yn, mf0, mf1, a01_o, sv, bv, beside, self.kl_parts = hold(
            yn, mf0, mf1, a01_o, sv, bv, beside, self.kl_parts
        )
        ymf0 = across(mf0)
        av = near(sv)
        mf0_o, yn_o = swap_genes(mf0), swap_genes(yn)
        sf = join(cut(expr, 7, 1), cut(beside, 7, 1))
        expr_2, a01_2, beside_2, yn_2 = (expr, expr_o), (a01, a01_o), (beside, beside_o), (yn, yn_o)
        begun = run([expr_2, beside_2], [((0, 0, 0, q), (4, 1, 0, q)) for q in range(4, 8)], 1)
        ymf0, av, mf0_o, yn_o, mf1, bv, mapped, *begun = hold(
            ymf0, av, mf0_o, yn_o, mf1, bv, mapped, *begun[0], *begun[1]
        )
        ymf1 = across(mf1)
        ev = near(bv)
        cv = middle(av)
        ymf0_o, mf1_o = swap_genes(ymf0), swap_genes(mf1)
        (high0, low0), (panel0,) = run(
            [expr_2, a01_2, (mf0, mf0_o), beside_2, yn_2, (ymf0, ymf0_o)], [whole(0, 0)], 2, column=0, columns=2
        )
        ymf1, ev, cv, high0, mf1_o, av, mapped = hold(ymf1, ev, cv, high0, mf1_o, av, mapped)
        ynv = across(av)
        fv = near(cv)
        ymf1_o = swap_genes(ymf1)
        high0_away = swap_cells(high0)
        av_o = swap_genes(av)
        (partial1,), (panel1,) = run([expr_2, a01_2, (mf1, mf1_o), beside_2, yn_2, (ymf1, ymf1_o)], [whole(1, 1)], 2)
        ynv, fv, partial1, high0_away, av_o, sf, mapped = hold(ynv, fv, partial1, high0_away, av_o, sf, mapped)
        m2, m34 = pick(bv, ev, cv, fv, 1, 2, pad=16)
        ym2 = across(m2)
        af, bf = near(sf), middle(sf)
        away1 = swap_cells(partial1)
        ynv_o = swap_genes(ynv)
        more = run(
            [(av, av_o), (ynv, ynv_o)], [((1, 0, 0, q), (5, 1, 0, q)) for q in range(3)], 1, (begun[0:3], begun[4:7])
        )
        ym2, m2, m34, mapped, *more = hold(ym2, m2, m34, mapped, *more[0], *more[1])
        ym34 = across(m34)
        ym2_o, m2_o = swap_genes(ym2), swap_genes(m2)
        af, bf = hold(af, bf)
        cf = middle(af)

        def rest(column):
            return ((2, 0, 0, column), (3, 0, 1, column), (6, 1, 0, column), (7, 1, 1, column))

        (high2, low), (panel2,) = run(
            [(m2, m2_o), (ym2, ym2_o)], [rest(0)], 1, (more[0:1], more[3:4]), near=True, column=0, columns=4
        )
        stats0 = self.stats([high0, high0_away], target_0, 0, 2 * unit)
        cf, high2, away1, m34, bf, af, target_2, *stats0 = hold(
            cf, high2, away1, m34, bf, af, self.target_sent[2], *stats0
        )
        target_2 = swap_genes(target_2)
        ef, ff = near(bf), near(cf)
        m34_o = swap_genes(m34)
        high2_away = swap_cells(high2)
        stats1 = self.stats([partial1, away1], target_1, 2 * unit, 2 * unit)
        ym34, ef, m34, mapped, high2_away, af, low0, target_2, target_3, *stats1 = hold(
            ym34, ef, m34, mapped, high2_away, af, low0, target_2, self.target_sent[3], *stats1
        )
        ym34_o, af_o = swap_genes(ym34), swap_genes(af)
        low0_first_away = swap_cells(cut(low0, 0, 2))
        target_3 = swap_genes(target_3)
        self.target_other = (target_0, target_1, target_2, target_3)
        sources = [(m34, m34_o), (ym34, ym34_o)]
        (high3, low), (panel3,) = run(sources, [rest(0)], 1, (more[1:2], more[4:5]), column=1, columns=4, left=low, near=True)
        high3_away = swap_cells(high3)
        (high4, low), (panel4,) = run(sources, [rest(1)], 1, (more[2:3], more[5:6]), column=2, columns=4, left=low, near=True)
        ff, high3_away, high4, low0_first_away, target_3, af_o, mapped = hold(
            ff, high3_away, high4, low0_first_away, target_3, af_o, mapped
        )
        high4_away = swap_cells(high4)
        (mff,) = pick(bf, ef, cf, ff, 1)
        mff_o = swap_genes(mff)
        late = ((1, 0, 0, 0), (2, 1, 0, 0), (3, 1, 2, 0), (5, 0, 1, 0), (6, 1, 1, 0), (7, 1, 3, 0))
        (highf, low), (panelf,) = run(
            [(af, af_o), (mff, mff_o)], [late], 1, (begun[3:4], begun[7:8]), column=3, columns=4, left=low, near=True
        )
        highf, high2, high2_away = hold(highf, high2, high2_away)
        highf_away = swap_cells(highf)
        low0_last = cut(low0, 2, 2)
        high4_away, highf_away, low0_last = hold(high4_away, highf_away, low0_last)
        low0_last_away = swap_cells(low0_last)
        late = [
            self.stats([high2, high2_away], target_2, 4 * unit, unit),
            self.stats([high3, high3_away], target_2, 5 * unit, unit),
            self.stats([high4, high4_away], target_3, 6 * unit, unit),
            self.stats([highf, highf_away], target_3, 7 * unit, unit),
        ]
        widths = (2 * unit,) * 2 + (unit,) * 4
        panels = (panel0, panel1, panel2, panel3, panel4, panelf)
        return order, widths, panels, [stats0, stats1, *late], (low0, low0_first_away, low0_last_away), low


def body(logits, filter_logits, expression, spot_expression, cell_mask, spot_counts):
    cells_total = logits.shape[0] * lax.axis_size("cells")
    spots = logits.shape[1]
    spots_total = spots * lax.axis_size("spots") * lax.axis_size("genes")
    genes_total = expression.shape[1] * lax.axis_size("genes")
    step = Step(logits, filter_logits, expression, spot_expression, cell_mask, spot_counts)
    gathered = step.gathered_line() if lax.axis_size("spots") == 8 else step.gathered_whole()
    order, widths, panels, stats, left, late_left = gathered
    gene_stats, preds, spot_stats = zip(*stats)
    split = 2
    gene, (kept, sent) = sum_spots_genes(
        jnp.concatenate([*gene_stats, step.kl_parts], axis=1),
        (*preds[:split], *left),
        lambda *first: share(step.core_flag, first[:split], first[split:], [0, None] if left else [None] * split),
    )
    spot = functools.reduce(jnp.add, spot_stats)
    cols = jnp.concatenate([step.shift, step.density, step.counts], axis=0)
    turned, col, sums = grad_pred(
        step.core_flag, widths, genes_total, spots_total, spot, gene, cols, step.target, step.target_other, preds
    )
    left, places = [], [None] * (len(widths) - split)
    if late_left is not None:
        turned, late_left = hold(turned, late_left)
        left, places = [late_left, swap_cells(late_left)], [2 * sum(widths[split:q]) for q in range(split, len(widths))]
    turned, sent = hold(turned, sent)
    theirs = swap_genes(sent)
    grad_logits, row = backward(order, step.logits, step.enable, step.retain, col, turned, panels)

    row, core, theirs, *left = hold(row, step.core_flag, theirs, *left)
    half = expression.shape[1]

    def lay_both(late_kept, late_sent):
        predicted = lay(core, kept, theirs, half, 0)
        return (lay(core, late_kept, swap_genes(late_sent), half, 1, predicted),)

    row_sums, (predicted,) = sum_spots_genes(jnp.concatenate([row, sums], axis=0), share(core, preds[split:], left, places), lay_both)
    copies = lax.axis_size("spots") * lax.axis_size("genes")
    filter_grad, total_loss = final(
        genes_total, spots_total, cells_total, copies, row_sums, gene, step.cell_count, step.enable, step.retain
    )
    return (predicted, total_loss.reshape(()), grad_logits, filter_grad.reshape(-1))


def solution(mesh):
    placed = (
        P("cells", ("spots", "genes")),
        P("cells"),
        P(("cells", "spots"), "genes"),
        P("spots", "genes"),
        P("cells"),
        P(("spots", "genes")),
    )
    return jax.shard_map(
        body,
        mesh=mesh,
        in_specs=placed,
        out_specs=(P("spots", "genes"), P(), P("cells", ("spots", "genes")), P("cells")),
        check_vma=False,
    )
```
